32 devices in a mesh: tile: 16 (over z, y, x), plane: 2 (over core).
Axes of the slice: x: 2, y: 2, z: 4, core: 2. Of those that a mesh axis runs over, the one named last changes fastest.
Arguments:
- ref_feat: bfloat16 [32, 4, 4096], P(None, None, 'tile'), may hold values from -6 to 6
- src_feat: bfloat16 [4, 32, 4, 4096], P(None, 'plane', None, 'tile'), may hold values from -6 to 6
- shifts: int32 [4, 16], P(None, 'plane'), may hold values from 0 to 128, as said below
- conv_one: bfloat16 [8, 8, 3, 3, 3], replicated, may hold values from -0.4375 to 0.4375
- bias_one: float32 [8], replicated, may hold values from -0.5 to 0.5
- conv_two: bfloat16 [8, 8, 3, 3, 3], replicated, may hold values from -0.4375 to 0.4375
- bias_two: float32 [8], replicated, may hold values from -0.5 to 0.5
- view_head: float32 [8], replicated, may hold values from -2 to 2
Outputs:
- joined: bfloat16 [8, 16, 4, 4096], P(None, 'plane', None, 'tile')
The draws below stay inside these ranges and needn't reach their ends.
Inputs may be any that keep to these rules, and one draw needn't show every extreme that they name: `shifts`: for every view the shift never falls from one plane to the next; it is 0 at plane 0 and 128 at plane 16 - 1.
All inputs are finite; a program needn't handle non-finite values.
Results may differ from the reference program's by a relative error of at most 0.0053.
Values may be sent and summed in bfloat16 or wider, within the bound.
No kernel may reach another device: no remote copies, remote signals or barrier semaphores. Data moves between devices by JAX's collectives and lax.ppermute only.
A program may use at most 64 MiB of HBM per device.

```python
import jax
import jax.numpy as jnp
from jax import lax

CHANNELS = 32
GROUPS = 8
CONV_CH = 8
VIEWS = 4
ROWS = 4
MAX_SHIFT = 128
PLANES = 16
WIDTH = 4096


def draw_shifts(key, part):
    values = jax.random.randint(key, (VIEWS, PLANES - 2), 0, MAX_SHIFT + 1).astype(jnp.int32)
    ordered = jnp.sort(values, axis=1)
    first = jnp.zeros((VIEWS, 1), jnp.int32)
    last = jnp.full((VIEWS, 1), MAX_SHIFT, jnp.int32)
    return jnp.concatenate([first, ordered, last], axis=1)


def steps_of(key, dims, shards, low, top_value):
    factor_of, own = 1.0, jax.random.fold_in(key, 6)
    for position, blocks in shards:
        draws = jnp.exp(jax.random.uniform(jax.random.fold_in(own, position), (blocks,), jnp.float32, low / len(shards), top_value / len(shards)))
        factor_of = factor_of * jnp.repeat(draws, dims[position] // blocks).reshape([-1 if axis == position else 1 for axis in range(len(dims))])
    return factor_of


def bell_draw(own_key, extent, width, most, pieces=(), kind=jnp.bfloat16):
    entries = jax.random.normal(own_key, extent, jnp.float32) * width
    if len(pieces) > 0:
        entries = steps_of(own_key, extent, pieces, -0.22, 0.18) * entries
    return jnp.clip(entries, min=-most, max=most).astype(kind)


def setup_inputs(seed: int = 0) -> dict:
    key_of = jax.random.split(jax.random.key(seed), 9)
    ref_feat = bell_draw(key_of[0], (CHANNELS, ROWS, WIDTH), 1.0, 6.0, ((2, 16),))
    src_feat = bell_draw(key_of[1], (VIEWS, CHANNELS, ROWS, WIDTH), 1.0, 6.0, ((1, 2), (3, 16)))
    shifts = draw_shifts(jax.random.fold_in(key_of[8], 71), 0)
    conv_one = bell_draw(key_of[3], (CONV_CH, GROUPS, 3, 3, 3), (27 * GROUPS) ** -0.5, 0.4375)
    bias_one = jnp.clip(jax.random.uniform(key_of[4], (CONV_CH,), jnp.float32, -0.5, 0.5), -0.5, 0.5)
    conv_two = bell_draw(key_of[5], (CONV_CH, CONV_CH, 3, 3, 3), (27 * CONV_CH) ** -0.5, 0.4375)
    bias_two = jnp.clip(jax.random.uniform(key_of[6], (CONV_CH,), jnp.float32, -0.5, 0.5), -0.5, 0.5)
    view_head = bell_draw(key_of[7], (CONV_CH,), CONV_CH ** -0.5, 2.0, (), jnp.float32)
    return {"ref_feat": ref_feat, "src_feat": src_feat, "shifts": shifts, "conv_one": conv_one, "bias_one": bias_one, "conv_two": conv_two, "bias_two": bias_two, "view_head": view_head}


def convolve(volume, kernel, offset):
    result = lax.conv_general_dilated(volume.astype(jnp.float32)[None], kernel.astype(jnp.float32), (1, 1, 1), [(1, 1), (1, 1), (1, 1)], dimension_numbers=("NCDHW", "OIDHW", "NCDHW"), precision=lax.Precision.HIGHEST)[0]
    return jax.nn.relu(result + offset[:, None, None, None])


def reference(ref_feat, src_feat, shifts, conv_one, bias_one, conv_two, bias_two, view_head):
    ref_wide = ref_feat.astype(jnp.float32)
    weighted = jnp.zeros((GROUPS, PLANES, ROWS, WIDTH), jnp.float32)
    total_weight = jnp.zeros((PLANES, ROWS, WIDTH), jnp.float32)
    for view_idx in range(VIEWS):
        padded = jnp.pad(src_feat[view_idx], ((0, 0), (0, 0), (MAX_SHIFT, 0)))

        def one_plane(offset):
            start = (MAX_SHIFT - offset).astype(jnp.int32)
            shifted = lax.dynamic_slice_in_dim(padded, start, WIDTH, 2).astype(jnp.float32)
            products = (ref_wide * shifted).reshape(GROUPS, CHANNELS // GROUPS, ROWS, WIDTH)
            return jnp.mean(products, axis=1)

        matches = jnp.transpose(lax.map(one_plane, shifts[view_idx]), (1, 0, 2, 3)).astype(jnp.bfloat16)
        first_out = convolve(matches, conv_one, bias_one).astype(jnp.bfloat16)
        second_out = convolve(first_out, conv_two, bias_two)
        scores = jnp.einsum("c,cdhw->dhw", view_head, second_out)
        weight = jax.nn.sigmoid(scores)
        weighted = weighted + weight[None] * matches.astype(jnp.float32)
        total_weight = total_weight + weight
    return (weighted / total_weight[None]).astype(jnp.bfloat16)
```

```python
import jax
import jax.numpy as jnp
from jax import lax
from jax.experimental import pallas as pl
from jax.experimental.pallas import tpu as pltpu
from jax.sharding import PartitionSpec as P

GROUPS = 8
MAX_SHIFT = 128
LEAD = MAX_SHIFT + 16
EDGE = 16
FAR = -3.0e38


def iota(shape, dim):
    return lax.broadcasted_iota(jnp.int32, shape, dim)


def dot(left, right):
    return jnp.dot(left, right, preferred_element_type=jnp.float32)


def dot_nt(left, right):
    return lax.dot_general(
        left, right, (((1,), (1,)), ((), ())), preferred_element_type=jnp.float32
    )


def pack_body(place, own_ref, other_ref, ref_ref, cols_ref, ref_cols_ref, packet_ref):
    views, half, rows, width = own_ref.shape
    lanes = 2 * half * rows
    inner = lanes // (GROUPS * rows)
    role, order = place[0], place[1]
    eye = (iota((width, width), 0) == iota((width, width), 1)).astype(jnp.bfloat16)
    to = iota((lanes, lanes), 0)
    k, g, h = to // (GROUPS * rows), (to // rows) % GROUPS, to % rows
    perm = ((g * inner + k) * rows + h == iota((lanes, lanes), 1)).astype(jnp.bfloat16)

    def turned(block):
        ordered = dot(perm, block).astype(jnp.bfloat16)
        return dot_nt(eye, ordered).astype(jnp.bfloat16)

    for v in range(views):
        own = own_ref[v].reshape(half * rows, width)
        other = other_ref[v].reshape(half * rows, width)
        low = jnp.where(order == 0, own, other)
        high = jnp.where(order == 0, other, own)
        cols_ref[v] = turned(jnp.concatenate([low, high], axis=0))
    ref_cols_ref[...] = turned(ref_ref[...].reshape(lanes, width))
    for v in range(views):
        start = pl.multiple_of(jnp.where(role == 0, width - LEAD, 0), 16)
        packet_ref[v * LEAD : (v + 1) * LEAD] = cols_ref[v, pl.ds(start, LEAD)]
    start = pl.multiple_of(jnp.where(role == 0, width - EDGE, 0), 16)
    packet_ref[views * LEAD :] = ref_cols_ref[pl.ds(start, EDGE)]


def lane_table(values_ref, rows, lane):
    which = (lane // rows) % GROUPS
    table = jnp.zeros(lane.shape, jnp.float32)
    for o in range(GROUPS):
        table = jnp.where(which == o, values_ref[o], table)
    return table


def build_band(taps_ref, which, band_ref, rows):
    block = GROUPS * rows
    spread = iota((3 * GROUPS, 128), 1) // rows == iota((3 * GROUPS, 128), 0)
    wide = dot(taps_ref[which], spread.astype(jnp.bfloat16)).astype(jnp.bfloat16)
    stretch = (iota((block, GROUPS), 0) // rows == iota((block, GROUPS), 1)).astype(jnp.bfloat16)
    lane = iota((block, 128), 1)
    gap = iota((block, 128), 0) % rows - lane % rows + 1
    depth, out_lanes = band_ref.shape[0] // 3, band_ref.shape[1]
    per_tile = 128 // block
    zero = jnp.zeros((block, 128), jnp.bfloat16)
    for e in range(3):
        base = jnp.zeros((block, 128), jnp.float32)
        for b in range(3):
            at = (b * 3 + e) * GROUPS
            base = jnp.where(gap == b, dot(stretch, wide[at : at + GROUPS]), base)
        for j in range(depth // block):
            offset = j - 2
            first, turn = offset // per_tile, offset % per_tile
            moved = pltpu.roll(base, turn * block, 1) if turn else base
            for t in range(out_lanes // 128):
                if t == first:
                    part = jnp.where(lane >= turn * block, moved, 0.0).astype(jnp.bfloat16)
                elif t == first + 1 and turn > per_tile - 3:
                    part = jnp.where(lane < turn * block, moved, 0.0).astype(jnp.bfloat16)
                else:
                    part = zero
                at = e * depth + j * block
                band_ref[at : at + block, t * 128 : (t + 1) * 128] = part


def main_body(
    place,
    shifts,
    before,
    after,
    bias_one,
    bias_two,
    view_head,
    cols_ref,
    ref_cols_ref,
    got_ref,
    swapped_ref,
    taps_ref,
    out_ref,
    src,
    ref_wide,
    match,
    first,
    band_one,
    band_two,
):
    views, width, lanes = cols_ref.shape
    groups, planes, rows, _ = out_ref.shape
    block = groups * rows
    span = (planes + 4) * block
    tall = match.shape[1] - 8
    order = place[1]
    is_first_tile, is_last_tile = place[2], place[3]
    is_first_plane, is_last_plane = place[4], place[5]

    build_band(taps_ref, 0, band_one, rows)
    build_band(taps_ref, 1, band_two, rows)

    row_which = (iota((block, 128), 0) // rows) % groups
    head = jnp.zeros((block, 128), jnp.float32)
    for o in range(groups):
        head = jnp.where(row_which == o, view_head[o], head)
    lane = iota((block, 128), 1)
    head = jnp.where(iota((block, 128), 0) % rows == lane % rows, head, 0.0)
    head_high = head.astype(jnp.bfloat16).astype(jnp.float32)
    head_low = head - head_high

    def diagonal(part):
        pieces = []
        for j in range(planes):
            row = []
            for t in range(planes * block // 128):
                here = lane // block + t * (128 // block) == j
                row.append(jnp.where(here, part, 0.0).astype(jnp.bfloat16))
            pieces.append(jnp.concatenate(row, axis=1))
        return jnp.concatenate(pieces, axis=0)

    high = diagonal(head_high)
    head_all = jnp.concatenate([high, high, diagonal(head_low)], axis=0)

    left = jnp.where(order == 0, got_ref[...], swapped_ref[...])
    right = jnp.where(order == 0, swapped_ref[...], got_ref[...])
    for v in range(views):
        src[v, 0:LEAD] = left[v * LEAD : (v + 1) * LEAD].astype(jnp.float32)
        src[v, LEAD : LEAD + width] = cols_ref[v].astype(jnp.float32)
        src[v, LEAD + width :] = right[v * LEAD : v * LEAD + EDGE].astype(jnp.float32)
    ref_wide[0:EDGE] = left[views * LEAD :].astype(jnp.float32)
    ref_wide[EDGE : EDGE + width] = ref_cols_ref[...].astype(jnp.float32)
    ref_wide[EDGE + width :] = right[views * LEAD : views * LEAD + EDGE].astype(jnp.float32)

    span_lane = iota((1, span), 1) // block
    outside = ((span_lane < 2) & (is_first_plane == 1)) | (
        (span_lane >= planes + 2) & (is_last_plane == 1)
    )
    scale = jnp.where(outside, 0.0, 1.0 / (lanes // block))
    base_one = lane_table(bias_one, rows, iota((1, span), 1))
    outside = ((span_lane == 0) & (is_first_plane == 1)) | (
        (span_lane == planes + 1) & (is_last_plane == 1)
    )
    base_one = jnp.where(outside, FAR, base_one)
    base_two = lane_table(bias_two, rows, iota((1, planes * block), 1))

    def shift_of(v, d):
        if d < 0:
            return before[v, planes + d]
        return shifts[v, d] if d < planes else after[v, d - planes]

    chunk = tall // 3
    quarter = iota((chunk, 128), 1) // block
    lower, middle, even = quarter < 2, (quarter == 1) | (quarter == 2), quarter % 2 == 0
    weighted = jnp.zeros((width, planes * block), jnp.float32)
    total = jnp.zeros((width, planes * block), jnp.float32)
    for v in range(views):
        for q in range(span // 128):
            for r in range(0, tall, chunk):
                here = ref_wide[EDGE - 2 + r : EDGE - 2 + r + chunk]

                def product(j):
                    start = LEAD - 2 + r - shift_of(v, q * 4 + j - 2)
                    return src[v, pl.ds(start, chunk)] * here

                a, c, b, d = (product(j) for j in range(4))
                x = jnp.where(lower, a, b) + pltpu.roll(jnp.where(lower, b, a), 64, 1)
                z = jnp.where(middle, c, d) + pltpu.roll(jnp.where(middle, d, c), 64, 1)
                y = jnp.where(even, x, z) + pltpu.roll(jnp.where(even, z, x), 96, 1)
                y = y * scale[:, q * 128 : (q + 1) * 128]
                match[v, r : r + chunk, q * 128 : (q + 1) * 128] = y.astype(jnp.bfloat16).astype(
                    jnp.float32
                )
        moved = [match[v, e : e + tall].astype(jnp.bfloat16) for e in range(3)]
        raw = dot(jnp.concatenate(moved, axis=1), band_one[...])
        wide_out = raw.shape[1]
        raw = jnp.maximum(raw + base_one[:, :wide_out], 0.0)
        first[v, 0:tall, 0:wide_out] = raw.astype(jnp.bfloat16).astype(jnp.float32)
        rest = span - wide_out
        raw = sum(
            dot(moved[e][:, wide_out:], band_one[e * span : e * span + rest, 0:rest])
            for e in range(3)
        )
        raw = jnp.maximum(raw + base_one[:, wide_out:], 0.0)
        first[v, 0:tall, wide_out:] = raw.astype(jnp.bfloat16).astype(jnp.float32)

        @pl.when(is_first_tile == 1)
        def _():
            first[v, 0:1] = jnp.zeros((1, span), jnp.float32)

        @pl.when(is_last_tile == 1)
        def _():
            first[v, width + 1 : width + 2] = jnp.zeros((1, span), jnp.float32)

        moved = [first[v, e : e + width].astype(jnp.bfloat16) for e in range(3)]
        second = dot(jnp.concatenate(moved, axis=1), band_two[...])
        second = jnp.maximum(second + base_two, 0.0)
        upper = second.astype(jnp.bfloat16)
        under = (second - upper.astype(jnp.float32)).astype(jnp.bfloat16)
        score = dot(jnp.concatenate([upper, under, upper], axis=1), head_all)
        weight = 1.0 / (1.0 + jnp.exp(-score))
        total = total + weight
        weighted = weighted + weight * match[v, 2 : 2 + width, 2 * block : (planes + 2) * block]
    joined = (weighted / total).astype(jnp.bfloat16)
    size = planes * block
    to = iota((size, size), 0)
    g, j, h = to // (planes * rows), (to // rows) % planes, to % rows
    perm = ((j * groups + g) * rows + h == iota((size, size), 1)).astype(jnp.bfloat16)
    turned = dot_nt(perm, joined).astype(jnp.bfloat16)
    out_ref[...] = turned.reshape(groups, planes, rows, width)


def whole(memory):
    return pl.BlockSpec(memory_space=memory)


def per_device(ref_feat, src_feat, shifts, conv_one, bias_one, conv_two, bias_two, view_head):
    views, _, rows, width = src_feat.shape
    planes = shifts.shape[1]
    lanes = ref_feat.shape[0] * rows
    tiles, sides = lax.axis_size("tile"), lax.axis_size("plane")
    tile, plane = lax.axis_index("tile"), lax.axis_index("plane")
    if sides == 2:
        swap = [(0, 1), (1, 0)]
        own, other, order = src_feat, lax.ppermute(src_feat, "plane", swap), plane
        before = after = lax.ppermute(shifts, "plane", swap)
    else:
        full = lax.all_gather(src_feat, "plane", axis=1, tiled=True)
        half = full.shape[1] // 2
        own, other, order = full[:, :half], full[:, half:], 0 * plane
        before = lax.ppermute(shifts, "plane", [(i, i + 1) for i in range(sides - 1)])
        after = lax.ppermute(shifts, "plane", [(i + 1, i) for i in range(sides - 1)])
    ends = [tile == 0, tile == tiles - 1, plane == 0, plane == sides - 1]
    place = jnp.stack([jnp.minimum(plane, 1), order] + [e.astype(jnp.int32) for e in ends])

    packet_rows = views * LEAD + EDGE
    bf16 = jnp.bfloat16
    vmem, smem = pltpu.VMEM, pltpu.SMEM
    cols, ref_cols, packet = pl.pallas_call(
        pack_body,
        out_shape=[
            jax.ShapeDtypeStruct((views, width, lanes), bf16),
            jax.ShapeDtypeStruct((width, lanes), bf16),
            jax.ShapeDtypeStruct((packet_rows, lanes), bf16),
        ],
        in_specs=[whole(smem)] + [whole(vmem)] * 3,
        out_specs=[whole(vmem)] * 3,
        name="pack_columns",
    )(place, own, other, ref_feat)

    pairs = [(sides * i, sides * (i + 1)) for i in range(tiles - 1)]
    pairs += [(sides * (i + 1) + 1, sides * i + 1) for i in range(tiles - 1)]
    got = lax.ppermute(packet, ("tile", "plane"), pairs)
    if sides == 2:
        swapped = lax.ppermute(got, "plane", [(0, 1), (1, 0)])
    else:
        both = lax.all_gather(got, "plane", axis=0)
        got, swapped = both[0], both[1]

    def taps(kernel):
        flipped = jnp.flip(kernel, axis=2)
        return jnp.transpose(flipped, (3, 4, 1, 2, 0)).reshape(9 * GROUPS, 3 * GROUPS)

    both_taps = jnp.stack([taps(conv_one), taps(conv_two)])
    span = (planes + 4) * GROUPS * rows
    out_lanes = planes * GROUPS * rows
    tall = width + 8
    return pl.pallas_call(
        main_body,
        out_shape=jax.ShapeDtypeStruct((GROUPS, planes, rows, width), bf16),
        in_specs=[whole(smem)] * 7 + [whole(vmem)] * 5,
        out_specs=whole(vmem),
        scratch_shapes=[
            pltpu.VMEM((views, LEAD + width + EDGE, lanes), jnp.float32),
            pltpu.VMEM((EDGE + width + EDGE, lanes), jnp.float32),
            pltpu.VMEM((views, tall + 8, span), jnp.float32),
            pltpu.VMEM((views, tall + 8, span), jnp.float32),
            pltpu.VMEM((3 * span, out_lanes), bf16),
            pltpu.VMEM((3 * span, out_lanes), bf16),
        ],
        compiler_params=pltpu.CompilerParams(vmem_limit_bytes=48 * 1024 * 1024),
        name="cost_volume",
    )(
        place,
        shifts,
        before,
        after,
        bias_one,
        bias_two,
        view_head,
        cols,
        ref_cols,
        got,
        swapped,
        both_taps,
    )


def solution(mesh):
    placed = (
        P(None, None, "tile"),
        P(None, "plane", None, "tile"),
        P(None, "plane"),
        P(),
        P(),
        P(),
        P(),
        P(),
    )
    return jax.shard_map(
        per_device,
        mesh=mesh,
        in_specs=placed,
        out_specs=P(None, "plane", None, "tile"),
        check_vma=False,
    )
```

```python
import jax
import jax.numpy as jnp
from jax import lax
from jax.experimental import pallas as pl
from jax.experimental.pallas import tpu as pltpu
from jax.sharding import PartitionSpec as P

GROUPS = 8
MAX_SHIFT = 128
LEAD = MAX_SHIFT + 16
EDGE = 16
FAR = -3.0e38


def iota(shape, dim):
    return lax.broadcasted_iota(jnp.int32, shape, dim)


def dot(left, right):
    return jnp.dot(left, right, preferred_element_type=jnp.float32)


def dot_nt(left, right):
    return lax.dot_general(
        left, right, (((1,), (1,)), ((), ())), preferred_element_type=jnp.float32
    )


def turning(own_ref, other_ref, order, pick):
    _, half, rows, width = own_ref.shape
    lanes = 2 * half * rows
    inner = 2 * half // GROUPS
    to = iota((lanes, lanes), 1)
    k, g, h = to // (GROUPS * rows), (to // rows) % GROUPS, to % rows
    place = (g * inner + k - half * order + 2 * half) % (2 * half)
    perm = (place * rows + h == iota((lanes, lanes), 0)).astype(jnp.bfloat16)
    plain = ((g * inner + k) * rows + h == iota((lanes, lanes), 0)).astype(jnp.bfloat16)

    def turned(own, other=None):
        block = own if other is None else jnp.concatenate([own, other], axis=0)
        block = block.reshape(lanes, width)
        columns = dot_nt(pick, block).astype(jnp.bfloat16)
        return dot(columns, plain if other is None else perm).astype(jnp.bfloat16)

    return turned


def pack_body(own_ref, other_ref, ref_ref, packet_ref):
    views, _, _, width = own_ref.shape
    role, order, *_ = position()
    start = jnp.where(role == 0, width - LEAD, 0)
    pick = (iota((LEAD, width), 0) + start == iota((LEAD, width), 1)).astype(jnp.bfloat16)
    turned = turning(own_ref, other_ref, order, pick)
    for v in range(views):
        packet_ref[v * LEAD : (v + 1) * LEAD] = turned(own_ref[v], other_ref[v])
    start = jnp.where(role == 0, width - EDGE, 0)
    pick = (iota((EDGE, width), 0) + start == iota((EDGE, width), 1)).astype(jnp.bfloat16)
    turned = turning(own_ref, other_ref, order, pick)
    packet_ref[views * LEAD :] = turned(ref_ref[...])


def position():
    tile, plane = lax.axis_index("tile"), lax.axis_index("plane")
    tiles, sides = lax.axis_size("tile"), lax.axis_size("plane")
    order = plane if sides == 2 else 0 * plane
    role = jnp.minimum(plane, 1)
    return role, order, tile == 0, tile == tiles - 1, plane == 0, plane == sides - 1


def lane_table(values_ref, rows, lane):
    which = (lane // rows) % GROUPS
    table = jnp.zeros(lane.shape, jnp.float32)
    for o in range(GROUPS):
        table = jnp.where(which == o, values_ref[o], table)
    return table


def build_band(taps_ref, which, band_ref, rows):
    block = GROUPS * rows
    spread = iota((3 * GROUPS, 128), 1) // rows == iota((3 * GROUPS, 128), 0)
    wide = dot(taps_ref[which], spread.astype(jnp.bfloat16)).astype(jnp.bfloat16)
    stretch = (iota((block, GROUPS), 0) // rows == iota((block, GROUPS), 1)).astype(jnp.bfloat16)
    lane = iota((block, 128), 1)
    gap = iota((block, 128), 0) % rows - lane % rows + 1
    depth, out_lanes = band_ref.shape[0] // 3, band_ref.shape[1]
    per_tile = 128 // block
    zero = jnp.zeros((block, 128), jnp.bfloat16)
    for e in range(3):
        base = jnp.zeros((block, 128), jnp.float32)
        for b in range(3):
            at = (b * 3 + e) * GROUPS
            base = jnp.where(gap == b, dot(stretch, wide[at : at + GROUPS]), base)
        for j in range(depth // block):
            offset = j - 2
            first, turn = offset // per_tile, offset % per_tile
            moved = pltpu.roll(base, turn * block, 1) if turn else base
            for t in range(out_lanes // 128):
                if t == first:
                    part = jnp.where(lane >= turn * block, moved, 0.0).astype(jnp.bfloat16)
                elif t == first + 1 and turn > per_tile - 3:
                    part = jnp.where(lane < turn * block, moved, 0.0).astype(jnp.bfloat16)
                else:
                    part = zero
                at = e * depth + j * block
                band_ref[at : at + block, t * 128 : (t + 1) * 128] = part


def volume(sizes, shift_refs, bias_refs, view_head, taps_ref, src, wide, match, first, band_one, band_two, ends):
    planes, rows, inner = sizes
    block = GROUPS * rows
    span = (planes + 4) * block
    out_lanes = planes * block
    shifts, before, after = shift_refs
    bias_one, bias_two = bias_refs
    is_first_plane, is_last_plane = ends
    build_band(taps_ref, 0, band_one, rows)
    build_band(taps_ref, 1, band_two, rows)

    row, lane = iota((out_lanes, out_lanes), 0), iota((out_lanes, out_lanes), 1)
    same = (row // block == lane // block) & (row % rows == lane % rows)
    spread = same.astype(jnp.bfloat16)
    spread = jnp.concatenate([spread, spread], axis=0)

    span_lane = iota((1, span), 1) // block
    outside = ((span_lane < 2) & is_first_plane) | ((span_lane >= planes + 2) & is_last_plane)
    scale = jnp.where(outside, 0.0, 1.0 / inner)
    base_one = lane_table(bias_one, rows, iota((1, span), 1))
    outside = ((span_lane == 0) & is_first_plane) | ((span_lane == planes + 1) & is_last_plane)
    base_one = jnp.where(outside, FAR, base_one)
    base_two = lane_table(bias_two, rows, iota((1, out_lanes), 1))
    head = lane_table(view_head, rows, iota((1, out_lanes), 1))

    def shift_of(v, d):
        if d < 0:
            return before[v, planes + d]
        return shifts[v, d] if d < planes else after[v, d - planes]

    def fill(v, pieces):
        for at, src_at, wide_at, count in pieces:
            quarter = iota((count, 128), 1) // block
            lower, middle, even = quarter < 2, (quarter == 1) | (quarter == 2), quarter % 2 == 0
            here = wide[wide_at : wide_at + count]
            for q in range(span // 128):

                def product(j):
                    return src[v, pl.ds(src_at - shift_of(v, q * 4 + j - 2), count)] * here

                a, c, b, d = (product(j) for j in range(4))
                x = jnp.where(lower, a, b) + pltpu.roll(jnp.where(lower, b, a), 64, 1)
                z = jnp.where(middle, c, d) + pltpu.roll(jnp.where(middle, d, c), 64, 1)
                y = jnp.where(even, x, z) + pltpu.roll(jnp.where(even, z, x), 96, 1)
                y = y * scale[:, q * 128 : (q + 1) * 128]
                y = y.astype(jnp.bfloat16).astype(jnp.float32)
                match[v, at : at + count, q * 128 : (q + 1) * 128] = y

    def weigh(v, tall, out_rows, mend):
        moved = [match[v, e : e + tall].astype(jnp.bfloat16) for e in range(3)]
        raw = dot(jnp.concatenate(moved, axis=1), band_one[...])
        raw = jnp.maximum(raw + base_one[:, :out_lanes], 0.0)
        first[v, 0:tall, 0:out_lanes] = raw.astype(jnp.bfloat16).astype(jnp.float32)
        rest = span - out_lanes
        raw = sum(
            dot(moved[e][:, out_lanes:], band_one[e * span : e * span + rest, 0:rest])
            for e in range(3)
        )
        raw = jnp.maximum(raw + base_one[:, out_lanes:], 0.0)
        first[v, 0:tall, out_lanes:] = raw.astype(jnp.bfloat16).astype(jnp.float32)
        mend(v)
        moved = [first[v, e : e + out_rows].astype(jnp.bfloat16) for e in range(3)]
        second = dot(jnp.concatenate(moved, axis=1), band_two[...])
        second = jnp.maximum(second + base_two, 0.0) * head
        upper = second.astype(jnp.bfloat16)
        under = (second - upper.astype(jnp.float32)).astype(jnp.bfloat16)
        score = dot(jnp.concatenate([upper, under], axis=1), spread)
        weight = 1.0 / (1.0 + jnp.exp(-score))
        return weight, weight * match[v, 2 : 2 + out_rows, 2 * block : (planes + 2) * block]

    return fill, weigh


def inner_body(
    shifts,
    before,
    after,
    bias_one,
    bias_two,
    view_head,
    own_ref,
    other_ref,
    ref_ref,
    taps_ref,
    cols_ref,
    ref_cols_ref,
    late_ref,
    src,
    wide,
    match,
    first,
    band_one,
    band_two,
):
    views, half, rows, width = own_ref.shape
    planes = shifts.shape[1]
    _, order, _, _, *ends = position()
    pick = (iota((width, width), 0) == iota((width, width), 1)).astype(jnp.bfloat16)
    turned = turning(own_ref, other_ref, order, pick)
    lanes = 2 * half * rows
    none = jnp.zeros((8, lanes), jnp.float32)
    columns = turned(ref_ref[...])
    ref_cols_ref[...] = columns
    wide[0:width] = columns.astype(jnp.float32)
    wide[width:] = none
    for v in range(views):
        columns = turned(own_ref[v], other_ref[v])
        cols_ref[v] = columns
        src[v, 0:8] = none
        src[v, 8 : 8 + width] = columns.astype(jnp.float32)
        src[v, 8 + width :] = none
    sizes = (planes, rows, 2 * half // GROUPS)
    fill, weigh = volume(
        sizes,
        (shifts, before, after),
        (bias_one, bias_two),
        view_head,
        taps_ref,
        src,
        wide,
        match,
        first,
        band_one,
        band_two,
        ends,
    )
    out_rows = width - MAX_SHIFT
    tall = out_rows + 8
    base = MAX_SHIFT - 2
    total = weighted = 0.0
    for v in range(views):
        fill(v, [(r, 8 + base + r, base + r, min(48, tall - r)) for r in range(0, tall, 48)])
        weight, part = weigh(v, tall, out_rows, lambda v: None)
        total, weighted = total + weight, weighted + part
    late_ref[...] = (weighted / total).astype(jnp.bfloat16)


def outer_body(
    shifts,
    before,
    after,
    bias_one,
    bias_two,
    view_head,
    cols_ref,
    ref_cols_ref,
    late_ref,
    got_ref,
    swapped_ref,
    taps_ref,
    out_ref,
    src,
    wide,
    match,
    first,
    band_one,
    band_two,
    joined,
):
    views, width, lanes = cols_ref.shape
    groups, planes, rows, _ = out_ref.shape
    block = groups * rows
    _, order, is_first_tile, is_last_tile, *ends = position()

    left = jnp.where(order == 0, got_ref[...], swapped_ref[...])
    right = jnp.where(order == 0, swapped_ref[...], got_ref[...])
    for v in range(views):
        src[v, 0:LEAD] = left[v * LEAD : (v + 1) * LEAD].astype(jnp.float32)
        src[v, LEAD : LEAD + width] = cols_ref[v].astype(jnp.float32)
        src[v, LEAD + width :] = right[v * LEAD : v * LEAD + EDGE].astype(jnp.float32)
    wide[0:EDGE] = left[views * LEAD :].astype(jnp.float32)
    wide[EDGE : EDGE + width] = ref_cols_ref[...].astype(jnp.float32)
    wide[EDGE + width :] = right[views * LEAD : views * LEAD + EDGE].astype(jnp.float32)
    fill, weigh = volume(
        (planes, rows, lanes // block),
        (shifts, before, after),
        (bias_one, bias_two),
        view_head,
        taps_ref,
        src,
        wide,
        match,
        first,
        band_one,
        band_two,
        ends,
    )
    main = MAX_SHIFT + 8
    tall = main + 8
    pieces = [(r, LEAD - 2 + r, EDGE - 2 + r, min(48, main - r)) for r in range(0, main, 48)]
    pieces += [(main, LEAD + width - 4, EDGE + width - 4, 8)]
    none = jnp.zeros((1, match.shape[2]), jnp.float32)

    def mend(v):
        @pl.when(is_first_tile)
        def _():
            first[v, 0:1] = none

        @pl.when(is_last_tile)
        def _():
            first[v, main + 3 : main + 4] = none

    total = weighted = 0.0
    for v in range(views):
        fill(v, pieces)
        weight, part = weigh(v, tall, tall, mend)
        total, weighted = total + weight, weighted + part
    part = weighted / total
    joined[0:MAX_SHIFT] = part[0:MAX_SHIFT]
    joined[MAX_SHIFT:] = late_ref[...].astype(jnp.float32)
    joined[MAX_SHIFT : MAX_SHIFT + 2] = part[MAX_SHIFT : MAX_SHIFT + 2]
    joined[width - 2 :] = part[main : main + 2]
    size = planes * block
    to = iota((size, size), 0)
    g, j, h = to // (planes * rows), (to // rows) % planes, to % rows
    perm = ((j * groups + g) * rows + h == iota((size, size), 1)).astype(jnp.bfloat16)
    turned = dot_nt(perm, joined[...].astype(jnp.bfloat16)).astype(jnp.bfloat16)
    out_ref[...] = turned.reshape(groups, planes, rows, width)


def whole(memory):
    return pl.BlockSpec(memory_space=memory)


def swap_planes(value):
    return lax.ppermute(value, "plane", [(0, 1), (1, 0)])


def per_device(ref_feat, src_feat, shifts, conv_one, bias_one, conv_two, bias_two, view_head):
    views, _, rows, width = src_feat.shape
    planes = shifts.shape[1]
    lanes = ref_feat.shape[0] * rows
    tiles, sides = lax.axis_size("tile"), lax.axis_size("plane")
    if sides == 2:
        own, other = src_feat, swap_planes(src_feat)
        before = after = swap_planes(shifts)
    else:
        full = lax.all_gather(src_feat, "plane", axis=1, tiled=True)
        half = full.shape[1] // 2
        own, other = full[:, :half], full[:, half:]
        before = lax.ppermute(shifts, "plane", [(i, i + 1) for i in range(sides - 1)])
        after = lax.ppermute(shifts, "plane", [(i + 1, i) for i in range(sides - 1)])

    bf16, f32 = jnp.bfloat16, jnp.float32
    vmem, smem = pltpu.VMEM, pltpu.SMEM
    packet = pl.pallas_call(
        pack_body,
        out_shape=jax.ShapeDtypeStruct((views * LEAD + EDGE, lanes), bf16),
        in_specs=[whole(vmem)] * 3,
        out_specs=whole(vmem),
        compiler_params=pltpu.CompilerParams(vmem_limit_bytes=8 * 1024 * 1024),
        name="pack_edges",
    )(own, other, ref_feat)

    pairs = [(sides * i, sides * (i + 1)) for i in range(tiles - 1)]
    pairs += [(sides * (i + 1) + 1, sides * i + 1) for i in range(tiles - 1)]
    got = lax.ppermute(packet, ("tile", "plane"), pairs)
    if sides == 2:
        swapped = swap_planes(got)
    else:
        both = lax.all_gather(got, "plane", axis=0)
        got, swapped = both[0], both[1]

    def taps(kernel):
        flipped = jnp.flip(kernel, axis=2)
        return jnp.transpose(flipped, (3, 4, 1, 2, 0)).reshape(9 * GROUPS, 3 * GROUPS)

    both_taps = jnp.stack([taps(conv_one), taps(conv_two)])
    own, other, before, after, both_taps, packet = lax.optimization_barrier(
        (own, other, before, after, both_taps, packet)
    )
    del packet
    span = (planes + 4) * GROUPS * rows
    out_lanes = planes * GROUPS * rows
    late_rows = width - MAX_SHIFT
    scalars = (shifts, before, after, bias_one, bias_two, view_head)
    bands = [pltpu.VMEM((3 * span, out_lanes), bf16)] * 2
    params = pltpu.CompilerParams(vmem_limit_bytes=24 * 1024 * 1024)
    cols, ref_cols, late = pl.pallas_call(
        inner_body,
        out_shape=[
            jax.ShapeDtypeStruct((views, width, lanes), bf16),
            jax.ShapeDtypeStruct((width, lanes), bf16),
            jax.ShapeDtypeStruct((late_rows, out_lanes), bf16),
        ],
        in_specs=[whole(smem)] * 6 + [whole(vmem)] * 4,
        out_specs=[whole(vmem)] * 3,
        scratch_shapes=[
            pltpu.VMEM((views, width + 16, lanes), f32),
            pltpu.VMEM((width + 8, lanes), f32),
            pltpu.VMEM((views, late_rows + 16, span), f32),
            pltpu.VMEM((views, late_rows + 16, span), f32),
        ]
        + bands,
        compiler_params=params,
        cost_estimate=pl.CostEstimate(
            flops=5 * 10**9, bytes_accessed=10**6, transcendentals=10**5
        ),
        name="inner_columns",
    )(*scalars, own, other, ref_feat, both_taps)
    return pl.pallas_call(
        outer_body,
        out_shape=jax.ShapeDtypeStruct((GROUPS, planes, rows, width), bf16),
        in_specs=[whole(smem)] * 6 + [whole(vmem)] * 6,
        out_specs=whole(vmem),
        scratch_shapes=[
            pltpu.VMEM((views, LEAD + width + EDGE, lanes), f32),
            pltpu.VMEM((EDGE + width + EDGE, lanes), f32),
            pltpu.VMEM((views, MAX_SHIFT + 24, span), f32),
            pltpu.VMEM((views, MAX_SHIFT + 24, span), f32),
        ]
        + bands
        + [pltpu.VMEM((width, out_lanes), f32)],
        compiler_params=params,
        name="outer_columns",
    )(*scalars, cols, ref_cols, late, got, swapped, both_taps)


def solution(mesh):
    placed = (
        P(None, None, "tile"),
        P(None, "plane", None, "tile"),
        P(None, "plane"),
        P(),
        P(),
        P(),
        P(),
        P(),
    )
    return jax.shard_map(
        per_device,
        mesh=mesh,
        in_specs=placed,
        out_specs=P(None, "plane", None, "tile"),
        check_vma=False,
    )
```

```python
import jax
import jax.numpy as jnp
from jax import lax
from jax.experimental import pallas as pl
from jax.experimental.pallas import tpu as pltpu
from jax.sharding import PartitionSpec as P

GROUPS = 8
MAX_SHIFT = 128
LEAD = MAX_SHIFT + 16
EDGE = 16
FAR = -3.0e38


def iota(shape, dim):
    return lax.broadcasted_iota(jnp.int32, shape, dim)


def dot(left, right):
    return jnp.dot(left, right, preferred_element_type=jnp.float32)


def dot_nt(left, right):
    return lax.dot_general(
        left, right, (((1,), (1,)), ((), ())), preferred_element_type=jnp.float32
    )


def position():
    tile, plane = lax.axis_index("tile"), lax.axis_index("plane")
    tiles, sides = lax.axis_size("tile"), lax.axis_size("plane")
    order = plane if sides == 2 else 0 * plane
    role = jnp.minimum(plane, 1)
    return role, order, tile == 0, tile == tiles - 1, plane == 0, plane == sides - 1


def columns_of(count, width, start):
    picked = iota((count, width), 0) + start == iota((count, width), 1)
    return picked.astype(jnp.bfloat16)


def lane_order(half, rows, side):
    lanes = 2 * half * rows
    inner = 2 * half // GROUPS
    at, to = iota((lanes, 2 * lanes), 0), iota((lanes, 2 * lanes), 1)
    k, g = (to // (GROUPS * rows)) % inner, (to // rows) % GROUPS
    channel = g * inner + k - half * side
    row = (to // lanes) * (half * rows) + channel * rows + to % rows
    held = (channel >= 0) & (channel < half) & (row == at)
    return held.astype(jnp.bfloat16)


def ref_order(lanes, rows):
    at, to = iota((lanes, lanes), 0), iota((lanes, lanes), 1)
    k, g, h = to // (GROUPS * rows), (to // rows) % GROUPS, to % rows
    return ((g * (lanes // (GROUPS * rows)) + k) * rows + h == at).astype(jnp.bfloat16)


def turned_half(half_ref, pick, side):
    views, half, rows, width = half_ref.shape
    lanes = 2 * half * rows
    block = half_ref[...].reshape(views * half * rows, width)
    columns = dot_nt(pick, block).astype(jnp.bfloat16)
    order = lane_order(half, rows, side)
    return [dot(columns[:, i : i + lanes], order) for i in range(0, columns.shape[1], lanes)]


def turned_ref(ref_ref, pick):
    channels, rows, width = ref_ref.shape
    lanes = channels * rows
    columns = dot_nt(pick, ref_ref[...].reshape(lanes, width)).astype(jnp.bfloat16)
    return dot(columns, ref_order(lanes, rows))


def edge_start(role, width, count):
    return jnp.where(role == 0, width - count, 0)


def store_pairs(target_ref, pairs):
    lanes = target_ref.shape[1]
    for i, pair in enumerate(pairs):
        for k in range(2):
            at = (2 * i + k) * LEAD
            part = pair[:, k * lanes : (k + 1) * lanes]
            target_ref[at : at + LEAD] = part.astype(jnp.bfloat16)


def pack_own_body(own_ref, ref_ref, part_ref):
    width = own_ref.shape[3]
    role, order, *_ = position()
    pick = columns_of(LEAD, width, edge_start(role, width, LEAD))
    store_pairs(part_ref, turned_half(own_ref, pick, order))
    pick = columns_of(EDGE, width, edge_start(role, width, EDGE))
    part_ref[own_ref.shape[0] * LEAD :] = turned_ref(ref_ref, pick).astype(jnp.bfloat16)


def pack_other_body(part_ref, other_ref, packet_ref):
    width = other_ref.shape[3]
    lanes = packet_ref.shape[1]
    role, order, *_ = position()
    pick = columns_of(LEAD, width, edge_start(role, width, LEAD))
    pairs = turned_half(other_ref, pick, 1 - order)
    for i, pair in enumerate(pairs):
        for k in range(2):
            at = (2 * i + k) * LEAD
            part = pair[:, k * lanes : (k + 1) * lanes]
            both = part_ref[at : at + LEAD].astype(jnp.float32) + part
            packet_ref[at : at + LEAD] = both.astype(jnp.bfloat16)
    at = other_ref.shape[0] * LEAD
    packet_ref[at:] = part_ref[at:]


def lane_table(values_ref, rows, lane):
    which = (lane // rows) % GROUPS
    table = jnp.zeros(lane.shape, jnp.float32)
    for o in range(GROUPS):
        table = jnp.where(which == o, values_ref[o], table)
    return table


def build_band(taps_ref, which, band_ref, rows):
    block = GROUPS * rows
    spread = iota((3 * GROUPS, 128), 1) // rows == iota((3 * GROUPS, 128), 0)
    wide = dot(taps_ref[which], spread.astype(jnp.bfloat16)).astype(jnp.bfloat16)
    stretch = (iota((block, GROUPS), 0) // rows == iota((block, GROUPS), 1)).astype(jnp.bfloat16)
    lane = iota((block, 128), 1)
    gap = iota((block, 128), 0) % rows - lane % rows + 1
    depth, out_lanes = band_ref.shape[0] // 3, band_ref.shape[1]
    per_tile = 128 // block
    zero = jnp.zeros((block, 128), jnp.bfloat16)
    for e in range(3):
        base = jnp.zeros((block, 128), jnp.float32)
        for b in range(3):
            at = (b * 3 + e) * GROUPS
            base = jnp.where(gap == b, dot(stretch, wide[at : at + GROUPS]), base)
        for j in range(depth // block):
            offset = j - 2
            first, turn = offset // per_tile, offset % per_tile
            moved = pltpu.roll(base, turn * block, 1) if turn else base
            for t in range(out_lanes // 128):
                if t == first:
                    part = jnp.where(lane >= turn * block, moved, 0.0).astype(jnp.bfloat16)
                elif t == first + 1 and turn > per_tile - 3:
                    part = jnp.where(lane < turn * block, moved, 0.0).astype(jnp.bfloat16)
                else:
                    part = zero
                at = e * depth + j * block
                band_ref[at : at + block, t * 128 : (t + 1) * 128] = part


def build_tables(planes, rows, inner, bias_one, bias_two, view_head, ends, table_ref, spread_ref):
    block = GROUPS * rows
    out_lanes = planes * block
    span = table_ref.shape[1]
    is_first_plane, is_last_plane = ends
    at = iota((1, span), 1)
    plane = at // block
    outside = ((plane < 2) & is_first_plane) | ((plane >= planes + 2) & is_last_plane)
    table_ref[0:1] = jnp.where(outside, 0.0, 1.0 / inner)
    outside = ((plane == 0) & is_first_plane) | ((plane == planes + 1) & is_last_plane)
    table_ref[1:2] = jnp.where(outside, FAR, lane_table(bias_one, rows, at))
    table_ref[2:3] = lane_table(bias_two, rows, at)
    table_ref[3:4] = lane_table(view_head, rows, at)
    row, lane = iota((out_lanes, out_lanes), 0), iota((out_lanes, out_lanes), 1)
    same = ((row // block == lane // block) & (row % rows == lane % rows)).astype(jnp.bfloat16)
    spread_ref[0:out_lanes] = same
    spread_ref[out_lanes:] = same


def fill(v, pieces, shift_of, src, wide, match, table_ref, block):
    for at, src_at, wide_at, count in pieces:
        quarter = iota((count, 128), 1) // block
        lower, middle, even = quarter < 2, (quarter == 1) | (quarter == 2), quarter % 2 == 0
        here = wide[wide_at : wide_at + count]
        for q in range(match.shape[1] // 128):

            def product(j):
                return src[v, pl.ds(src_at - shift_of(v, q * 4 + j - 2), count)] * here

            a, c, b, d = (product(j) for j in range(4))
            x = jnp.where(lower, a, b) + pltpu.roll(jnp.where(lower, b, a), 64, 1)
            z = jnp.where(middle, c, d) + pltpu.roll(jnp.where(middle, d, c), 64, 1)
            y = jnp.where(even, x, z) + pltpu.roll(jnp.where(even, z, x), 96, 1)
            y = y * table_ref[0:1, q * 128 : (q + 1) * 128]
            y = y.astype(jnp.bfloat16).astype(jnp.float32)
            match[at : at + count, q * 128 : (q + 1) * 128] = y


def weigh(views, tall, planes, block, match, first, table_ref, band_one, band_two, spread_ref, mend):
    out_lanes = planes * block
    span = match.shape[1]
    rest = span - out_lanes
    high = views * tall
    moved = [match[e : e + high].astype(jnp.bfloat16) for e in range(3)]
    raw = dot(jnp.concatenate(moved, axis=1), band_one[...])
    raw = jnp.maximum(raw + table_ref[1:2, 0:out_lanes], 0.0)
    first[0:high, 0:out_lanes] = raw.astype(jnp.bfloat16).astype(jnp.float32)
    raw = sum(
        dot(moved[e][:, out_lanes:], band_one[e * span : e * span + rest, 0:rest])
        for e in range(3)
    )
    raw = jnp.maximum(raw + table_ref[1:2, out_lanes:], 0.0)
    first[0:high, out_lanes:] = raw.astype(jnp.bfloat16).astype(jnp.float32)
    mend()
    moved = [first[e : e + high].astype(jnp.bfloat16) for e in range(3)]
    second = dot(jnp.concatenate(moved, axis=1), band_two[...])
    second = jnp.maximum(second + table_ref[2:3, 0:out_lanes], 0.0) * table_ref[3:4, 0:out_lanes]
    upper = second.astype(jnp.bfloat16)
    under = (second - upper.astype(jnp.float32)).astype(jnp.bfloat16)
    score = dot(jnp.concatenate([upper, under], axis=1), spread_ref[...])
    weight = 1.0 / (1.0 + jnp.exp(-score))
    total = weighted = 0.0
    for v in range(views):
        part = weight[v * tall : (v + 1) * tall]
        at = v * tall + 2
        total = total + part
        weighted = weighted + part * match[at : at + tall, 2 * block : 2 * block + out_lanes]
    return weighted / total


def shift_reader(shifts, before, after):
    planes = shifts.shape[1]

    def shift_of(v, d):
        if d < 0:
            return before[v, planes + d]
        return shifts[v, d] if d < planes else after[v, d - planes]

    return shift_of


def inner_body(
    shifts,
    before,
    after,
    bias_one,
    bias_two,
    view_head,
    own_ref,
    other_ref,
    ref_ref,
    taps_ref,
    cols_ref,
    ref_cols_ref,
    late_ref,
    table_ref,
    spread_ref,
    band_one,
    band_two,
    src,
    wide,
    match,
    first,
):
    views, half, rows, width = own_ref.shape
    planes = shifts.shape[1]
    lanes = 2 * half * rows
    inner = 2 * half // GROUPS
    block = GROUPS * rows
    _, order, _, _, *ends = position()
    pick = columns_of(width, width, 0)
    none = jnp.zeros((8, lanes), jnp.float32)
    columns = turned_ref(ref_ref, pick)
    ref_cols_ref[...] = columns.astype(jnp.bfloat16)
    wide[0:width] = columns
    wide[width:] = none
    pairs = zip(turned_half(own_ref, pick, order), turned_half(other_ref, pick, 1 - order))
    for i, (low, high) in enumerate(pairs):
        columns = low + high
        for k in range(2):
            v = 2 * i + k
            part = columns[:, k * lanes : (k + 1) * lanes]
            cols_ref[v] = part.astype(jnp.bfloat16)
            src[v, 0:8] = none
            src[v, 8 : 8 + width] = part
            src[v, 8 + width :] = none
    build_tables(
        planes, rows, inner, bias_one, bias_two, view_head, ends, table_ref, spread_ref
    )
    build_band(taps_ref, 0, band_one, rows)
    build_band(taps_ref, 1, band_two, rows)
    shift_of = shift_reader(shifts, before, after)
    out_rows = width - MAX_SHIFT
    tall = out_rows + 8
    base = MAX_SHIFT - 2
    for v in range(views):
        pieces = [
            (v * tall + r, 8 + base + r, base + r, min(48, tall - r)) for r in range(0, tall, 48)
        ]
        fill(v, pieces, shift_of, src, wide, match, table_ref, block)
    joined = weigh(
        views,
        tall,
        planes,
        block,
        match,
        first,
        table_ref,
        band_one,
        band_two,
        spread_ref,
        lambda: None,
    )
    late_ref[...] = joined[0:out_rows].astype(jnp.bfloat16)


def outer_body(
    shifts,
    before,
    after,
    cols_ref,
    ref_cols_ref,
    late_ref,
    table_ref,
    spread_ref,
    band_one,
    band_two,
    got_ref,
    swapped_ref,
    out_ref,
    src,
    wide,
    match,
    first,
    joined,
):
    views, width, lanes = cols_ref.shape
    groups, planes, rows, _ = out_ref.shape
    block = groups * rows
    _, order, is_first_tile, is_last_tile, *_ = position()

    left = jnp.where(order == 0, got_ref[...], swapped_ref[...])
    right = jnp.where(order == 0, swapped_ref[...], got_ref[...])
    for v in range(views):
        src[v, 0:LEAD] = left[v * LEAD : (v + 1) * LEAD].astype(jnp.float32)
        src[v, LEAD : LEAD + width] = cols_ref[v].astype(jnp.float32)
        src[v, LEAD + width :] = right[v * LEAD : v * LEAD + EDGE].astype(jnp.float32)
    wide[0:EDGE] = left[views * LEAD :].astype(jnp.float32)
    wide[EDGE : EDGE + width] = ref_cols_ref[...].astype(jnp.float32)
    wide[EDGE + width :] = right[views * LEAD : views * LEAD + EDGE].astype(jnp.float32)
    main = MAX_SHIFT + 8
    tall = main + 8
    shift_of = shift_reader(shifts, before, after)
    for v in range(views):
        at = v * tall
        pieces = [
            (at + r, LEAD - 2 + r, EDGE - 2 + r, min(48, main - r)) for r in range(0, main, 48)
        ]
        pieces += [(at + main, LEAD + width - 4, EDGE + width - 4, 8)]
        fill(v, pieces, shift_of, src, wide, match, table_ref, block)
    none = jnp.zeros((1, match.shape[1]), jnp.float32)

    def mend():
        for v in range(views):
            for row, at_end in ((v * tall, is_first_tile), (v * tall + main + 3, is_last_tile)):
                first[row : row + 1] = jnp.where(at_end, none, first[row : row + 1])

    part = weigh(
        views,
        tall,
        planes,
        block,
        match,
        first,
        table_ref,
        band_one,
        band_two,
        spread_ref,
        mend,
    )
    joined[0:MAX_SHIFT] = part[0:MAX_SHIFT]
    joined[MAX_SHIFT:] = late_ref[...].astype(jnp.float32)
    joined[MAX_SHIFT : MAX_SHIFT + 2] = part[MAX_SHIFT : MAX_SHIFT + 2]
    joined[width - 2 :] = part[main : main + 2]
    size = planes * block
    to = iota((size, size), 0)
    g, j, h = to // (planes * rows), (to // rows) % planes, to % rows
    perm = ((j * groups + g) * rows + h == iota((size, size), 1)).astype(jnp.bfloat16)
    turned = dot_nt(perm, joined[...].astype(jnp.bfloat16)).astype(jnp.bfloat16)
    out_ref[...] = turned.reshape(groups, planes, rows, width)


def whole(memory):
    return pl.BlockSpec(memory_space=memory)


def limit(mebibytes):
    return pltpu.CompilerParams(vmem_limit_bytes=mebibytes * 1024 * 1024)


def swap_planes(value):
    return lax.ppermute(value, "plane", [(0, 1), (1, 0)])


def per_device(ref_feat, src_feat, shifts, conv_one, bias_one, conv_two, bias_two, view_head):
    views, _, rows, width = src_feat.shape
    planes = shifts.shape[1]
    lanes = ref_feat.shape[0] * rows
    tiles, sides = lax.axis_size("tile"), lax.axis_size("plane")
    bf16, f32 = jnp.bfloat16, jnp.float32
    vmem, smem = pltpu.VMEM, pltpu.SMEM
    shape = jax.ShapeDtypeStruct
    if sides == 2:
        own, other = src_feat, swap_planes(src_feat)
    else:
        full = lax.all_gather(src_feat, "plane", axis=1, tiled=True)
        half = full.shape[1] // 2
        own, other = full[:, :half], full[:, half:]

    packet_shape = shape((views * LEAD + EDGE, lanes), bf16)
    part = pl.pallas_call(
        pack_own_body,
        out_shape=packet_shape,
        in_specs=[whole(vmem)] * 2,
        out_specs=whole(vmem),
        compiler_params=limit(8),
        name="pack_own",
    )(own, ref_feat)
    packet = pl.pallas_call(
        pack_other_body,
        out_shape=packet_shape,
        in_specs=[whole(vmem)] * 2,
        out_specs=whole(vmem),
        compiler_params=limit(8),
        name="pack_other",
    )(part, other)

    pairs = [(sides * i, sides * (i + 1)) for i in range(tiles - 1)]
    pairs += [(sides * (i + 1) + 1, sides * i + 1) for i in range(tiles - 1)]
    got = lax.ppermute(packet, ("tile", "plane"), pairs)

    own, other, shifts, conv_one, conv_two, packet = lax.optimization_barrier(
        (own, other, shifts, conv_one, conv_two, packet)
    )
    if sides == 2:
        before = after = swap_planes(shifts)
    else:
        before = lax.ppermute(shifts, "plane", [(i, i + 1) for i in range(sides - 1)])
        after = lax.ppermute(shifts, "plane", [(i + 1, i) for i in range(sides - 1)])

    def taps(kernel):
        flipped = jnp.flip(kernel, axis=2)
        return jnp.transpose(flipped, (3, 4, 1, 2, 0)).reshape(9 * GROUPS, 3 * GROUPS)

    both_taps = jnp.stack([taps(conv_one), taps(conv_two)])
    span = (planes + 4) * GROUPS * rows
    out_lanes = planes * GROUPS * rows
    late_rows = width - MAX_SHIFT
    high = views * (late_rows + 8) + 8
    inner = pl.pallas_call(
        inner_body,
        out_shape=[
            shape((views, width, lanes), bf16),
            shape((width, lanes), bf16),
            shape((late_rows, out_lanes), bf16),
            shape((8, span), f32),
            shape((2 * out_lanes, out_lanes), bf16),
            shape((3 * span, out_lanes), bf16),
            shape((3 * span, out_lanes), bf16),
        ],
        in_specs=[whole(smem)] * 6 + [whole(vmem)] * 4,
        out_specs=[whole(vmem)] * 7,
        scratch_shapes=[
            pltpu.VMEM((views, width + 16, lanes), f32),
            pltpu.VMEM((width + 8, lanes), f32),
            pltpu.VMEM((high, span), f32),
            pltpu.VMEM((high, span), f32),
        ],
        compiler_params=limit(24),
        cost_estimate=pl.CostEstimate(
            flops=5 * 10**9, bytes_accessed=10**6, transcendentals=10**5
        ),
        name="inner_columns",
    )(shifts, before, after, bias_one, bias_two, view_head, own, other, ref_feat, both_taps)
    got, *inner = lax.optimization_barrier((got, *inner))
    if sides == 2:
        swapped = swap_planes(got)
    else:
        both = lax.all_gather(got, "plane", axis=0)
        got, swapped = both[0], both[1]
    high = views * (MAX_SHIFT + 16) + 8
    return pl.pallas_call(
        outer_body,
        out_shape=shape((GROUPS, planes, rows, width), bf16),
        in_specs=[whole(smem)] * 3 + [whole(vmem)] * 9,
        out_specs=whole(vmem),
        scratch_shapes=[
            pltpu.VMEM((views, LEAD + width + EDGE, lanes), f32),
            pltpu.VMEM((EDGE + width + EDGE, lanes), f32),
            pltpu.VMEM((high, span), f32),
            pltpu.VMEM((high, span), f32),
            pltpu.VMEM((width, out_lanes), f32),
        ],
        compiler_params=limit(24),
        name="outer_columns",
    )(shifts, before, after, *inner, got, swapped)


def solution(mesh):
    placed = (
        P(None, None, "tile"),
        P(None, "plane", None, "tile"),
        P(None, "plane"),
        P(),
        P(),
        P(),
        P(),
        P(),
    )
    return jax.shard_map(
        per_device,
        mesh=mesh,
        in_specs=placed,
        out_specs=P(None, "plane", None, "tile"),
        check_vma=False,
    )
```

```python
import jax
import jax.numpy as jnp
from jax import lax
from jax.experimental import pallas as pl
from jax.experimental.pallas import tpu as pltpu
from jax.sharding import PartitionSpec as P

GROUPS = 8
MAX_SHIFT = 128
LEAD = MAX_SHIFT + 16
EDGE = 16
BATCH = 2
FAR = -3.0e38


def iota(shape, dim):
    return lax.broadcasted_iota(jnp.int32, shape, dim)


def dot(left, right):
    return jnp.dot(left, right, preferred_element_type=jnp.float32)


def dot_nt(left, right):
    return lax.dot_general(
        left, right, (((1,), (1,)), ((), ())), preferred_element_type=jnp.float32
    )


def position():
    tile, plane = lax.axis_index("tile"), lax.axis_index("plane")
    tiles, sides = lax.axis_size("tile"), lax.axis_size("plane")
    order = plane if sides == 2 else 0 * plane
    role = jnp.minimum(plane, 1)
    return role, order, tile == 0, tile == tiles - 1, plane == 0, plane == sides - 1


def columns_of(count, width, start):
    picked = iota((count, width), 0) + start == iota((count, width), 1)
    return picked.astype(jnp.bfloat16)


def lane_order(half, rows, side):
    lanes = 2 * half * rows
    inner = 2 * half // GROUPS
    at, to = iota((lanes, 2 * lanes), 0), iota((lanes, 2 * lanes), 1)
    k, g = (to // (GROUPS * rows)) % inner, (to // rows) % GROUPS
    channel = g * inner + k - half * side
    row = (to // lanes) * (half * rows) + channel * rows + to % rows
    held = (channel >= 0) & (channel < half) & (row == at)
    return held.astype(jnp.bfloat16)


def ref_order(lanes, rows):
    at, to = iota((lanes, lanes), 0), iota((lanes, lanes), 1)
    k, g, h = to // (GROUPS * rows), (to // rows) % GROUPS, to % rows
    return ((g * (lanes // (GROUPS * rows)) + k) * rows + h == at).astype(jnp.bfloat16)


def turned_half(half_ref, pick, side):
    views, half, rows, width = half_ref.shape
    lanes = 2 * half * rows
    block = half_ref[...].reshape(views * half * rows, width)
    columns = dot_nt(pick, block).astype(jnp.bfloat16)
    order = lane_order(half, rows, side)
    return [dot(columns[:, i : i + lanes], order) for i in range(0, columns.shape[1], lanes)]


def turned_ref(ref_ref, pick):
    channels, rows, width = ref_ref.shape
    lanes = channels * rows
    columns = dot_nt(pick, ref_ref[...].reshape(lanes, width)).astype(jnp.bfloat16)
    return dot(columns, ref_order(lanes, rows))


def edge_start(role, width, count):
    return jnp.where(role == 0, width - count, 0)


def store_pairs(target_ref, pairs):
    lanes = target_ref.shape[1]
    for i, pair in enumerate(pairs):
        for k in range(2):
            at = (2 * i + k) * LEAD
            part = pair[:, k * lanes : (k + 1) * lanes]
            target_ref[at : at + LEAD] = part.astype(jnp.bfloat16)


def pack_own_body(own_hbm, ref_hbm, part_ref, own_ref, ref_ref, sems):
    copies = [
        pltpu.make_async_copy(own_hbm, own_ref, sems.at[0]),
        pltpu.make_async_copy(ref_hbm, ref_ref, sems.at[1]),
    ]
    for copy in copies:
        copy.start()
    width = own_ref.shape[3]
    role, order, *_ = position()
    pick = columns_of(LEAD, width, edge_start(role, width, LEAD))
    pick_ref = columns_of(EDGE, width, edge_start(role, width, EDGE))
    copies[0].wait()
    store_pairs(part_ref, turned_half(own_ref, pick, order))
    copies[1].wait()
    part_ref[own_ref.shape[0] * LEAD :] = turned_ref(ref_ref, pick_ref).astype(jnp.bfloat16)


def pack_other_body(part_ref, other_ref, packet_ref):
    width = other_ref.shape[3]
    lanes = packet_ref.shape[1]
    role, order, *_ = position()
    pick = columns_of(LEAD, width, edge_start(role, width, LEAD))
    pairs = turned_half(other_ref, pick, 1 - order)
    for i, pair in enumerate(pairs):
        for k in range(2):
            at = (2 * i + k) * LEAD
            part = pair[:, k * lanes : (k + 1) * lanes]
            both = part_ref[at : at + LEAD].astype(jnp.float32) + part
            packet_ref[at : at + LEAD] = both.astype(jnp.bfloat16)
    at = other_ref.shape[0] * LEAD
    packet_ref[at:] = part_ref[at:]


def lane_table(values_ref, rows, lane):
    which = (lane // rows) % GROUPS
    table = jnp.zeros(lane.shape, jnp.float32)
    for o in range(GROUPS):
        table = jnp.where(which == o, values_ref[o], table)
    return table


def build_band(taps_ref, which, band_ref, rows):
    block = GROUPS * rows
    spread = iota((3 * GROUPS, 128), 1) // rows == iota((3 * GROUPS, 128), 0)
    wide = dot(taps_ref[which], spread.astype(jnp.bfloat16)).astype(jnp.bfloat16)
    stretch = (iota((block, GROUPS), 0) // rows == iota((block, GROUPS), 1)).astype(jnp.bfloat16)
    lane = iota((block, 128), 1)
    gap = iota((block, 128), 0) % rows - lane % rows + 1
    depth, out_lanes = band_ref.shape[0] // 3, band_ref.shape[1]
    per_tile = 128 // block
    zero = jnp.zeros((block, 128), jnp.bfloat16)
    for e in range(3):
        base = jnp.zeros((block, 128), jnp.float32)
        for b in range(3):
            at = (b * 3 + e) * GROUPS
            base = jnp.where(gap == b, dot(stretch, wide[at : at + GROUPS]), base)
        for j in range(depth // block):
            offset = j - 2
            first, turn = offset // per_tile, offset % per_tile
            moved = pltpu.roll(base, turn * block, 1) if turn else base
            for t in range(out_lanes // 128):
                if t == first:
                    part = jnp.where(lane >= turn * block, moved, 0.0).astype(jnp.bfloat16)
                elif t == first + 1 and turn > per_tile - 3:
                    part = jnp.where(lane < turn * block, moved, 0.0).astype(jnp.bfloat16)
                else:
                    part = zero
                at = e * depth + j * block
                band_ref[at : at + block, t * 128 : (t + 1) * 128] = part


def build_tables(planes, rows, inner, bias_one, bias_two, view_head, ends, table_ref, spread_ref):
    block = GROUPS * rows
    out_lanes = planes * block
    span = table_ref.shape[1]
    is_first_plane, is_last_plane = ends
    at = iota((1, span), 1)
    plane = at // block
    outside = ((plane < 2) & is_first_plane) | ((plane >= planes + 2) & is_last_plane)
    table_ref[0:1] = jnp.where(outside, 0.0, 1.0 / inner)
    outside = ((plane == 0) & is_first_plane) | ((plane == planes + 1) & is_last_plane)
    table_ref[1:2] = jnp.where(outside, FAR, lane_table(bias_one, rows, at))
    table_ref[2:3] = lane_table(bias_two, rows, at)
    table_ref[3:4] = lane_table(view_head, rows, at)
    row, lane = iota((out_lanes, out_lanes), 0), iota((out_lanes, out_lanes), 1)
    same = ((row // block == lane // block) & (row % rows == lane % rows)).astype(jnp.bfloat16)
    spread_ref[0:out_lanes] = same
    spread_ref[out_lanes:] = same


def fill(pieces, near, src, wide, match, table_ref, block):
    for at, src_at, wide_at, count in pieces:
        quarter = iota((count, 128), 1) // block
        lower, middle, even = quarter < 2, (quarter == 1) | (quarter == 2), quarter % 2 == 0
        here = wide[wide_at : wide_at + count]
        for q in range(match.shape[1] // 128):

            def product(j):
                return src[pl.ds(src_at - near[q * 4 + j], count)] * here

            a, c, b, d = (product(j) for j in range(4))
            x = jnp.where(lower, a, b) + pltpu.roll(jnp.where(lower, b, a), 64, 1)
            z = jnp.where(middle, c, d) + pltpu.roll(jnp.where(middle, d, c), 64, 1)
            y = jnp.where(even, x, z) + pltpu.roll(jnp.where(even, z, x), 96, 1)
            y = y * table_ref[0:1, q * 128 : (q + 1) * 128]
            y = y.astype(jnp.bfloat16).astype(jnp.float32)
            match[at : at + count, q * 128 : (q + 1) * 128] = y


def convolve_first(low, high, planes, block, match, first, table_ref, band_one):
    out_lanes = planes * block
    span = match.shape[1]
    rest = span - out_lanes
    moved = [match[low + e : high + e].astype(jnp.bfloat16) for e in range(3)]
    raw = dot(jnp.concatenate(moved, axis=1), band_one[...])
    raw = jnp.maximum(raw + table_ref[1:2, 0:out_lanes], 0.0)
    first[low:high, 0:out_lanes] = raw.astype(jnp.bfloat16).astype(jnp.float32)
    raw = sum(
        dot(moved[e][:, out_lanes:], band_one[e * span : e * span + rest, 0:rest])
        for e in range(3)
    )
    raw = jnp.maximum(raw + table_ref[1:2, out_lanes:], 0.0)
    first[low:high, out_lanes:] = raw.astype(jnp.bfloat16).astype(jnp.float32)


def weights(low, high, planes, block, first, table_ref, band_two, spread_ref):
    out_lanes = planes * block
    moved = [first[low + e : high + e].astype(jnp.bfloat16) for e in range(3)]
    second = dot(jnp.concatenate(moved, axis=1), band_two[...])
    second = jnp.maximum(second + table_ref[2:3, 0:out_lanes], 0.0) * table_ref[3:4, 0:out_lanes]
    upper = second.astype(jnp.bfloat16)
    under = (second - upper.astype(jnp.float32)).astype(jnp.bfloat16)
    score = dot(jnp.concatenate([upper, under], axis=1), spread_ref[...])
    return 1.0 / (1.0 + jnp.exp(-score))


def blend(views, tall, batch, planes, block, filled, mend, match, first, tables):
    table_ref, band_one, band_two, spread_ref = tables
    out_lanes = planes * block
    starts = range(0, views, batch)
    for at in starts:
        for v in range(at, at + batch):
            filled(v)
        convolve_first(
            at * tall, (at + batch) * tall, planes, block, match, first, table_ref, band_one
        )
        for v in range(at, at + batch):
            mend(v * tall)
    total = weighted = 0.0
    for at in starts:
        weight = weights(
            at * tall, (at + batch) * tall, planes, block, first, table_ref, band_two, spread_ref
        )
        for v in range(batch):
            part = weight[v * tall : (v + 1) * tall]
            row = (at + v) * tall + 2
            total = total + part
            weighted = weighted + part * match[row : row + tall, 2 * block : 2 * block + out_lanes]
    return weighted / total


def pack_shifts(shifts, before, after, word_ref):
    for row, ref in enumerate((before, shifts, after)):
        word = ref[0:1]
        for v in range(1, ref.shape[0]):
            word = word | (ref[v : v + 1] << (8 * v))
        word_ref[row : row + 1, 0 : word.shape[1]] = word


def read_shifts(views, planes, word_ref):
    at = [(0, planes - 2), (0, planes - 1)] + [(1, d) for d in range(planes)] + [(2, 0), (2, 1)]
    words = [word_ref[row, d] for row, d in at]
    return [[(word >> (8 * v)) & 255 for word in words] for v in range(views)]


def inner_body(
    shifts,
    before,
    after,
    bias_one,
    bias_two,
    view_head,
    own_ref,
    other_ref,
    ref_ref,
    taps_ref,
    cols_ref,
    ref_cols_ref,
    late_ref,
    word_ref,
    table_ref,
    spread_ref,
    band_one,
    band_two,
    src,
    wide,
    match,
    first,
):
    views, half, rows, width = own_ref.shape
    planes = shifts.shape[1]
    lanes = 2 * half * rows
    inner = 2 * half // GROUPS
    block = GROUPS * rows
    _, order, _, _, *ends = position()
    pick = columns_of(width, width, 0)
    none = jnp.zeros((8, lanes), jnp.float32)
    columns = turned_ref(ref_ref, pick)
    ref_cols_ref[...] = columns.astype(jnp.bfloat16)
    wide[0:width] = columns
    wide[width:] = none
    pairs = zip(turned_half(own_ref, pick, order), turned_half(other_ref, pick, 1 - order))
    for i, (low, high) in enumerate(pairs):
        columns = low + high
        for k in range(2):
            v = 2 * i + k
            part = columns[:, k * lanes : (k + 1) * lanes]
            cols_ref[v] = part.astype(jnp.bfloat16)
            src[v, 0:8] = none
            src[v, 8 : 8 + width] = part
            src[v, 8 + width :] = none
    build_tables(
        planes, rows, inner, bias_one, bias_two, view_head, ends, table_ref, spread_ref
    )
    build_band(taps_ref, 0, band_one, rows)
    build_band(taps_ref, 1, band_two, rows)
    pack_shifts(shifts, before, after, word_ref)
    near = read_shifts(views, planes, word_ref)
    out_rows = width - MAX_SHIFT
    tall = out_rows + 8
    base = MAX_SHIFT - 2

    def filled(v):
        pieces = [
            (v * tall + r, 8 + base + r, base + r, min(48, tall - r)) for r in range(0, tall, 48)
        ]
        fill(pieces, near[v], src.at[v], wide, match, table_ref, block)

    tables = table_ref, band_one, band_two, spread_ref
    joined = blend(
        views, tall, BATCH, planes, block, filled, lambda row: None, match, first, tables
    )
    late_ref[...] = joined[0:out_rows].astype(jnp.bfloat16)


def outer_body(
    cols_ref,
    ref_cols_ref,
    late_ref,
    word_ref,
    table_ref,
    spread_ref,
    band_one,
    band_two,
    got_ref,
    swapped_ref,
    out_ref,
    src,
    wide,
    match,
    first,
    joined,
):
    views, width, lanes = cols_ref.shape
    groups, planes, rows, _ = out_ref.shape
    block = groups * rows
    _, order, is_first_tile, is_last_tile, *_ = position()

    near = read_shifts(views, planes, word_ref)
    left = jnp.where(order == 0, got_ref[...], swapped_ref[...])
    right = jnp.where(order == 0, swapped_ref[...], got_ref[...])
    for v in range(views):
        src[v, 0:LEAD] = left[v * LEAD : (v + 1) * LEAD].astype(jnp.float32)
        src[v, LEAD : LEAD + width] = cols_ref[v].astype(jnp.float32)
        src[v, LEAD + width :] = right[v * LEAD : v * LEAD + EDGE].astype(jnp.float32)
    wide[0:EDGE] = left[views * LEAD :].astype(jnp.float32)
    wide[EDGE : EDGE + width] = ref_cols_ref[...].astype(jnp.float32)
    wide[EDGE + width :] = right[views * LEAD : views * LEAD + EDGE].astype(jnp.float32)
    main = MAX_SHIFT + 8
    tall = main + 8
    none = jnp.zeros((1, match.shape[1]), jnp.float32)

    def filled(v):
        at = v * tall
        pieces = [
            (at + r, LEAD - 2 + r, EDGE - 2 + r, min(48, main - r)) for r in range(0, main, 48)
        ]
        pieces += [(at + main, LEAD + width - 4, EDGE + width - 4, 8)]
        fill(pieces, near[v], src.at[v], wide, match, table_ref, block)

    def mend(row):
        for at, at_end in ((row, is_first_tile), (row + main + 3, is_last_tile)):
            first[at : at + 1] = jnp.where(at_end, none, first[at : at + 1])

    tables = table_ref, band_one, band_two, spread_ref
    part = blend(views, tall, BATCH, planes, block, filled, mend, match, first, tables)
    joined[0:MAX_SHIFT] = part[0:MAX_SHIFT]
    joined[MAX_SHIFT:] = late_ref[...].astype(jnp.float32)
    joined[MAX_SHIFT : MAX_SHIFT + 2] = part[MAX_SHIFT : MAX_SHIFT + 2]
    joined[width - 2 :] = part[main : main + 2]
    size = planes * block
    to = iota((size, size), 0)
    g, j, h = to // (planes * rows), (to // rows) % planes, to % rows
    perm = ((j * groups + g) * rows + h == iota((size, size), 1)).astype(jnp.bfloat16)
    turned = dot_nt(perm, joined[...].astype(jnp.bfloat16)).astype(jnp.bfloat16)
    out_ref[...] = turned.reshape(groups, planes, rows, width)


def whole(memory):
    return pl.BlockSpec(memory_space=memory)


def limit(mebibytes):
    return pltpu.CompilerParams(vmem_limit_bytes=mebibytes * 1024 * 1024)


def swap_planes(value):
    return lax.ppermute(value, "plane", [(0, 1), (1, 0)])


def per_device(ref_feat, src_feat, shifts, conv_one, bias_one, conv_two, bias_two, view_head):
    views, _, rows, width = src_feat.shape
    planes = shifts.shape[1]
    lanes = ref_feat.shape[0] * rows
    tiles, sides = lax.axis_size("tile"), lax.axis_size("plane")
    bf16, f32 = jnp.bfloat16, jnp.float32
    vmem = pltpu.VMEM
    shape = jax.ShapeDtypeStruct
    if sides == 2:
        own, other = src_feat, swap_planes(src_feat)
    else:
        full = lax.all_gather(src_feat, "plane", axis=1, tiled=True)
        half = full.shape[1] // 2
        own, other = full[:, :half], full[:, half:]

    packet_shape = shape((views * LEAD + EDGE, lanes), bf16)
    part = pl.pallas_call(
        pack_own_body,
        out_shape=packet_shape,
        in_specs=[whole(pltpu.HBM)] * 2,
        out_specs=whole(vmem),
        scratch_shapes=[
            pltpu.VMEM(own.shape, bf16),
            pltpu.VMEM(ref_feat.shape, bf16),
            pltpu.SemaphoreType.DMA((2,)),
        ],
        compiler_params=limit(8),
        name="pack_own",
    )(*(pltpu.with_memory_space_constraint(x, pltpu.HBM) for x in (own, ref_feat)))
    packet = pl.pallas_call(
        pack_other_body,
        out_shape=packet_shape,
        in_specs=[whole(vmem)] * 2,
        out_specs=whole(vmem),
        compiler_params=limit(8),
        name="pack_other",
    )(part, other)

    pairs = [(sides * i, sides * (i + 1)) for i in range(tiles - 1)]
    pairs += [(sides * (i + 1) + 1, sides * i + 1) for i in range(tiles - 1)]
    got = lax.ppermute(packet, ("tile", "plane"), pairs)

    own, other, shifts, conv_one, conv_two, packet = lax.optimization_barrier(
        (own, other, shifts, conv_one, conv_two, packet)
    )
    if sides == 2:
        before = after = swap_planes(shifts)
    else:
        before = lax.ppermute(shifts, "plane", [(i, i + 1) for i in range(sides - 1)])
        after = lax.ppermute(shifts, "plane", [(i + 1, i) for i in range(sides - 1)])

    def taps(kernel):
        flipped = jnp.flip(kernel, axis=2)
        return jnp.transpose(flipped, (3, 4, 1, 2, 0)).reshape(9 * GROUPS, 3 * GROUPS)

    both_taps = jnp.stack([taps(conv_one), taps(conv_two)])
    span = (planes + 4) * GROUPS * rows
    out_lanes = planes * GROUPS * rows
    late_rows = width - MAX_SHIFT
    high = views * (late_rows + 8) + 8
    inner = pl.pallas_call(
        inner_body,
        out_shape=[
            shape((views, width, lanes), bf16),
            shape((width, lanes), bf16),
            shape((late_rows, out_lanes), bf16),
            shape((8, 128), jnp.int32),
            shape((8, span), f32),
            shape((2 * out_lanes, out_lanes), bf16),
            shape((3 * span, out_lanes), bf16),
            shape((3 * span, out_lanes), bf16),
        ],
        in_specs=[whole(vmem)] * 10,
        out_specs=[whole(vmem)] * 8,
        scratch_shapes=[
            pltpu.VMEM((views, width + 16, lanes), f32),
            pltpu.VMEM((width + 8, lanes), f32),
            pltpu.VMEM((high, span), f32),
            pltpu.VMEM((high, span), f32),
        ],
        compiler_params=limit(24),
        cost_estimate=pl.CostEstimate(
            flops=5 * 10**9, bytes_accessed=10**6, transcendentals=10**5
        ),
        name="inner_columns",
    )(shifts, before, after, bias_one, bias_two, view_head, own, other, ref_feat, both_taps)
    got, *inner = lax.optimization_barrier((got, *inner))
    if sides == 2:
        swapped = swap_planes(got)
    else:
        both = lax.all_gather(got, "plane", axis=0)
        got, swapped = both[0], both[1]
    high = views * (MAX_SHIFT + 16) + 8
    return pl.pallas_call(
        outer_body,
        out_shape=shape((GROUPS, planes, rows, width), bf16),
        in_specs=[whole(vmem)] * 10,
        out_specs=whole(vmem),
        scratch_shapes=[
            pltpu.VMEM((views, LEAD + width + EDGE, lanes), f32),
            pltpu.VMEM((EDGE + width + EDGE, lanes), f32),
            pltpu.VMEM((high, span), f32),
            pltpu.VMEM((high, span), f32),
            pltpu.VMEM((width, out_lanes), f32),
        ],
        compiler_params=limit(24),
        name="outer_columns",
    )(*inner, got, swapped)


def solution(mesh):
    placed = (
        P(None, None, "tile"),
        P(None, "plane", None, "tile"),
        P(None, "plane"),
        P(),
        P(),
        P(),
        P(),
        P(),
    )
    return jax.shard_map(
        per_device,
        mesh=mesh,
        in_specs=placed,
        out_specs=P(None, "plane", None, "tile"),
        check_vma=False,
    )
```

```python
import jax
import jax.numpy as jnp
from jax import lax
from jax.experimental import pallas as pl
from jax.experimental.pallas import tpu as pltpu
from jax.sharding import PartitionSpec as P

GROUPS = 8
MAX_SHIFT = 128
LEAD = MAX_SHIFT + 16
EDGE = 16
BATCH = 2
FAR = -3.0e38


def iota(shape, dim):
    return lax.broadcasted_iota(jnp.int32, shape, dim)


def dot(left, right):
    return jnp.dot(left, right, preferred_element_type=jnp.float32)


def dot_nt(left, right):
    return lax.dot_general(
        left, right, (((1,), (1,)), ((), ())), preferred_element_type=jnp.float32
    )


def position():
    tile, plane = lax.axis_index("tile"), lax.axis_index("plane")
    tiles, sides = lax.axis_size("tile"), lax.axis_size("plane")
    order = plane if sides == 2 else 0 * plane
    role = jnp.minimum(plane, 1)
    return role, order, tile == 0, tile == tiles - 1, plane == 0, plane == sides - 1


def columns_of(count, width, start):
    picked = iota((count, width), 0) + start == iota((count, width), 1)
    return picked.astype(jnp.bfloat16)


def lane_order(half, rows, side):
    lanes = 2 * half * rows
    inner = 2 * half // GROUPS
    at, to = iota((lanes, 2 * lanes), 0), iota((lanes, 2 * lanes), 1)
    k, g = (to // (GROUPS * rows)) % inner, (to // rows) % GROUPS
    channel = g * inner + k - half * side
    row = (to // lanes) * (half * rows) + channel * rows + to % rows
    held = (channel >= 0) & (channel < half) & (row == at)
    return held.astype(jnp.bfloat16)


def ref_order(lanes, rows):
    at, to = iota((lanes, lanes), 0), iota((lanes, lanes), 1)
    k, g, h = to // (GROUPS * rows), (to // rows) % GROUPS, to % rows
    return ((g * (lanes // (GROUPS * rows)) + k) * rows + h == at).astype(jnp.bfloat16)


def turned_half(half_ref, pick, side):
    views, half, rows, width = half_ref.shape
    lanes = 2 * half * rows
    block = half_ref[...].reshape(views * half * rows, width)
    columns = dot_nt(pick, block).astype(jnp.bfloat16)
    order = lane_order(half, rows, side)
    return [dot(columns[:, i : i + lanes], order) for i in range(0, columns.shape[1], lanes)]


def turned_ref(ref_ref, pick):
    channels, rows, width = ref_ref.shape
    lanes = channels * rows
    columns = dot_nt(pick, ref_ref[...].reshape(lanes, width)).astype(jnp.bfloat16)
    return dot(columns, ref_order(lanes, rows))


def edge_start(role, width, count):
    return jnp.where(role == 0, width - count, 0)


def stage_body(own_hbm, ref_hbm, own_ref, ref_ref, sems):
    copies = [
        pltpu.make_async_copy(own_hbm, own_ref, sems.at[0]),
        pltpu.make_async_copy(ref_hbm, ref_ref, sems.at[1]),
    ]
    for copy in copies:
        copy.start()
    for copy in copies:
        copy.wait()


def pack_body(own_ref, other_ref, ref_ref, packet_ref):
    width = own_ref.shape[3]
    lanes = packet_ref.shape[1]
    role, order, *_ = position()
    pick = columns_of(LEAD, width, edge_start(role, width, LEAD))
    halves = zip(turned_half(own_ref, pick, order), turned_half(other_ref, pick, 1 - order))
    for i, (low, high) in enumerate(halves):
        pair = (low + high).astype(jnp.bfloat16)
        for k in range(2):
            at = (2 * i + k) * LEAD
            packet_ref[at : at + LEAD] = pair[:, k * lanes : (k + 1) * lanes]
    pick = columns_of(EDGE, width, edge_start(role, width, EDGE))
    packet_ref[own_ref.shape[0] * LEAD :] = turned_ref(ref_ref, pick).astype(jnp.bfloat16)


def lane_table(values_ref, rows, lane):
    which = (lane // rows) % GROUPS
    table = jnp.zeros(lane.shape, jnp.float32)
    for o in range(GROUPS):
        table = jnp.where(which == o, values_ref[o], table)
    return table


def build_band(taps_ref, which, band_ref, rows):
    block = GROUPS * rows
    spread = iota((3 * GROUPS, 128), 1) // rows == iota((3 * GROUPS, 128), 0)
    wide = dot(taps_ref[which], spread.astype(jnp.bfloat16)).astype(jnp.bfloat16)
    stretch = (iota((block, GROUPS), 0) // rows == iota((block, GROUPS), 1)).astype(jnp.bfloat16)
    lane = iota((block, 128), 1)
    gap = iota((block, 128), 0) % rows - lane % rows + 1
    depth, out_lanes = band_ref.shape[0] // 3, band_ref.shape[1]
    per_tile = 128 // block
    zero = jnp.zeros((block, 128), jnp.bfloat16)
    for e in range(3):
        base = jnp.zeros((block, 128), jnp.float32)
        for b in range(3):
            at = (b * 3 + e) * GROUPS
            base = jnp.where(gap == b, dot(stretch, wide[at : at + GROUPS]), base)
        for j in range(depth // block):
            offset = j - 2
            first, turn = offset // per_tile, offset % per_tile
            moved = pltpu.roll(base, turn * block, 1) if turn else base
            for t in range(out_lanes // 128):
                if t == first:
                    part = jnp.where(lane >= turn * block, moved, 0.0).astype(jnp.bfloat16)
                elif t == first + 1 and turn > per_tile - 3:
                    part = jnp.where(lane < turn * block, moved, 0.0).astype(jnp.bfloat16)
                else:
                    part = zero
                at = e * depth + j * block
                band_ref[at : at + block, t * 128 : (t + 1) * 128] = part


def build_tables(planes, rows, inner, bias_one, bias_two, view_head, ends, table_ref, spread_ref):
    block = GROUPS * rows
    out_lanes = planes * block
    span = table_ref.shape[1]
    is_first_plane, is_last_plane = ends
    at = iota((1, span), 1)
    plane = at // block
    outside = ((plane < 2) & is_first_plane) | ((plane >= planes + 2) & is_last_plane)
    table_ref[0:1] = jnp.where(outside, 0.0, 1.0 / inner)
    outside = ((plane == 0) & is_first_plane) | ((plane == planes + 1) & is_last_plane)
    table_ref[1:2] = jnp.where(outside, FAR, lane_table(bias_one, rows, at))
    table_ref[2:3] = lane_table(bias_two, rows, at)
    table_ref[3:4] = lane_table(view_head, rows, at)
    row, lane = iota((out_lanes, out_lanes), 0), iota((out_lanes, out_lanes), 1)
    same = ((row // block == lane // block) & (row % rows == lane % rows)).astype(jnp.bfloat16)
    spread_ref[0:out_lanes] = same
    spread_ref[out_lanes:] = same


def fill(pieces, near, src, wide, match, table_ref, block):
    for at, src_at, wide_at, count in pieces:
        quarter = iota((count, 128), 1) // block
        lower, middle, even = quarter < 2, (quarter == 1) | (quarter == 2), quarter % 2 == 0
        here = wide[wide_at : wide_at + count]
        for q in range(match.shape[1] // 128):

            def product(j):
                return src[pl.ds(src_at - near[q * 4 + j], count)] * here

            a, c, b, d = (product(j) for j in range(4))
            x = jnp.where(lower, a, b) + pltpu.roll(jnp.where(lower, b, a), 64, 1)
            z = jnp.where(middle, c, d) + pltpu.roll(jnp.where(middle, d, c), 64, 1)
            y = jnp.where(even, x, z) + pltpu.roll(jnp.where(even, z, x), 96, 1)
            y = y * table_ref[0:1, q * 128 : (q + 1) * 128]
            y = y.astype(jnp.bfloat16).astype(jnp.float32)
            match[at : at + count, q * 128 : (q + 1) * 128] = y


def convolve_first(low, high, planes, block, match, first, table_ref, band_one):
    out_lanes = planes * block
    span = match.shape[1]
    rest = span - out_lanes
    moved = [match[low + e : high + e].astype(jnp.bfloat16) for e in range(3)]
    raw = dot(jnp.concatenate(moved, axis=1), band_one[...])
    raw = jnp.maximum(raw + table_ref[1:2, 0:out_lanes], 0.0)
    first[low:high, 0:out_lanes] = raw
    raw = sum(
        dot(moved[e][:, out_lanes:], band_one[e * span : e * span + rest, 0:rest])
        for e in range(3)
    )
    raw = jnp.maximum(raw + table_ref[1:2, out_lanes:], 0.0)
    first[low:high, out_lanes:] = raw


def weights(low, high, planes, block, first, table_ref, band_two, spread_ref):
    out_lanes = planes * block
    moved = [first[low + e : high + e].astype(jnp.bfloat16) for e in range(3)]
    second = dot(jnp.concatenate(moved, axis=1), band_two[...])
    second = jnp.maximum(second + table_ref[2:3, 0:out_lanes], 0.0) * table_ref[3:4, 0:out_lanes]
    upper = second.astype(jnp.bfloat16)
    under = (second - upper.astype(jnp.float32)).astype(jnp.bfloat16)
    score = dot(jnp.concatenate([upper, under], axis=1), spread_ref[...])
    return 1.0 / (1.0 + jnp.exp(-score))


def first_stage(views, tall, planes, block, filled, mend, match, first, table_ref, band_one):
    for at in range(0, views, BATCH):
        for v in range(at, at + BATCH):
            filled(v)
        convolve_first(
            at * tall, (at + BATCH) * tall, planes, block, match, first, table_ref, band_one
        )
        for v in range(at, at + BATCH):
            mend(v * tall)


def second_stage(views, tall, planes, block, match, first, table_ref, band_two, spread_ref):
    out_lanes = planes * block
    total = weighted = 0.0
    for at in range(0, views, BATCH):
        weight = weights(
            at * tall, (at + BATCH) * tall, planes, block, first, table_ref, band_two, spread_ref
        )
        for v in range(BATCH):
            part = weight[v * tall : (v + 1) * tall]
            row = (at + v) * tall + 2
            total = total + part
            weighted = weighted + part * match[row : row + tall, 2 * block : 2 * block + out_lanes]
    return weighted / total


def pack_shifts(shifts, before, after, word_ref):
    for row, ref in enumerate((before, shifts, after)):
        word = ref[0:1]
        for v in range(1, ref.shape[0]):
            word = word | (ref[v : v + 1] << (8 * v))
        word_ref[row : row + 1, 0 : word.shape[1]] = word


def read_shifts(views, planes, word_ref):
    at = [(0, planes - 2), (0, planes - 1)] + [(1, d) for d in range(planes)] + [(2, 0), (2, 1)]
    words = [word_ref[row, d] for row, d in at]
    return [[(word >> (8 * v)) & 255 for word in words] for v in range(views)]


def inner_body(
    shifts,
    before,
    after,
    bias_one,
    bias_two,
    view_head,
    own_ref,
    other_ref,
    ref_ref,
    taps_ref,
    cols_ref,
    ref_cols_ref,
    word_ref,
    table_ref,
    spread_ref,
    band_one,
    band_two,
    match,
    first,
    src,
    wide,
):
    views, half, rows, width = own_ref.shape
    planes = shifts.shape[1]
    lanes = 2 * half * rows
    inner = 2 * half // GROUPS
    block = GROUPS * rows
    _, order, _, _, *ends = position()
    pick = columns_of(width, width, 0)
    none = jnp.zeros((8, lanes), jnp.float32)
    columns = turned_ref(ref_ref, pick)
    ref_cols_ref[...] = columns.astype(jnp.bfloat16)
    wide[0:width] = columns
    wide[width:] = none
    pairs = zip(turned_half(own_ref, pick, order), turned_half(other_ref, pick, 1 - order))
    for i, (low, high) in enumerate(pairs):
        columns = low + high
        for k in range(2):
            v = 2 * i + k
            part = columns[:, k * lanes : (k + 1) * lanes]
            cols_ref[v] = part.astype(jnp.bfloat16)
            src[v, 0:8] = none
            src[v, 8 : 8 + width] = part
            src[v, 8 + width :] = none
    build_tables(
        planes, rows, inner, bias_one, bias_two, view_head, ends, table_ref, spread_ref
    )
    build_band(taps_ref, 0, band_one, rows)
    build_band(taps_ref, 1, band_two, rows)
    pack_shifts(shifts, before, after, word_ref)
    near = read_shifts(views, planes, word_ref)
    out_rows = width - MAX_SHIFT
    tall = out_rows + 8
    base = MAX_SHIFT - 2

    def filled(v):
        pieces = [
            (v * tall + r, 8 + base + r, base + r, min(48, tall - r)) for r in range(0, tall, 48)
        ]
        fill(pieces, near[v], src.at[v], wide, match, table_ref, block)

    first_stage(
        views, tall, planes, block, filled, lambda row: None, match, first, table_ref, band_one
    )
    for ref in (match, first):
        ref[views * tall :] = jnp.zeros((8, match.shape[1]), jnp.float32)


def late_body(match, first, table_ref, spread_ref, band_two, late_ref):
    out_rows, out_lanes = late_ref.shape
    block = (match.shape[1] - out_lanes) // 4
    views = match.shape[0] // (out_rows + 8)
    joined = second_stage(
        views, out_rows + 8, out_lanes // block, block, match, first, table_ref, band_two, spread_ref
    )
    late_ref[...] = joined[0:out_rows].astype(jnp.bfloat16)


def outer_body(
    cols_ref,
    ref_cols_ref,
    word_ref,
    table_ref,
    spread_ref,
    band_one,
    band_two,
    late_ref,
    got_ref,
    swapped_ref,
    out_ref,
    src,
    wide,
    match,
    first,
    joined,
):
    views, width, lanes = cols_ref.shape
    groups, planes, rows, _ = out_ref.shape
    block = groups * rows
    _, order, is_first_tile, is_last_tile, *_ = position()

    near = read_shifts(views, planes, word_ref)
    left = jnp.where(order == 0, got_ref[...], swapped_ref[...])
    right = jnp.where(order == 0, swapped_ref[...], got_ref[...])
    for v in range(views):
        src[v, 0:LEAD] = left[v * LEAD : (v + 1) * LEAD].astype(jnp.float32)
        src[v, LEAD : LEAD + width] = cols_ref[v].astype(jnp.float32)
        src[v, LEAD + width :] = right[v * LEAD : v * LEAD + EDGE].astype(jnp.float32)
    wide[0:EDGE] = left[views * LEAD :].astype(jnp.float32)
    wide[EDGE : EDGE + width] = ref_cols_ref[...].astype(jnp.float32)
    wide[EDGE + width :] = right[views * LEAD : views * LEAD + EDGE].astype(jnp.float32)
    main = MAX_SHIFT + 8
    tall = main + 8
    none = jnp.zeros((1, match.shape[1]), jnp.float32)

    def filled(v):
        at = v * tall
        pieces = [
            (at + r, LEAD - 2 + r, EDGE - 2 + r, min(48, main - r)) for r in range(0, main, 48)
        ]
        pieces += [(at + main, LEAD + width - 4, EDGE + width - 4, 8)]
        fill(pieces, near[v], src.at[v], wide, match, table_ref, block)

    def mend(row):
        for at, at_end in ((row, is_first_tile), (row + main + 3, is_last_tile)):
            first[at : at + 1] = jnp.where(at_end, none, first[at : at + 1])

    first_stage(views, tall, planes, block, filled, mend, match, first, table_ref, band_one)
    part = second_stage(
        views, tall, planes, block, match, first, table_ref, band_two, spread_ref
    )
    joined[0:MAX_SHIFT] = part[0:MAX_SHIFT]
    joined[MAX_SHIFT:] = late_ref[...].astype(jnp.float32)
    joined[MAX_SHIFT : MAX_SHIFT + 2] = part[MAX_SHIFT : MAX_SHIFT + 2]
    joined[width - 2 :] = part[main : main + 2]
    size = planes * block
    to = iota((size, size), 0)
    g, j, h = to // (planes * rows), (to // rows) % planes, to % rows
    perm = ((j * groups + g) * rows + h == iota((size, size), 1)).astype(jnp.bfloat16)
    turned = dot_nt(perm, joined[...].astype(jnp.bfloat16)).astype(jnp.bfloat16)
    out_ref[...] = turned.reshape(groups, planes, rows, width)


def whole(memory):
    return pl.BlockSpec(memory_space=memory)


def limit(mebibytes):
    return pltpu.CompilerParams(vmem_limit_bytes=mebibytes * 1024 * 1024)


def swap_planes(value):
    return lax.ppermute(value, "plane", [(0, 1), (1, 0)])


def per_device(ref_feat, src_feat, shifts, conv_one, bias_one, conv_two, bias_two, view_head):
    views, _, rows, width = src_feat.shape
    planes = shifts.shape[1]
    lanes = ref_feat.shape[0] * rows
    tiles, sides = lax.axis_size("tile"), lax.axis_size("plane")
    bf16, f32 = jnp.bfloat16, jnp.float32
    vmem = pltpu.VMEM
    shape = jax.ShapeDtypeStruct
    if sides == 2:
        own, other = src_feat, swap_planes(src_feat)
    else:
        full = lax.all_gather(src_feat, "plane", axis=1, tiled=True)
        half = full.shape[1] // 2
        own, other = full[:, :half], full[:, half:]

    packet_shape = shape((views * LEAD + EDGE, lanes), bf16)
    own, ref_feat = pl.pallas_call(
        stage_body,
        out_shape=[shape(own.shape, bf16), shape(ref_feat.shape, bf16)],
        in_specs=[whole(pltpu.HBM)] * 2,
        out_specs=[whole(vmem)] * 2,
        scratch_shapes=[pltpu.SemaphoreType.DMA((2,))],
        compiler_params=limit(8),
        name="stage",
    )(*(pltpu.with_memory_space_constraint(x, pltpu.HBM) for x in (own, ref_feat)))
    packet = pl.pallas_call(
        pack_body,
        out_shape=packet_shape,
        in_specs=[whole(vmem)] * 3,
        out_specs=whole(vmem),
        compiler_params=limit(8),
        name="pack_edges",
    )(own, other, ref_feat)

    pairs = [(sides * i, sides * (i + 1)) for i in range(tiles - 1)]
    pairs += [(sides * (i + 1) + 1, sides * i + 1) for i in range(tiles - 1)]
    got = lax.ppermute(packet, ("tile", "plane"), pairs)

    own, other, shifts, conv_one, conv_two, packet = lax.optimization_barrier(
        (own, other, shifts, conv_one, conv_two, packet)
    )
    if sides == 2:
        before = after = swap_planes(shifts)
    else:
        before = lax.ppermute(shifts, "plane", [(i, i + 1) for i in range(sides - 1)])
        after = lax.ppermute(shifts, "plane", [(i + 1, i) for i in range(sides - 1)])

    def taps(kernel):
        flipped = jnp.flip(kernel, axis=2)
        return jnp.transpose(flipped, (3, 4, 1, 2, 0)).reshape(9 * GROUPS, 3 * GROUPS)

    both_taps = jnp.stack([taps(conv_one), taps(conv_two)])
    span = (planes + 4) * GROUPS * rows
    out_lanes = planes * GROUPS * rows
    late_rows = width - MAX_SHIFT
    high = views * (late_rows + 8) + 8
    *inner, match, first = pl.pallas_call(
        inner_body,
        out_shape=[
            shape((views, width, lanes), bf16),
            shape((width, lanes), bf16),
            shape((8, 128), jnp.int32),
            shape((8, span), f32),
            shape((2 * out_lanes, out_lanes), bf16),
            shape((3 * span, out_lanes), bf16),
            shape((3 * span, out_lanes), bf16),
            shape((high, span), f32),
            shape((high, span), f32),
        ],
        in_specs=[whole(vmem)] * 10,
        out_specs=[whole(vmem)] * 9,
        scratch_shapes=[
            pltpu.VMEM((views, width + 16, lanes), f32),
            pltpu.VMEM((width + 8, lanes), f32),
        ],
        compiler_params=limit(24),
        cost_estimate=pl.CostEstimate(
            flops=3 * 10**9, bytes_accessed=10**6, transcendentals=10**5
        ),
        name="inner_columns",
    )(shifts, before, after, bias_one, bias_two, view_head, own, other, ref_feat, both_taps)
    got, match, first, *inner = lax.optimization_barrier((got, match, first, *inner))
    if sides == 2:
        swapped = swap_planes(got)
    else:
        both = lax.all_gather(got, "plane", axis=0)
        got, swapped = both[0], both[1]
    late = pl.pallas_call(
        late_body,
        out_shape=shape((late_rows, out_lanes), bf16),
        in_specs=[whole(vmem)] * 5,
        out_specs=whole(vmem),
        compiler_params=limit(24),
        cost_estimate=pl.CostEstimate(
            flops=2 * 10**9, bytes_accessed=10**6, transcendentals=10**5
        ),
        name="late_columns",
    )(match, first, inner[3], inner[4], inner[6])
    high = views * (MAX_SHIFT + 16) + 8
    return pl.pallas_call(
        outer_body,
        out_shape=shape((GROUPS, planes, rows, width), bf16),
        in_specs=[whole(vmem)] * 10,
        out_specs=whole(vmem),
        scratch_shapes=[
            pltpu.VMEM((views, LEAD + width + EDGE, lanes), f32),
            pltpu.VMEM((EDGE + width + EDGE, lanes), f32),
            pltpu.VMEM((high, span), f32),
            pltpu.VMEM((high, span), f32),
            pltpu.VMEM((width, out_lanes), f32),
        ],
        compiler_params=limit(24),
        name="outer_columns",
    )(*inner, late, got, swapped)


def solution(mesh):
    placed = (
        P(None, None, "tile"),
        P(None, "plane", None, "tile"),
        P(None, "plane"),
        P(),
        P(),
        P(),
        P(),
        P(),
    )
    return jax.shard_map(
        per_device,
        mesh=mesh,
        in_specs=placed,
        out_specs=P(None, "plane", None, "tile"),
        check_vma=False,
    )
```

```python
import jax
import jax.numpy as jnp
from jax import lax
from jax.experimental import pallas as pl
from jax.experimental.pallas import tpu as pltpu
from jax.sharding import PartitionSpec as P

GROUPS = 8
MAX_SHIFT = 128
LEAD = MAX_SHIFT + 8
EDGE = 16
BATCH = 2
FAR = -3.0e38


def iota(shape, dim):
    return lax.broadcasted_iota(jnp.int32, shape, dim)


def dot(left, right):
    return jnp.dot(left, right, preferred_element_type=jnp.float32)


def dot_nt(left, right):
    return lax.dot_general(
        left, right, (((1,), (1,)), ((), ())), preferred_element_type=jnp.float32
    )


def position():
    tile, plane = lax.axis_index("tile"), lax.axis_index("plane")
    tiles, sides = lax.axis_size("tile"), lax.axis_size("plane")
    order = plane if sides == 2 else 0 * plane
    role = jnp.minimum(plane, 1)
    return role, order, tile == 0, tile == tiles - 1, plane == 0, plane == sides - 1


def columns_of(count, width, start):
    picked = iota((count, width), 0) + start == iota((count, width), 1)
    return picked.astype(jnp.bfloat16)


def lane_order(half, rows, side):
    lanes = 2 * half * rows
    inner = 2 * half // GROUPS
    at, to = iota((lanes, 2 * lanes), 0), iota((lanes, 2 * lanes), 1)
    k, g = (to // (GROUPS * rows)) % inner, (to // rows) % GROUPS
    channel = g * inner + k - half * side
    row = (to // lanes) * (half * rows) + channel * rows + to % rows
    held = (channel >= 0) & (channel < half) & (row == at)
    return held.astype(jnp.bfloat16)


def ref_order(lanes, rows):
    at, to = iota((lanes, lanes), 0), iota((lanes, lanes), 1)
    k, g, h = to // (GROUPS * rows), (to // rows) % GROUPS, to % rows
    return ((g * (lanes // (GROUPS * rows)) + k) * rows + h == at).astype(jnp.bfloat16)


def turned_half(half_ref, pick, side):
    views, half, rows, width = half_ref.shape
    lanes = 2 * half * rows
    block = half_ref[...].reshape(views * half * rows, width)
    columns = dot_nt(pick, block).astype(jnp.bfloat16)
    order = lane_order(half, rows, side)
    return [dot(columns[:, i : i + lanes], order) for i in range(0, columns.shape[1], lanes)]


def turned_ref(ref_ref, pick):
    channels, rows, width = ref_ref.shape
    lanes = channels * rows
    columns = dot_nt(pick, ref_ref[...].reshape(lanes, width)).astype(jnp.bfloat16)
    return dot(columns, ref_order(lanes, rows))


def edge_start(role, width, count):
    return jnp.where(role == 0, width - count, 0)


def stacked(pair, lanes):
    return jnp.concatenate([pair[:, 0:lanes], pair[:, lanes:]], axis=0)


def pack_own_body(own_hbm, ref_hbm, own_ref, ref_ref, part_ref, sems):
    copies = [
        pltpu.make_async_copy(own_hbm, own_ref, sems.at[0]),
        pltpu.make_async_copy(ref_hbm, ref_ref, sems.at[1]),
    ]
    for copy in copies:
        copy.start()
    views, _, _, width = own_ref.shape
    lanes = part_ref.shape[1]
    role, order, *_ = position()
    pick = columns_of(LEAD, width, edge_start(role, width, LEAD))
    pick_ref = columns_of(EDGE, width, edge_start(role, width, EDGE))
    copies[0].wait()
    for i, pair in enumerate(turned_half(own_ref, pick, order)):
        at = 2 * i * LEAD
        part_ref[at : at + 2 * LEAD] = stacked(pair, lanes).astype(jnp.bfloat16)
    copies[1].wait()
    part_ref[views * LEAD :] = turned_ref(ref_ref, pick_ref).astype(jnp.bfloat16)


def pack_other_body(part_ref, other_ref, packet_ref):
    views, _, _, width = other_ref.shape
    lanes = packet_ref.shape[1]
    role, order, *_ = position()
    pick = columns_of(LEAD, width, edge_start(role, width, LEAD))
    for i, pair in enumerate(turned_half(other_ref, pick, 1 - order)):
        at = 2 * i * LEAD
        both = part_ref[at : at + 2 * LEAD].astype(jnp.float32) + stacked(pair, lanes)
        packet_ref[at : at + 2 * LEAD] = both.astype(jnp.bfloat16)
    packet_ref[views * LEAD :] = part_ref[views * LEAD :]


def lane_table(values_ref, rows, lane):
    which = lane // rows % GROUPS
    table = jnp.zeros(lane.shape, jnp.float32)
    for o in range(GROUPS):
        table = jnp.where(which == o, values_ref[o], table)
    return table


def base_blocks(taps_ref, which, rows, apart):
    block = GROUPS * rows
    slots = 128 // (4 * rows)
    at, lane = iota((3 * GROUPS, 128), 0), iota((3 * GROUPS, 128), 1)
    if apart:
        spreads = [
            (lane // (slots * rows) + t * 4 == at % GROUPS)
            & ((lane // rows) % slots == at // GROUPS)
            for t in range(2)
        ]
    else:
        spreads = [lane // rows == at]
    stretch = (iota((block, GROUPS), 0) // rows == iota((block, GROUPS), 1)).astype(jnp.bfloat16)
    gap = iota((block, 128), 0) % rows - iota((block, 128), 1) % rows + 1
    found = []
    for spread in spreads:
        wide = dot(taps_ref[which], spread.astype(jnp.bfloat16)).astype(jnp.bfloat16)
        for e in range(3):
            base = jnp.zeros((block, 128), jnp.float32)
            for b in range(3):
                at = (b * 3 + e) * GROUPS
                base = jnp.where(gap == b, dot(stretch, wide[at : at + GROUPS]), base)
            found.append(base)
    return [found[i : i + 3] for i in range(0, len(found), 3)]


def band_rows(e, j, block):
    per_tile = 128 // block
    whole = 2 * per_tile
    if j < whole:
        return (e * whole + j) * block
    return (3 * whole + 2 * e + j - whole) * block


def build_band_one(taps_ref, band_ref, rest_ref, rows):
    block = GROUPS * rows
    lane = iota((block, 128), 1)
    per_tile = 128 // block
    zero = jnp.zeros((block, 128), jnp.bfloat16)
    (bases,) = base_blocks(taps_ref, 0, rows, False)
    for e, base in enumerate(bases):
        low_parts, high_parts = [], []
        for turn in range(per_tile):
            moved = pltpu.roll(base, turn * block, 1) if turn else base
            high_parts.append(jnp.where(lane >= turn * block, moved, 0.0).astype(jnp.bfloat16))
            low_parts.append(jnp.where(lane < turn * block, moved, 0.0).astype(jnp.bfloat16))
        for j in range(2 * per_tile + 2):
            first, turn = (j - 2) // per_tile, (j - 2) % per_tile
            at = band_rows(e, j, block)
            for t in range(2):
                part = zero
                if t == first:
                    part = high_parts[turn]
                elif t == first + 1 and turn > per_tile - 3:
                    part = low_parts[turn]
                band_ref[at : at + block, t * 128 : (t + 1) * 128] = part
                if t == 0 and j < per_tile:
                    rest_ref[(e * per_tile + j) * block : (e * per_tile + j + 1) * block] = part
    for j in range(2):
        at = (3 * (2 * per_tile + 2) + j) * block
        band_ref[at : at + block] = jnp.zeros((block, 256), jnp.bfloat16)


def build_band_two(taps_ref, band_ref, rows):
    block = GROUPS * rows
    per_tile = 128 // block
    slots = 2 * per_tile
    plane = (iota((block, 128), 1) // rows) % slots
    for t, bases in enumerate(base_blocks(taps_ref, 1, rows, True)):
        for e, base in enumerate(bases):
            for j in range(slots + 2):
                turn = (j - 2) * rows % 128
                moved = pltpu.roll(base, turn, 1) if turn else base
                held = (plane >= j - 2) & (plane <= j)
                at = band_rows(e, j, block)
                band_ref[at : at + block, t * 128 : (t + 1) * 128] = jnp.where(
                    held, moved, 0.0
                ).astype(jnp.bfloat16)
    for j in range(2):
        at = (3 * (slots + 2) + j) * block
        band_ref[at : at + block] = jnp.zeros((block, 256), jnp.bfloat16)


def build_tables(planes, rows, inner, bias_one, bias_two, view_head, ends, table_ref, spread_ref, perm_ref):
    block = GROUPS * rows
    out_lanes = planes * block
    span = table_ref.shape[1]
    is_first_plane, is_last_plane = ends
    at = iota((1, span), 1)
    plane = at // block
    outside = ((plane < 2) & is_first_plane) | ((plane >= planes + 2) & is_last_plane)
    table_ref[0:1] = jnp.where(outside, 0.0, 1.0 / inner)
    outside = ((plane == 0) & is_first_plane) | ((plane == planes + 1) & is_last_plane)
    table_ref[1:2] = jnp.where(outside, FAR, lane_table(bias_one, rows, at))
    table_ref[2:3] = lane_table(bias_two, planes * rows, at)
    table_ref[3:4] = lane_table(view_head, planes * rows, at)
    row, lane = iota(spread_ref.shape, 0), iota(spread_ref.shape, 1)
    same = (row // rows % planes == lane // block) & (row % rows == lane % rows)
    spread_ref[...] = same.astype(jnp.bfloat16)
    to = iota(perm_ref.shape, 0)
    g, j, h = to // (planes * rows), (to // rows) % planes, to % rows
    perm = (j * GROUPS + g) * rows + h == iota(perm_ref.shape, 1)
    perm_ref[...] = perm.astype(jnp.bfloat16)


def fill(pieces, near, src, wide, match, table_ref, block):
    for at, src_at, wide_at, count in pieces:
        quarter = iota((count, 128), 1) // block
        lower, middle, even = quarter < 2, (quarter == 1) | (quarter == 2), quarter % 2 == 0
        here = wide[wide_at : wide_at + count]
        for q in range(match.shape[1] // 128):

            def product(j):
                return src[pl.ds(src_at - near[q * 4 + j], count)] * here

            a, c, b, d = (product(j) for j in range(4))
            x = jnp.where(lower, a, b) + pltpu.roll(jnp.where(lower, b, a), 64, 1)
            z = jnp.where(middle, c, d) + pltpu.roll(jnp.where(middle, d, c), 64, 1)
            y = jnp.where(even, x, z) + pltpu.roll(jnp.where(even, z, x), 96, 1)
            y = y * table_ref[0:1, q * 128 : (q + 1) * 128]
            y = y.astype(jnp.bfloat16).astype(jnp.float32)
            match[at : at + count, q * 128 : (q + 1) * 128] = y


def three_taps(volume, low, high, out_lanes):
    tile = volume.shape[1] - out_lanes
    parts = [volume[low + e : high + e] for e in range(3)]
    tails = [part[:, out_lanes:] for part in parts]
    near = iota((high - low, tile), 1) < tile // 2
    paired = jnp.where(near, tails[0], pltpu.roll(tails[1], tile // 2, 1))
    sides = [part[:, 0:out_lanes] for part in parts] + [paired, tails[2]]
    wide = jnp.concatenate([side.astype(jnp.bfloat16) for side in sides], axis=1)
    return wide, jnp.concatenate([tail.astype(jnp.bfloat16) for tail in tails], axis=1)


def convolve_first(low, high, planes, block, match, first, table_ref, band_one, rest_ref):
    out_lanes = planes * block
    wide, tails = three_taps(match, low, high, out_lanes)
    raw = dot(wide, band_one[...])
    first[low:high, 0:out_lanes] = jnp.maximum(raw + table_ref[1:2, 0:out_lanes], 0.0)
    raw = dot(tails, rest_ref[...])
    first[low:high, out_lanes:] = jnp.maximum(raw + table_ref[1:2, out_lanes:], 0.0)


def weights(low, high, planes, block, first, table_ref, band_two, spread_ref):
    out_lanes = planes * block
    wide, _ = three_taps(first, low, high, out_lanes)
    second = dot(wide, band_two[...])
    second = jnp.maximum(second + table_ref[2:3, 0:out_lanes], 0.0) * table_ref[3:4, 0:out_lanes]
    half = out_lanes // 2
    second = second[:, 0:half] + second[:, half:]
    upper = second.astype(jnp.bfloat16)
    under = (second - upper.astype(jnp.float32)).astype(jnp.bfloat16)
    score = dot(jnp.concatenate([upper, under], axis=1), spread_ref[...])
    return 1.0 / (1.0 + jnp.exp(-score))


def first_stage(
    views, tall, planes, block, filled, mend, match, first, table_ref, band_one, rest_ref
):
    for at in range(0, views, BATCH):
        for v in range(at, at + BATCH):
            filled(v)
        low, high = at * tall, (at + BATCH) * tall
        convolve_first(low, high, planes, block, match, first, table_ref, band_one, rest_ref)
        for v in range(at, at + BATCH):
            mend(v * tall)


def second_stage(views, tall, planes, block, match, first, table_ref, band_two, spread_ref):
    out_lanes = planes * block
    total = weighted = 0.0
    for at in range(0, views, BATCH):
        weight = weights(
            at * tall, (at + BATCH) * tall, planes, block, first, table_ref, band_two, spread_ref
        )
        for v in range(BATCH):
            part = weight[v * tall : (v + 1) * tall]
            row = (at + v) * tall + 2
            total = total + part
            weighted = weighted + part * match[row : row + tall, 2 * block : 2 * block + out_lanes]
    return weighted / total


def pack_shifts(shifts, before, after, word_ref):
    for row, ref in enumerate((before, shifts, after)):
        word = ref[0:1]
        for v in range(1, ref.shape[0]):
            word = word | (ref[v : v + 1] << (8 * v))
        word_ref[row : row + 1, 0 : word.shape[1]] = word


def read_shifts(views, planes, word_ref):
    at = [(0, planes - 2), (0, planes - 1)] + [(1, d) for d in range(planes)] + [(2, 0), (2, 1)]
    words = [word_ref[row, d] for row, d in at]
    return [[(word >> (8 * v)) & 255 for word in words] for v in range(views)]


def inner_body(
    shifts,
    before,
    after,
    bias_one,
    bias_two,
    view_head,
    own_ref,
    other_ref,
    ref_ref,
    taps_ref,
    cols_ref,
    ref_cols_ref,
    word_ref,
    table_ref,
    spread_ref,
    perm_ref,
    band_one,
    rest_ref,
    band_two,
    match,
    first,
    src,
    wide,
):
    views, half, rows, width = own_ref.shape
    planes = shifts.shape[1]
    lanes = 2 * half * rows
    inner = 2 * half // GROUPS
    block = GROUPS * rows
    _, order, _, _, *ends = position()
    pick = columns_of(width, width, 0)
    none = jnp.zeros((8, lanes), jnp.float32)
    columns = turned_ref(ref_ref, pick)
    ref_cols_ref[...] = columns.astype(jnp.bfloat16)
    wide[0:width] = columns
    wide[width:] = none
    pairs = zip(turned_half(own_ref, pick, order), turned_half(other_ref, pick, 1 - order))
    for i, (low, high) in enumerate(pairs):
        columns = low + high
        for k in range(2):
            v = 2 * i + k
            part = columns[:, k * lanes : (k + 1) * lanes]
            cols_ref[v] = part.astype(jnp.bfloat16)
            src[v, 0:8] = none
            src[v, 8 : 8 + width] = part
            src[v, 8 + width :] = none
    build_tables(
        planes, rows, inner, bias_one, bias_two, view_head, ends, table_ref, spread_ref, perm_ref
    )
    build_band_one(taps_ref, band_one, rest_ref, rows)
    build_band_two(taps_ref, band_two, rows)
    pack_shifts(shifts, before, after, word_ref)
    near = read_shifts(views, planes, word_ref)
    out_rows = width - MAX_SHIFT
    tall = out_rows + 8
    base = MAX_SHIFT - 2

    def filled(v):
        pieces = [
            (v * tall + r, 8 + base + r, base + r, min(48, tall - r)) for r in range(0, tall, 48)
        ]
        fill(pieces, near[v], src.at[v], wide, match, table_ref, block)

    first_stage(
        views,
        tall,
        planes,
        block,
        filled,
        lambda row: None,
        match,
        first,
        table_ref,
        band_one,
        rest_ref,
    )
    for ref in (match, first):
        ref[views * tall :] = jnp.zeros((8, match.shape[1]), jnp.float32)


def late_body(match, first, table_ref, spread_ref, band_two, late_ref):
    out_rows, out_lanes = late_ref.shape
    block = (match.shape[1] - out_lanes) // 4
    views = match.shape[0] // (out_rows + 8)
    joined = second_stage(
        views, out_rows + 8, out_lanes // block, block, match, first, table_ref, band_two, spread_ref
    )
    late_ref[...] = joined[0:out_rows].astype(jnp.bfloat16)


def outer_body(
    cols_ref,
    ref_cols_ref,
    word_ref,
    table_ref,
    spread_ref,
    perm_ref,
    band_one,
    rest_ref,
    band_two,
    late_ref,
    got_ref,
    swapped_ref,
    out_ref,
    src,
    wide,
    match,
    first,
    joined,
):
    views, width, lanes = cols_ref.shape
    groups, planes, rows, _ = out_ref.shape
    block = groups * rows
    _, order, is_first_tile, is_last_tile, *_ = position()

    near = read_shifts(views, planes, word_ref)
    left = jnp.where(order == 0, got_ref[...], swapped_ref[...])
    right = jnp.where(order == 0, swapped_ref[...], got_ref[...])
    for v in range(0, views, 2):
        at = v * LEAD
        pair = left[at : at + 2 * LEAD].astype(jnp.float32)
        ends = right[at : at + LEAD + 24].astype(jnp.float32)
        for k in range(2):
            src[v + k, 0:LEAD] = pair[k * LEAD : (k + 1) * LEAD]
            src[v + k, LEAD : LEAD + width] = cols_ref[v + k].astype(jnp.float32)
            src[v + k, LEAD + width :] = ends[k * LEAD : k * LEAD + EDGE]
    wide[0:EDGE] = left[views * LEAD :].astype(jnp.float32)
    wide[EDGE : EDGE + width] = ref_cols_ref[...].astype(jnp.float32)
    wide[EDGE + width :] = right[views * LEAD : views * LEAD + EDGE].astype(jnp.float32)
    main = MAX_SHIFT + 8
    tall = main + 8
    none = jnp.zeros((1, match.shape[1]), jnp.float32)

    def filled(v):
        at = v * tall
        pieces = [
            (at + r, LEAD - 2 + r, EDGE - 2 + r, min(48, main - r)) for r in range(0, main, 48)
        ]
        pieces += [(at + main, LEAD + width - 4, EDGE + width - 4, 8)]
        fill(pieces, near[v], src.at[v], wide, match, table_ref, block)

    def mend(row):
        for at, at_end in ((row, is_first_tile), (row + main + 3, is_last_tile)):
            first[at : at + 1] = jnp.where(at_end, none, first[at : at + 1])

    first_stage(
        views, tall, planes, block, filled, mend, match, first, table_ref, band_one, rest_ref
    )
    part = second_stage(
        views, tall, planes, block, match, first, table_ref, band_two, spread_ref
    )
    joined[0:MAX_SHIFT] = part[0:MAX_SHIFT]
    joined[MAX_SHIFT:] = late_ref[...].astype(jnp.float32)
    joined[MAX_SHIFT : MAX_SHIFT + 2] = part[MAX_SHIFT : MAX_SHIFT + 2]
    joined[width - 2 :] = part[main : main + 2]
    turned = dot_nt(perm_ref[...], joined[...].astype(jnp.bfloat16)).astype(jnp.bfloat16)
    out_ref[...] = turned.reshape(groups, planes, rows, width)


def whole(memory):
    return pl.BlockSpec(memory_space=memory)


def limit(mebibytes):
    return pltpu.CompilerParams(vmem_limit_bytes=mebibytes * 1024 * 1024)


def swap_planes(value):
    return lax.ppermute(value, "plane", [(0, 1), (1, 0)])


def per_device(ref_feat, src_feat, shifts, conv_one, bias_one, conv_two, bias_two, view_head):
    views, _, rows, width = src_feat.shape
    planes = shifts.shape[1]
    lanes = ref_feat.shape[0] * rows
    tiles, sides = lax.axis_size("tile"), lax.axis_size("plane")
    bf16, f32 = jnp.bfloat16, jnp.float32
    vmem = pltpu.VMEM
    shape = jax.ShapeDtypeStruct
    if sides == 2:
        own, other = src_feat, swap_planes(src_feat)
    else:
        full = lax.all_gather(src_feat, "plane", axis=1, tiled=True)
        half = full.shape[1] // 2
        own, other = full[:, :half], full[:, half:]

    packet_shape = shape((views * LEAD + EDGE, lanes), bf16)
    own, ref_feat, part = pl.pallas_call(
        pack_own_body,
        out_shape=[shape(own.shape, bf16), shape(ref_feat.shape, bf16), packet_shape],
        in_specs=[whole(pltpu.HBM)] * 2,
        out_specs=[whole(vmem)] * 3,
        scratch_shapes=[pltpu.SemaphoreType.DMA((2,))],
        compiler_params=limit(8),
        name="pack_own",
    )(*(pltpu.with_memory_space_constraint(x, pltpu.HBM) for x in (own, ref_feat)))
    packet = pl.pallas_call(
        pack_other_body,
        out_shape=packet_shape,
        in_specs=[whole(vmem)] * 2,
        out_specs=whole(vmem),
        compiler_params=limit(8),
        name="pack_other",
    )(part, other)

    pairs = [(sides * i, sides * (i + 1)) for i in range(tiles - 1)]
    pairs += [(sides * (i + 1) + 1, sides * i + 1) for i in range(tiles - 1)]
    got = lax.ppermute(packet, ("tile", "plane"), pairs)

    own, other, shifts, conv_one, conv_two, packet = lax.optimization_barrier(
        (own, other, shifts, conv_one, conv_two, packet)
    )
    if sides == 2:
        before = after = swap_planes(shifts)
    else:
        before = lax.ppermute(shifts, "plane", [(i, i + 1) for i in range(sides - 1)])
        after = lax.ppermute(shifts, "plane", [(i + 1, i) for i in range(sides - 1)])

    def taps(kernel):
        flipped = jnp.flip(kernel, axis=2)
        return jnp.transpose(flipped, (3, 4, 1, 2, 0)).reshape(9 * GROUPS, 3 * GROUPS)

    both_taps = jnp.stack([taps(conv_one), taps(conv_two)])
    span = (planes + 4) * GROUPS * rows
    out_lanes = planes * GROUPS * rows
    late_rows = width - MAX_SHIFT
    high = views * (late_rows + 8) + 8
    *inner, match, first = pl.pallas_call(
        inner_body,
        out_shape=[
            shape((views, width, lanes), bf16),
            shape((width, lanes), bf16),
            shape((8, 128), jnp.int32),
            shape((8, span), f32),
            shape((256, out_lanes), bf16),
            shape((out_lanes, out_lanes), bf16),
            shape((4 * out_lanes, out_lanes), bf16),
            shape((3 * (span - out_lanes), span - out_lanes), bf16),
            shape((4 * out_lanes, out_lanes), bf16),
            shape((high, span), f32),
            shape((high, span), f32),
        ],
        in_specs=[whole(vmem)] * 10,
        out_specs=[whole(vmem)] * 11,
        scratch_shapes=[
            pltpu.VMEM((views, width + 16, lanes), f32),
            pltpu.VMEM((width + 8, lanes), f32),
        ],
        compiler_params=limit(24),
        cost_estimate=pl.CostEstimate(
            flops=3 * 10**9, bytes_accessed=10**6, transcendentals=10**5
        ),
        name="inner_columns",
    )(shifts, before, after, bias_one, bias_two, view_head, own, other, ref_feat, both_taps)
    got, match, first, *inner = lax.optimization_barrier((got, match, first, *inner))
    if sides == 2:
        swapped = swap_planes(got)
    else:
        both = lax.all_gather(got, "plane", axis=0)
        got, swapped = both[0], both[1]
    late = pl.pallas_call(
        late_body,
        out_shape=shape((late_rows, out_lanes), bf16),
        in_specs=[whole(vmem)] * 5,
        out_specs=whole(vmem),
        compiler_params=limit(24),
        cost_estimate=pl.CostEstimate(
            flops=2 * 10**9, bytes_accessed=10**6, transcendentals=10**5
        ),
        name="late_columns",
    )(match, first, inner[3], inner[4], inner[8])
    high = views * (MAX_SHIFT + 16) + 8
    return pl.pallas_call(
        outer_body,
        out_shape=shape((GROUPS, planes, rows, width), bf16),
        in_specs=[whole(vmem)] * 12,
        out_specs=whole(vmem),
        scratch_shapes=[
            pltpu.VMEM((views, LEAD + width + EDGE, lanes), f32),
            pltpu.VMEM((EDGE + width + EDGE, lanes), f32),
            pltpu.VMEM((high, span), f32),
            pltpu.VMEM((high, span), f32),
            pltpu.VMEM((width, out_lanes), f32),
        ],
        compiler_params=limit(24),
        name="outer_columns",
    )(*inner, late, got, swapped)


def solution(mesh):
    placed = (
        P(None, None, "tile"),
        P(None, "plane", None, "tile"),
        P(None, "plane"),
        P(),
        P(),
        P(),
        P(),
        P(),
    )
    return jax.shard_map(
        per_device,
        mesh=mesh,
        in_specs=placed,
        out_specs=P(None, "plane", None, "tile"),
        check_vma=False,
    )
```

```python
import jax
import jax.numpy as jnp
from jax import lax
from jax.experimental import pallas as pl
from jax.experimental.pallas import tpu as pltpu
from jax.sharding import PartitionSpec as P

GROUPS = 8
MAX_SHIFT = 128
LEAD = MAX_SHIFT + 8
EDGE = 16
BATCH = 2
FAR = -3.0e38


def iota(shape, dim):
    return lax.broadcasted_iota(jnp.int32, shape, dim)


def dot(left, right):
    return jnp.dot(left, right, preferred_element_type=jnp.float32)


def dot_nt(left, right):
    return lax.dot_general(
        left, right, (((1,), (1,)), ((), ())), preferred_element_type=jnp.float32
    )


def position():
    tile, plane = lax.axis_index("tile"), lax.axis_index("plane")
    tiles, sides = lax.axis_size("tile"), lax.axis_size("plane")
    order = plane if sides == 2 else 0 * plane
    role = jnp.minimum(plane, 1)
    return role, order, tile == 0, tile == tiles - 1, plane == 0, plane == sides - 1


def columns_of(count, width, start):
    picked = iota((count, width), 0) + start == iota((count, width), 1)
    return picked.astype(jnp.bfloat16)


def lane_order(half, rows, side):
    lanes = 2 * half * rows
    inner = 2 * half // GROUPS
    at, to = iota((lanes, 2 * lanes), 0), iota((lanes, 2 * lanes), 1)
    k, g = (to // (GROUPS * rows)) % inner, (to // rows) % GROUPS
    channel = g * inner + k - half * side
    row = (to // lanes) * (half * rows) + channel * rows + to % rows
    held = (channel >= 0) & (channel < half) & (row == at)
    return held.astype(jnp.bfloat16)


def ref_order(lanes, rows):
    at, to = iota((lanes, lanes), 0), iota((lanes, lanes), 1)
    k, g, h = to // (GROUPS * rows), (to // rows) % GROUPS, to % rows
    return ((g * (lanes // (GROUPS * rows)) + k) * rows + h == at).astype(jnp.bfloat16)


def turned_half(half_ref, pick, side):
    views, half, rows, width = half_ref.shape
    lanes = 2 * half * rows
    block = half_ref[...].reshape(views * half * rows, width)
    columns = dot_nt(pick, block).astype(jnp.bfloat16)
    order = lane_order(half, rows, side)
    return [dot(columns[:, i : i + lanes], order) for i in range(0, columns.shape[1], lanes)]


def turned_ref(ref_ref, pick):
    channels, rows, width = ref_ref.shape
    lanes = channels * rows
    columns = dot_nt(pick, ref_ref[...].reshape(lanes, width)).astype(jnp.bfloat16)
    return dot(columns, ref_order(lanes, rows))


def edge_start(role, width, count):
    return jnp.where(role == 0, width - count, 0)


def stacked(pair, lanes):
    return jnp.concatenate([pair[:, 0:lanes], pair[:, lanes:]], axis=0)


def pack_own_body(own_hbm, ref_hbm, own_ref, ref_ref, part_ref, sems):
    copies = [
        pltpu.make_async_copy(own_hbm, own_ref, sems.at[0]),
        pltpu.make_async_copy(ref_hbm, ref_ref, sems.at[1]),
    ]
    for copy in copies:
        copy.start()
    views, _, _, width = own_ref.shape
    lanes = part_ref.shape[1]
    role, order, *_ = position()
    pick = columns_of(LEAD, width, edge_start(role, width, LEAD))
    pick_ref = columns_of(EDGE, width, edge_start(role, width, EDGE))
    copies[0].wait()
    for i, pair in enumerate(turned_half(own_ref, pick, order)):
        at = 2 * i * LEAD
        part_ref[at : at + 2 * LEAD] = stacked(pair, lanes).astype(jnp.bfloat16)
    copies[1].wait()
    part_ref[views * LEAD :] = turned_ref(ref_ref, pick_ref).astype(jnp.bfloat16)


def pack_other_body(part_ref, other_ref, packet_ref):
    views, _, _, width = other_ref.shape
    lanes = packet_ref.shape[1]
    role, order, *_ = position()
    pick = columns_of(LEAD, width, edge_start(role, width, LEAD))
    for i, pair in enumerate(turned_half(other_ref, pick, 1 - order)):
        at = 2 * i * LEAD
        both = part_ref[at : at + 2 * LEAD].astype(jnp.float32) + stacked(pair, lanes)
        packet_ref[at : at + 2 * LEAD] = both.astype(jnp.bfloat16)
    packet_ref[views * LEAD :] = part_ref[views * LEAD :]


def lane_table(values_ref, rows, lane):
    which = lane // rows % GROUPS
    table = jnp.zeros(lane.shape, jnp.float32)
    for o in range(GROUPS):
        table = jnp.where(which == o, values_ref[o], table)
    return table


def base_blocks(taps_ref, which, rows, apart):
    block = GROUPS * rows
    slots = 128 // (4 * rows)
    at, lane = iota((3 * GROUPS, 128), 0), iota((3 * GROUPS, 128), 1)
    if apart:
        spreads = [
            (lane // (slots * rows) + t * 4 == at % GROUPS)
            & ((lane // rows) % slots == at // GROUPS)
            for t in range(2)
        ]
    else:
        spreads = [lane // rows == at]
    stretch = (iota((block, GROUPS), 0) // rows == iota((block, GROUPS), 1)).astype(jnp.bfloat16)
    gap = iota((block, 128), 0) % rows - iota((block, 128), 1) % rows + 1
    found = []
    for spread in spreads:
        wide = dot(taps_ref[which], spread.astype(jnp.bfloat16)).astype(jnp.bfloat16)
        for e in range(3):
            base = jnp.zeros((block, 128), jnp.float32)
            for b in range(3):
                at = (b * 3 + e) * GROUPS
                base = jnp.where(gap == b, dot(stretch, wide[at : at + GROUPS]), base)
            found.append(base)
    return [found[i : i + 3] for i in range(0, len(found), 3)]


def band_rows(e, j, block):
    per_tile = 128 // block
    whole = 2 * per_tile
    if j < whole:
        return (e * whole + j) * block
    return (3 * whole + 2 * e + j - whole) * block


def build_band_one(taps_ref, band_ref, rest_ref, rows):
    block = GROUPS * rows
    lane = iota((block, 128), 1)
    per_tile = 128 // block
    zero = jnp.zeros((block, 128), jnp.bfloat16)
    (bases,) = base_blocks(taps_ref, 0, rows, False)
    for e, base in enumerate(bases):
        low_parts, high_parts = [], []
        for turn in range(per_tile):
            moved = pltpu.roll(base, turn * block, 1) if turn else base
            high_parts.append(jnp.where(lane >= turn * block, moved, 0.0).astype(jnp.bfloat16))
            low_parts.append(jnp.where(lane < turn * block, moved, 0.0).astype(jnp.bfloat16))
        for j in range(2 * per_tile + 2):
            first, turn = (j - 2) // per_tile, (j - 2) % per_tile
            at = band_rows(e, j, block)
            for t in range(2):
                part = zero
                if t == first:
                    part = high_parts[turn]
                elif t == first + 1 and turn > per_tile - 3:
                    part = low_parts[turn]
                band_ref[at : at + block, t * 128 : (t + 1) * 128] = part
                if t == 0 and j < per_tile:
                    rest_ref[(e * per_tile + j) * block : (e * per_tile + j + 1) * block] = part
    for j in range(2):
        at = (3 * (2 * per_tile + 2) + j) * block
        band_ref[at : at + block] = jnp.zeros((block, 256), jnp.bfloat16)


def build_band_two(taps_ref, band_ref, rows):
    block = GROUPS * rows
    per_tile = 128 // block
    slots = 2 * per_tile
    plane = (iota((block, 128), 1) // rows) % slots
    for t, bases in enumerate(base_blocks(taps_ref, 1, rows, True)):
        for e, base in enumerate(bases):
            for j in range(slots + 2):
                turn = (j - 2) * rows % 128
                moved = pltpu.roll(base, turn, 1) if turn else base
                held = (plane >= j - 2) & (plane <= j)
                at = band_rows(e, j, block)
                band_ref[at : at + block, t * 128 : (t + 1) * 128] = jnp.where(
                    held, moved, 0.0
                ).astype(jnp.bfloat16)
    for j in range(2):
        at = (3 * (slots + 2) + j) * block
        band_ref[at : at + block] = jnp.zeros((block, 256), jnp.bfloat16)


def build_tables(planes, rows, inner, bias_one, bias_two, view_head, ends, table_ref, spread_ref, perm_ref):
    block = GROUPS * rows
    out_lanes = planes * block
    span = table_ref.shape[1]
    is_first_plane, is_last_plane = ends
    at = iota((1, span), 1)
    plane = at // block
    outside = ((plane < 2) & is_first_plane) | ((plane >= planes + 2) & is_last_plane)
    table_ref[0:1] = jnp.where(outside, 0.0, 1.0 / inner)
    outside = ((plane == 0) & is_first_plane) | ((plane == planes + 1) & is_last_plane)
    table_ref[1:2] = jnp.where(outside, FAR, lane_table(bias_one, rows, at))
    table_ref[2:3] = lane_table(bias_two, planes * rows, at)
    table_ref[3:4] = lane_table(view_head, planes * rows, at)
    row, lane = iota(spread_ref.shape, 0), iota(spread_ref.shape, 1)
    same = (row // rows % planes == lane // block) & (row % rows == lane % rows)
    spread_ref[...] = same.astype(jnp.bfloat16)
    to = iota(perm_ref.shape, 0)
    g, j, h = to // (planes * rows), (to // rows) % planes, to % rows
    perm = (j * GROUPS + g) * rows + h == iota(perm_ref.shape, 1)
    perm_ref[...] = perm.astype(jnp.bfloat16)


def fill(pieces, near, src, wide, match, table_ref, block):
    for at, src_at, wide_at, count in pieces:
        quarter = iota((count, 128), 1) // block
        lower, middle, even = quarter < 2, (quarter == 1) | (quarter == 2), quarter % 2 == 0
        here = wide[wide_at : wide_at + count]
        for q in range(match.shape[1] // 128):

            def product(j):
                return src[pl.ds(src_at - near[q * 4 + j], count)] * here

            a, c, b, d = (product(j) for j in range(4))
            x = jnp.where(lower, a, b) + pltpu.roll(jnp.where(lower, b, a), 64, 1)
            z = jnp.where(middle, c, d) + pltpu.roll(jnp.where(middle, d, c), 64, 1)
            y = jnp.where(even, x, z) + pltpu.roll(jnp.where(even, z, x), 96, 1)
            y = y * table_ref[0:1, q * 128 : (q + 1) * 128]
            y = y.astype(jnp.bfloat16).astype(jnp.float32)
            match[at : at + count, q * 128 : (q + 1) * 128] = y


def three_taps(volume, low, high, out_lanes):
    tile = volume.shape[1] - out_lanes
    parts = [volume[low + e : high + e] for e in range(3)]
    tails = [part[:, out_lanes:] for part in parts]
    near = iota((high - low, tile), 1) < tile // 2
    paired = jnp.where(near, tails[0], pltpu.roll(tails[1], tile // 2, 1))
    sides = [part[:, 0:out_lanes] for part in parts] + [paired, tails[2]]
    wide = jnp.concatenate([side.astype(jnp.bfloat16) for side in sides], axis=1)
    return wide, jnp.concatenate([tail.astype(jnp.bfloat16) for tail in tails], axis=1)


def convolve_first(low, high, planes, block, match, first, table_ref, band_one, rest_ref):
    out_lanes = planes * block
    wide, tails = three_taps(match, low, high, out_lanes)
    raw = dot(wide, band_one[...])
    first[low:high, 0:out_lanes] = jnp.maximum(raw + table_ref[1:2, 0:out_lanes], 0.0)
    raw = dot(tails, rest_ref[...])
    first[low:high, out_lanes:] = jnp.maximum(raw + table_ref[1:2, out_lanes:], 0.0)


def weights(low, high, planes, block, first, table_ref, band_two, spread_ref):
    out_lanes = planes * block
    wide, _ = three_taps(first, low, high, out_lanes)
    second = dot(wide, band_two[...])
    second = jnp.maximum(second + table_ref[2:3, 0:out_lanes], 0.0) * table_ref[3:4, 0:out_lanes]
    half = out_lanes // 2
    second = second[:, 0:half] + second[:, half:]
    upper = second.astype(jnp.bfloat16)
    under = (second - upper.astype(jnp.float32)).astype(jnp.bfloat16)
    score = dot(jnp.concatenate([upper, under], axis=1), spread_ref[...])
    return 1.0 / (1.0 + jnp.exp(-score))


def first_stage(
    views, tall, planes, block, filled, mend, match, first, table_ref, band_one, rest_ref
):
    for at in range(0, views, BATCH):
        for v in range(at, at + BATCH):
            filled(v)
        low, high = at * tall, (at + BATCH) * tall
        convolve_first(low, high, planes, block, match, first, table_ref, band_one, rest_ref)
        for v in range(at, at + BATCH):
            mend(v * tall)


def second_stage(views, tall, planes, block, match, first, table_ref, band_two, spread_ref):
    out_lanes = planes * block
    total = weighted = 0.0
    for at in range(0, views, BATCH):
        weight = weights(
            at * tall, (at + BATCH) * tall, planes, block, first, table_ref, band_two, spread_ref
        )
        for v in range(BATCH):
            part = weight[v * tall : (v + 1) * tall]
            row = (at + v) * tall + 2
            total = total + part
            weighted = weighted + part * match[row : row + tall, 2 * block : 2 * block + out_lanes]
    return weighted / total


def pack_shifts(shifts, before, after, word_ref):
    for row, ref in enumerate((before, shifts, after)):
        word = ref[0:1]
        for v in range(1, ref.shape[0]):
            word = word | (ref[v : v + 1] << (8 * v))
        word_ref[row : row + 1, 0 : word.shape[1]] = word


def read_shifts(views, planes, word_ref):
    at = [(0, planes - 2), (0, planes - 1)] + [(1, d) for d in range(planes)] + [(2, 0), (2, 1)]
    words = [word_ref[row, d] for row, d in at]
    return [[(word >> (8 * v)) & 255 for word in words] for v in range(views)]


def inner_body(
    shifts,
    before,
    after,
    bias_one,
    bias_two,
    view_head,
    own_ref,
    other_ref,
    ref_ref,
    taps_ref,
    cols_ref,
    ref_cols_ref,
    word_ref,
    table_ref,
    spread_ref,
    perm_ref,
    band_one,
    rest_ref,
    band_two,
    match,
    first,
    src,
    wide,
):
    views, half, rows, width = own_ref.shape
    planes = shifts.shape[1]
    lanes = 2 * half * rows
    inner = 2 * half // GROUPS
    block = GROUPS * rows
    _, order, _, _, *ends = position()
    pick = columns_of(width, width, 0)
    none = jnp.zeros((8, lanes), jnp.float32)
    columns = turned_ref(ref_ref, pick)
    ref_cols_ref[...] = columns.astype(jnp.bfloat16)
    wide[0:width] = columns
    wide[width:] = none
    pairs = zip(turned_half(own_ref, pick, order), turned_half(other_ref, pick, 1 - order))
    for i, (low, high) in enumerate(pairs):
        columns = low + high
        for k in range(2):
            v = 2 * i + k
            part = columns[:, k * lanes : (k + 1) * lanes]
            cols_ref[v] = part.astype(jnp.bfloat16)
            src[v, 0:8] = none
            src[v, 8 : 8 + width] = part
            src[v, 8 + width :] = none
    build_tables(
        planes, rows, inner, bias_one, bias_two, view_head, ends, table_ref, spread_ref, perm_ref
    )
    build_band_one(taps_ref, band_one, rest_ref, rows)
    build_band_two(taps_ref, band_two, rows)
    pack_shifts(shifts, before, after, word_ref)
    near = read_shifts(views, planes, word_ref)
    out_rows = width - MAX_SHIFT
    tall = out_rows + 8
    base = MAX_SHIFT - 2

    def filled(v):
        pieces = [
            (v * tall + r, 8 + base + r, base + r, min(48, tall - r)) for r in range(0, tall, 48)
        ]
        fill(pieces, near[v], src.at[v], wide, match, table_ref, block)

    first_stage(
        views,
        tall,
        planes,
        block,
        filled,
        lambda row: None,
        match,
        first,
        table_ref,
        band_one,
        rest_ref,
    )
    for ref in (match, first):
        ref[views * tall :] = jnp.zeros((8, match.shape[1]), jnp.float32)


def late_body(match, first, table_ref, spread_ref, band_two, late_ref):
    out_rows, out_lanes = late_ref.shape
    block = (match.shape[1] - out_lanes) // 4
    views = match.shape[0] // (out_rows + 8)
    joined = second_stage(
        views, out_rows + 8, out_lanes // block, block, match, first, table_ref, band_two, spread_ref
    )
    late_ref[...] = joined[0:out_rows].astype(jnp.bfloat16)


def outer_body(
    cols_ref,
    ref_cols_ref,
    word_ref,
    table_ref,
    spread_ref,
    perm_ref,
    band_one,
    rest_ref,
    band_two,
    late_ref,
    got_ref,
    swapped_ref,
    out_ref,
    src,
    wide,
    match,
    first,
    joined,
):
    views, width, lanes = cols_ref.shape
    groups, planes, rows, _ = out_ref.shape
    block = groups * rows
    _, order, is_first_tile, is_last_tile, *_ = position()

    near = read_shifts(views, planes, word_ref)
    left = jnp.where(order == 0, got_ref[...], swapped_ref[...])
    right = jnp.where(order == 0, swapped_ref[...], got_ref[...])
    left = jnp.where(is_first_tile, jnp.zeros_like(left), left)
    right = jnp.where(is_last_tile, jnp.zeros_like(right), right)
    for v in range(0, views, 2):
        at = v * LEAD
        pair = left[at : at + 2 * LEAD].astype(jnp.float32)
        ends = right[at : at + LEAD + 24].astype(jnp.float32)
        for k in range(2):
            src[v + k, 0:LEAD] = pair[k * LEAD : (k + 1) * LEAD]
            src[v + k, LEAD : LEAD + width] = cols_ref[v + k].astype(jnp.float32)
            src[v + k, LEAD + width :] = ends[k * LEAD : k * LEAD + EDGE]
    wide[0:EDGE] = left[views * LEAD :].astype(jnp.float32)
    wide[EDGE : EDGE + width] = ref_cols_ref[...].astype(jnp.float32)
    wide[EDGE + width :] = right[views * LEAD : views * LEAD + EDGE].astype(jnp.float32)
    main = MAX_SHIFT + 8
    tall = main + 8
    none = jnp.zeros((1, match.shape[1]), jnp.float32)

    def filled(v):
        at = v * tall
        pieces = [
            (at + r, LEAD - 2 + r, EDGE - 2 + r, min(48, main - r)) for r in range(0, main, 48)
        ]
        pieces += [(at + main, LEAD + width - 4, EDGE + width - 4, 8)]
        fill(pieces, near[v], src.at[v], wide, match, table_ref, block)

    def mend(row):
        for at, at_end in ((row, is_first_tile), (row + main + 3, is_last_tile)):
            first[at : at + 1] = jnp.where(at_end, none, first[at : at + 1])

    first_stage(
        views, tall, planes, block, filled, mend, match, first, table_ref, band_one, rest_ref
    )
    part = second_stage(
        views, tall, planes, block, match, first, table_ref, band_two, spread_ref
    )
    joined[0:MAX_SHIFT] = part[0:MAX_SHIFT]
    joined[MAX_SHIFT:] = late_ref[...].astype(jnp.float32)
    joined[MAX_SHIFT : MAX_SHIFT + 2] = part[MAX_SHIFT : MAX_SHIFT + 2]
    joined[width - 2 :] = part[main : main + 2]
    turned = dot_nt(perm_ref[...], joined[...].astype(jnp.bfloat16)).astype(jnp.bfloat16)
    out_ref[...] = turned.reshape(groups, planes, rows, width)


def whole(memory):
    return pl.BlockSpec(memory_space=memory)


def limit(mebibytes):
    return pltpu.CompilerParams(vmem_limit_bytes=mebibytes * 1024 * 1024)


def swap_planes(value):
    return lax.ppermute(value, "plane", [(0, 1), (1, 0)])


def per_device(ref_feat, src_feat, shifts, conv_one, bias_one, conv_two, bias_two, view_head):
    views, _, rows, width = src_feat.shape
    planes = shifts.shape[1]
    lanes = ref_feat.shape[0] * rows
    tiles, sides = lax.axis_size("tile"), lax.axis_size("plane")
    bf16, f32 = jnp.bfloat16, jnp.float32
    vmem = pltpu.VMEM
    shape = jax.ShapeDtypeStruct
    if sides == 2:
        own, other = src_feat, swap_planes(src_feat)
    else:
        full = lax.all_gather(src_feat, "plane", axis=1, tiled=True)
        half = full.shape[1] // 2
        own, other = full[:, :half], full[:, half:]

    packet_shape = shape((views * LEAD + EDGE, lanes), bf16)
    own, ref_feat, part = pl.pallas_call(
        pack_own_body,
        out_shape=[shape(own.shape, bf16), shape(ref_feat.shape, bf16), packet_shape],
        in_specs=[whole(pltpu.HBM)] * 2,
        out_specs=[whole(vmem)] * 3,
        scratch_shapes=[pltpu.SemaphoreType.DMA((2,))],
        compiler_params=limit(8),
        name="pack_own",
    )(*(pltpu.with_memory_space_constraint(x, pltpu.HBM) for x in (own, ref_feat)))
    packet = pl.pallas_call(
        pack_other_body,
        out_shape=packet_shape,
        in_specs=[whole(vmem)] * 2,
        out_specs=whole(vmem),
        compiler_params=limit(8),
        name="pack_other",
    )(part, other)

    pairs = [(sides * i, sides * (i + 1)) for i in range(tiles - 1)]
    pairs += [(sides * (i + 1) + 1, sides * i + 1) for i in range(tiles - 1)]
    pairs += [(sides * (tiles - 1), sides * (tiles - 1) + 1), (1, 0)]
    got = lax.ppermute(packet, ("tile", "plane"), pairs)

    own, other, shifts, conv_one, conv_two, packet = lax.optimization_barrier(
        (own, other, shifts, conv_one, conv_two, packet)
    )
    if sides == 2:
        before = after = swap_planes(shifts)
    else:
        before = lax.ppermute(shifts, "plane", [(i, i + 1) for i in range(sides - 1)])
        after = lax.ppermute(shifts, "plane", [(i + 1, i) for i in range(sides - 1)])

    def taps(kernel):
        flipped = jnp.flip(kernel, axis=2)
        return jnp.transpose(flipped, (3, 4, 1, 2, 0)).reshape(9 * GROUPS, 3 * GROUPS)

    both_taps = jnp.stack([taps(conv_one), taps(conv_two)])
    span = (planes + 4) * GROUPS * rows
    out_lanes = planes * GROUPS * rows
    late_rows = width - MAX_SHIFT
    high = views * (late_rows + 8) + 8
    *inner, match, first = pl.pallas_call(
        inner_body,
        out_shape=[
            shape((views, width, lanes), bf16),
            shape((width, lanes), bf16),
            shape((8, 128), jnp.int32),
            shape((8, span), f32),
            shape((256, out_lanes), bf16),
            shape((out_lanes, out_lanes), bf16),
            shape((4 * out_lanes, out_lanes), bf16),
            shape((3 * (span - out_lanes), span - out_lanes), bf16),
            shape((4 * out_lanes, out_lanes), bf16),
            shape((high, span), f32),
            shape((high, span), f32),
        ],
        in_specs=[whole(vmem)] * 10,
        out_specs=[whole(vmem)] * 11,
        scratch_shapes=[
            pltpu.VMEM((views, width + 16, lanes), f32),
            pltpu.VMEM((width + 8, lanes), f32),
        ],
        compiler_params=limit(24),
        cost_estimate=pl.CostEstimate(
            flops=3 * 10**9, bytes_accessed=10**6, transcendentals=10**5
        ),
        name="inner_columns",
    )(shifts, before, after, bias_one, bias_two, view_head, own, other, ref_feat, both_taps)
    got, match, first, *inner = lax.optimization_barrier((got, match, first, *inner))
    if sides == 2:
        swapped = swap_planes(got)
    else:
        both = lax.all_gather(got, "plane", axis=0)
        got, swapped = both[0], both[1]
    late = pl.pallas_call(
        late_body,
        out_shape=shape((late_rows, out_lanes), bf16),
        in_specs=[whole(vmem)] * 5,
        out_specs=whole(vmem),
        compiler_params=limit(24),
        cost_estimate=pl.CostEstimate(
            flops=2 * 10**9, bytes_accessed=10**6, transcendentals=10**5
        ),
        name="late_columns",
    )(match, first, inner[3], inner[4], inner[8])
    high = views * (MAX_SHIFT + 16) + 8
    return pl.pallas_call(
        outer_body,
        out_shape=shape((GROUPS, planes, rows, width), bf16),
        in_specs=[whole(vmem)] * 12,
        out_specs=whole(vmem),
        scratch_shapes=[
            pltpu.VMEM((views, LEAD + width + EDGE, lanes), f32),
            pltpu.VMEM((EDGE + width + EDGE, lanes), f32),
            pltpu.VMEM((high, span), f32),
            pltpu.VMEM((high, span), f32),
            pltpu.VMEM((width, out_lanes), f32),
        ],
        compiler_params=limit(24),
        name="outer_columns",
    )(*inner, late, got, swapped)


def solution(mesh):
    placed = (
        P(None, None, "tile"),
        P(None, "plane", None, "tile"),
        P(None, "plane"),
        P(),
        P(),
        P(),
        P(),
        P(),
    )
    return jax.shard_map(
        per_device,
        mesh=mesh,
        in_specs=placed,
        out_specs=P(None, "plane", None, "tile"),
        check_vma=False,
    )
```

```python
import jax
import jax.numpy as jnp
from jax import lax
from jax.experimental import pallas as pl
from jax.experimental.pallas import tpu as pltpu
from jax.sharding import PartitionSpec as P

GROUPS = 8
MAX_SHIFT = 128
LEAD = MAX_SHIFT + 8
EDGE = 16
BATCH = 2
FAR = -3.0e38


def iota(shape, dim):
    return lax.broadcasted_iota(jnp.int32, shape, dim)


def dot(left, right):
    return jnp.dot(left, right, preferred_element_type=jnp.float32)


def dot_nt(left, right):
    return lax.dot_general(
        left, right, (((1,), (1,)), ((), ())), preferred_element_type=jnp.float32
    )


def position():
    tile, plane = lax.axis_index("tile"), lax.axis_index("plane")
    tiles, sides = lax.axis_size("tile"), lax.axis_size("plane")
    order = plane if sides == 2 else 0 * plane
    role = jnp.minimum(plane, 1)
    return role, order, tile == 0, tile == tiles - 1, plane == 0, plane == sides - 1


def columns_of(count, width, start):
    picked = iota((count, width), 0) + start == iota((count, width), 1)
    return picked.astype(jnp.bfloat16)


def lane_order(half, rows, side):
    lanes = 2 * half * rows
    inner = 2 * half // GROUPS
    at, to = iota((lanes, 2 * lanes), 0), iota((lanes, 2 * lanes), 1)
    k, g = (to // (GROUPS * rows)) % inner, (to // rows) % GROUPS
    channel = g * inner + k - half * side
    row = (to // lanes) * (half * rows) + channel * rows + to % rows
    held = (channel >= 0) & (channel < half) & (row == at)
    return held.astype(jnp.bfloat16)


def ref_order(lanes, rows):
    at, to = iota((lanes, lanes), 0), iota((lanes, lanes), 1)
    k, g, h = to // (GROUPS * rows), (to // rows) % GROUPS, to % rows
    return ((g * (lanes // (GROUPS * rows)) + k) * rows + h == at).astype(jnp.bfloat16)


def turned_half(half_ref, pick, order):
    views, half, rows, width = half_ref.shape
    lanes = 2 * half * rows
    block = half_ref[...].reshape(views * half * rows, width)
    columns = dot_nt(pick, block).astype(jnp.bfloat16)
    return [dot(columns[:, i : i + lanes], order) for i in range(0, columns.shape[1], lanes)]


def turned_ref(ref_ref, pick):
    channels, rows, width = ref_ref.shape
    lanes = channels * rows
    columns = dot_nt(pick, ref_ref[...].reshape(lanes, width)).astype(jnp.bfloat16)
    return dot(columns, ref_order(lanes, rows))


def edge_start(role, width, count):
    return jnp.where(role == 0, width - count, 0)


def stacked(pair, lanes):
    return jnp.concatenate([pair[:, 0:lanes], pair[:, lanes:]], axis=0)


def pack_own_body(
    own_hbm, ref_hbm, own_ref, ref_ref, part_ref, pick_ref, own_order_ref, other_order_ref, sems
):
    copies = [
        pltpu.make_async_copy(own_hbm, own_ref, sems.at[0]),
        pltpu.make_async_copy(ref_hbm, ref_ref, sems.at[1]),
    ]
    for copy in copies:
        copy.start()
    views, half, rows, width = own_ref.shape
    lanes = part_ref.shape[1]
    role, order, *_ = position()
    pick_ref[...] = columns_of(LEAD, width, edge_start(role, width, LEAD))
    own_order_ref[...] = lane_order(half, rows, order)
    other_order_ref[...] = lane_order(half, rows, 1 - order)
    few = columns_of(EDGE, width, edge_start(role, width, EDGE))
    copies[0].wait()
    for i, pair in enumerate(turned_half(own_ref, pick_ref[...], own_order_ref[...])):
        at = 2 * i * LEAD
        part_ref[at : at + 2 * LEAD] = stacked(pair, lanes).astype(jnp.bfloat16)
    copies[1].wait()
    part_ref[views * LEAD :] = turned_ref(ref_ref, few).astype(jnp.bfloat16)


def pack_other_body(part_ref, pick_ref, other_order_ref, other_ref, packet_ref):
    views = other_ref.shape[0]
    lanes = packet_ref.shape[1]
    for i, pair in enumerate(turned_half(other_ref, pick_ref[...], other_order_ref[...])):
        at = 2 * i * LEAD
        both = part_ref[at : at + 2 * LEAD].astype(jnp.float32) + stacked(pair, lanes)
        packet_ref[at : at + 2 * LEAD] = both.astype(jnp.bfloat16)
    packet_ref[views * LEAD :] = part_ref[views * LEAD :]


def lane_table(values_ref, rows, lane):
    which = lane // rows % GROUPS
    table = jnp.zeros(lane.shape, jnp.float32)
    for o in range(GROUPS):
        table = jnp.where(which == o, values_ref[o], table)
    return table


def base_blocks(taps_ref, which, rows, apart):
    block = GROUPS * rows
    slots = 128 // (4 * rows)
    at, lane = iota((3 * GROUPS, 128), 0), iota((3 * GROUPS, 128), 1)
    if apart:
        spreads = [
            (lane // (slots * rows) + t * 4 == at % GROUPS)
            & ((lane // rows) % slots == at // GROUPS)
            for t in range(2)
        ]
    else:
        spreads = [lane // rows == at]
    stretch = (iota((block, GROUPS), 0) // rows == iota((block, GROUPS), 1)).astype(jnp.bfloat16)
    gap = iota((block, 128), 0) % rows - iota((block, 128), 1) % rows + 1
    found = []
    for spread in spreads:
        wide = dot(taps_ref[which], spread.astype(jnp.bfloat16)).astype(jnp.bfloat16)
        for e in range(3):
            base = jnp.zeros((block, 128), jnp.float32)
            for b in range(3):
                at = (b * 3 + e) * GROUPS
                base = jnp.where(gap == b, dot(stretch, wide[at : at + GROUPS]), base)
            found.append(base)
    return [found[i : i + 3] for i in range(0, len(found), 3)]


def band_rows(e, j, block):
    per_tile = 128 // block
    whole = 2 * per_tile
    if j < whole:
        return (e * whole + j) * block
    return (3 * whole + 2 * e + j - whole) * block


def build_band_one(taps_ref, band_ref, rest_ref, rows):
    block = GROUPS * rows
    lane = iota((block, 128), 1)
    per_tile = 128 // block
    zero = jnp.zeros((block, 128), jnp.bfloat16)
    (bases,) = base_blocks(taps_ref, 0, rows, False)
    for e, base in enumerate(bases):
        low_parts, high_parts = [], []
        for turn in range(per_tile):
            moved = pltpu.roll(base, turn * block, 1) if turn else base
            high_parts.append(jnp.where(lane >= turn * block, moved, 0.0).astype(jnp.bfloat16))
            low_parts.append(jnp.where(lane < turn * block, moved, 0.0).astype(jnp.bfloat16))
        for j in range(2 * per_tile + 2):
            first, turn = (j - 2) // per_tile, (j - 2) % per_tile
            at = band_rows(e, j, block)
            for t in range(2):
                part = zero
                if t == first:
                    part = high_parts[turn]
                elif t == first + 1 and turn > per_tile - 3:
                    part = low_parts[turn]
                band_ref[at : at + block, t * 128 : (t + 1) * 128] = part
                if t == 0 and j < per_tile:
                    rest_ref[(e * per_tile + j) * block : (e * per_tile + j + 1) * block] = part
    for j in range(2):
        at = (3 * (2 * per_tile + 2) + j) * block
        band_ref[at : at + block] = jnp.zeros((block, 256), jnp.bfloat16)


def build_band_two(taps_ref, band_ref, rows):
    block = GROUPS * rows
    per_tile = 128 // block
    slots = 2 * per_tile
    plane = (iota((block, 128), 1) // rows) % slots
    for t, bases in enumerate(base_blocks(taps_ref, 1, rows, True)):
        for e, base in enumerate(bases):
            for j in range(slots + 2):
                turn = (j - 2) * rows % 128
                moved = pltpu.roll(base, turn, 1) if turn else base
                held = (plane >= j - 2) & (plane <= j)
                at = band_rows(e, j, block)
                band_ref[at : at + block, t * 128 : (t + 1) * 128] = jnp.where(
                    held, moved, 0.0
                ).astype(jnp.bfloat16)
    for j in range(2):
        at = (3 * (slots + 2) + j) * block
        band_ref[at : at + block] = jnp.zeros((block, 256), jnp.bfloat16)


def build_tables(planes, rows, inner, bias_one, bias_two, view_head, ends, table_ref, spread_ref, perm_ref):
    block = GROUPS * rows
    out_lanes = planes * block
    span = table_ref.shape[1]
    is_first_plane, is_last_plane = ends
    at = iota((1, span), 1)
    plane = at // block
    outside = ((plane < 2) & is_first_plane) | ((plane >= planes + 2) & is_last_plane)
    table_ref[0:1] = jnp.where(outside, 0.0, 1.0 / inner)
    outside = ((plane == 0) & is_first_plane) | ((plane == planes + 1) & is_last_plane)
    table_ref[1:2] = jnp.where(outside, FAR, lane_table(bias_one, rows, at))
    table_ref[2:3] = lane_table(bias_two, planes * rows, at)
    table_ref[3:4] = lane_table(view_head, planes * rows, at)
    row, lane = iota(spread_ref.shape, 0), iota(spread_ref.shape, 1)
    same = (row // rows % planes == lane // block) & (row % rows == lane % rows)
    spread_ref[...] = same.astype(jnp.bfloat16)
    to = iota(perm_ref.shape, 0)
    g, j, h = to // (planes * rows), (to // rows) % planes, to % rows
    perm = (j * GROUPS + g) * rows + h == iota(perm_ref.shape, 1)
    perm_ref[...] = perm.astype(jnp.bfloat16)


def fill(pieces, near, src, wide, match, table_ref, block):
    for at, src_at, wide_at, count in pieces:
        quarter = iota((count, 128), 1) // block
        lower, middle, even = quarter < 2, (quarter == 1) | (quarter == 2), quarter % 2 == 0
        here = wide[wide_at : wide_at + count]
        for q in range(match.shape[1] // 128):

            def product(j):
                return src[pl.ds(src_at - near[q * 4 + j], count)] * here

            a, c, b, d = (product(j) for j in range(4))
            x = jnp.where(lower, a, b) + pltpu.roll(jnp.where(lower, b, a), 64, 1)
            z = jnp.where(middle, c, d) + pltpu.roll(jnp.where(middle, d, c), 64, 1)
            y = jnp.where(even, x, z) + pltpu.roll(jnp.where(even, z, x), 96, 1)
            y = y * table_ref[0:1, q * 128 : (q + 1) * 128]
            y = y.astype(jnp.bfloat16).astype(jnp.float32)
            match[at : at + count, q * 128 : (q + 1) * 128] = y


def three_taps(volume, low, high, out_lanes):
    tile = volume.shape[1] - out_lanes
    parts = [volume[low + e : high + e] for e in range(3)]
    tails = [part[:, out_lanes:] for part in parts]
    near = iota((high - low, tile), 1) < tile // 2
    paired = jnp.where(near, tails[0], pltpu.roll(tails[1], tile // 2, 1))
    sides = [part[:, 0:out_lanes] for part in parts] + [paired, tails[2]]
    wide = jnp.concatenate([side.astype(jnp.bfloat16) for side in sides], axis=1)
    return wide, jnp.concatenate([tail.astype(jnp.bfloat16) for tail in tails], axis=1)


def convolve_first(low, high, planes, block, match, first, table_ref, band_one, rest_ref):
    out_lanes = planes * block
    wide, tails = three_taps(match, low, high, out_lanes)
    raw = dot(wide, band_one[...])
    first[low:high, 0:out_lanes] = jnp.maximum(raw + table_ref[1:2, 0:out_lanes], 0.0)
    raw = dot(tails, rest_ref[...])
    first[low:high, out_lanes:] = jnp.maximum(raw + table_ref[1:2, out_lanes:], 0.0)


def convolve_second(low, high, planes, block, first, table_ref, band_two):
    out_lanes = planes * block
    wide, _ = three_taps(first, low, high, out_lanes)
    second = dot(wide, band_two[...])
    second = jnp.maximum(second + table_ref[2:3, 0:out_lanes], 0.0) * table_ref[3:4, 0:out_lanes]
    half = out_lanes // 2
    return second[:, 0:half] + second[:, half:]


def weights(second, spread_ref):
    upper = second.astype(jnp.bfloat16)
    under = (second - upper.astype(jnp.float32)).astype(jnp.bfloat16)
    score = dot(jnp.concatenate([upper, under], axis=1), spread_ref[...])
    return 1.0 / (1.0 + jnp.exp(-score))


def first_stage(
    views, tall, planes, block, filled, mend, match, first, table_ref, band_one, rest_ref
):
    for at in range(0, views, BATCH):
        for v in range(at, at + BATCH):
            filled(v)
        low, high = at * tall, (at + BATCH) * tall
        convolve_first(low, high, planes, block, match, first, table_ref, band_one, rest_ref)
        for v in range(at, at + BATCH):
            mend(v * tall)


def second_stage(views, tall, planes, block, match, first, table_ref, band_two, spread_ref):
    out_lanes = planes * block
    total = weighted = 0.0
    steps = range(0, views, BATCH)
    seconds = [
        convolve_second(at * tall, (at + BATCH) * tall, planes, block, first, table_ref, band_two)
        for at in steps
    ]
    for at, second in zip(steps, seconds):
        weight = weights(second, spread_ref)
        for v in range(BATCH):
            part = weight[v * tall : (v + 1) * tall]
            row = (at + v) * tall + 2
            total = total + part
            weighted = weighted + part * match[row : row + tall, 2 * block : 2 * block + out_lanes]
    return weighted / total


def pack_shifts(shifts, before, after, word_ref):
    for row, ref in enumerate((before, shifts, after)):
        word = ref[0:1]
        for v in range(1, ref.shape[0]):
            word = word | (ref[v : v + 1] << (8 * v))
        word_ref[row : row + 1, 0 : word.shape[1]] = word


def read_shifts(views, planes, word_ref):
    at = [(0, planes - 2), (0, planes - 1)] + [(1, d) for d in range(planes)] + [(2, 0), (2, 1)]
    words = [word_ref[row, d] for row, d in at]
    return [[(word >> (8 * v)) & 255 for word in words] for v in range(views)]


def inner_body(
    shifts,
    before,
    after,
    bias_one,
    bias_two,
    view_head,
    own_ref,
    other_ref,
    ref_ref,
    own_order_ref,
    other_order_ref,
    taps_ref,
    cols_ref,
    ref_cols_ref,
    word_ref,
    table_ref,
    spread_ref,
    perm_ref,
    band_one,
    rest_ref,
    band_two,
    match,
    first,
    src,
    wide,
):
    views, half, rows, width = own_ref.shape
    planes = shifts.shape[1]
    lanes = 2 * half * rows
    inner = 2 * half // GROUPS
    block = GROUPS * rows
    _, _, _, _, *ends = position()
    pick = columns_of(width, width, 0)
    none = jnp.zeros((8, lanes), jnp.float32)
    columns = turned_ref(ref_ref, pick)
    ref_cols_ref[...] = columns.astype(jnp.bfloat16)
    wide[0:width] = columns
    wide[width:] = none
    pairs = zip(
        turned_half(own_ref, pick, own_order_ref[...]),
        turned_half(other_ref, pick, other_order_ref[...]),
    )
    for i, (low, high) in enumerate(pairs):
        columns = low + high
        for k in range(2):
            v = 2 * i + k
            part = columns[:, k * lanes : (k + 1) * lanes]
            cols_ref[v] = part.astype(jnp.bfloat16)
            src[v, 0:8] = none
            src[v, 8 : 8 + width] = part
            src[v, 8 + width :] = none
    build_tables(
        planes, rows, inner, bias_one, bias_two, view_head, ends, table_ref, spread_ref, perm_ref
    )
    build_band_one(taps_ref, band_one, rest_ref, rows)
    build_band_two(taps_ref, band_two, rows)
    pack_shifts(shifts, before, after, word_ref)
    near = read_shifts(views, planes, word_ref)
    out_rows = width - MAX_SHIFT
    tall = out_rows + 8
    base = MAX_SHIFT - 2

    def filled(v):
        pieces = [
            (v * tall + r, 8 + base + r, base + r, min(48, tall - r)) for r in range(0, tall, 48)
        ]
        fill(pieces, near[v], src.at[v], wide, match, table_ref, block)

    first_stage(
        views,
        tall,
        planes,
        block,
        filled,
        lambda row: None,
        match,
        first,
        table_ref,
        band_one,
        rest_ref,
    )
    for ref in (match, first):
        ref[views * tall :] = jnp.zeros((8, match.shape[1]), jnp.float32)


def late_body(match, first, table_ref, spread_ref, band_two, late_ref):
    out_rows, out_lanes = late_ref.shape
    block = (match.shape[1] - out_lanes) // 4
    views = match.shape[0] // (out_rows + 8)
    joined = second_stage(
        views, out_rows + 8, out_lanes // block, block, match, first, table_ref, band_two, spread_ref
    )
    late_ref[...] = joined[0:out_rows].astype(jnp.bfloat16)


def outer_body(
    cols_ref,
    ref_cols_ref,
    word_ref,
    table_ref,
    spread_ref,
    perm_ref,
    band_one,
    rest_ref,
    band_two,
    late_ref,
    got_ref,
    swapped_ref,
    out_ref,
    src,
    wide,
    match,
    first,
    joined,
):
    views, width, lanes = cols_ref.shape
    groups, planes, rows, _ = out_ref.shape
    block = groups * rows
    _, order, is_first_tile, is_last_tile, *_ = position()

    near = read_shifts(views, planes, word_ref)
    left = jnp.where(order == 0, got_ref[...], swapped_ref[...])
    right = jnp.where(order == 0, swapped_ref[...], got_ref[...])
    left = jnp.where(is_first_tile, jnp.zeros_like(left), left)
    right = jnp.where(is_last_tile, jnp.zeros_like(right), right)
    for v in range(0, views, 2):
        at = v * LEAD
        pair = left[at : at + 2 * LEAD].astype(jnp.float32)
        ends = right[at : at + LEAD + 24].astype(jnp.float32)
        for k in range(2):
            src[v + k, 0:LEAD] = pair[k * LEAD : (k + 1) * LEAD]
            src[v + k, LEAD : LEAD + width] = cols_ref[v + k].astype(jnp.float32)
            src[v + k, LEAD + width :] = ends[k * LEAD : k * LEAD + EDGE]
    wide[0:EDGE] = left[views * LEAD :].astype(jnp.float32)
    wide[EDGE : EDGE + width] = ref_cols_ref[...].astype(jnp.float32)
    wide[EDGE + width :] = right[views * LEAD : views * LEAD + EDGE].astype(jnp.float32)
    main = MAX_SHIFT + 8
    tall = main + 8
    none = jnp.zeros((1, match.shape[1]), jnp.float32)

    def filled(v):
        at = v * tall
        pieces = [
            (at + r, LEAD - 2 + r, EDGE - 2 + r, min(48, main - r)) for r in range(0, main, 48)
        ]
        pieces += [(at + main, LEAD + width - 4, EDGE + width - 4, 8)]
        fill(pieces, near[v], src.at[v], wide, match, table_ref, block)

    def mend(row):
        for at, at_end in ((row, is_first_tile), (row + main + 3, is_last_tile)):
            first[at : at + 1] = jnp.where(at_end, none, first[at : at + 1])

    first_stage(
        views, tall, planes, block, filled, mend, match, first, table_ref, band_one, rest_ref
    )
    part = second_stage(
        views, tall, planes, block, match, first, table_ref, band_two, spread_ref
    )
    joined[0:MAX_SHIFT] = part[0:MAX_SHIFT]
    joined[MAX_SHIFT:] = late_ref[...].astype(jnp.float32)
    joined[MAX_SHIFT : MAX_SHIFT + 2] = part[MAX_SHIFT : MAX_SHIFT + 2]
    joined[width - 2 :] = part[main : main + 2]
    turned = dot_nt(perm_ref[...], joined[...].astype(jnp.bfloat16)).astype(jnp.bfloat16)
    out_ref[...] = turned.reshape(groups, planes, rows, width)


def whole(memory):
    return pl.BlockSpec(memory_space=memory)


def limit(mebibytes):
    return pltpu.CompilerParams(vmem_limit_bytes=mebibytes * 1024 * 1024)


def swap_planes(value):
    return lax.ppermute(value, "plane", [(0, 1), (1, 0)])


def per_device(ref_feat, src_feat, shifts, conv_one, bias_one, conv_two, bias_two, view_head):
    views, _, rows, width = src_feat.shape
    planes = shifts.shape[1]
    lanes = ref_feat.shape[0] * rows
    tiles, sides = lax.axis_size("tile"), lax.axis_size("plane")
    bf16, f32 = jnp.bfloat16, jnp.float32
    vmem = pltpu.VMEM
    shape = jax.ShapeDtypeStruct
    if sides == 2:
        own, other = src_feat, swap_planes(src_feat)
    else:
        full = lax.all_gather(src_feat, "plane", axis=1, tiled=True)
        half = full.shape[1] // 2
        own, other = full[:, :half], full[:, half:]

    packet_shape = shape((views * LEAD + EDGE, lanes), bf16)
    order_shape = shape((lanes, 2 * lanes), bf16)
    own, ref_feat, part, pick, own_order, other_order = pl.pallas_call(
        pack_own_body,
        out_shape=[
            shape(own.shape, bf16),
            shape(ref_feat.shape, bf16),
            packet_shape,
            shape((LEAD, width), bf16),
            order_shape,
            order_shape,
        ],
        in_specs=[whole(pltpu.HBM)] * 2,
        out_specs=[whole(vmem)] * 6,
        scratch_shapes=[pltpu.SemaphoreType.DMA((2,))],
        compiler_params=limit(8),
        name="pack_own",
    )(*(pltpu.with_memory_space_constraint(x, pltpu.HBM) for x in (own, ref_feat)))
    packet = pl.pallas_call(
        pack_other_body,
        out_shape=packet_shape,
        in_specs=[whole(vmem)] * 4,
        out_specs=whole(vmem),
        compiler_params=limit(8),
        name="pack_other",
    )(part, pick, other_order, other)

    pairs = [(sides * i, sides * (i + 1)) for i in range(tiles - 1)]
    pairs += [(sides * (i + 1) + 1, sides * i + 1) for i in range(tiles - 1)]
    pairs += [(sides * (tiles - 1), sides * (tiles - 1) + 1), (1, 0)]
    got = lax.ppermute(packet, ("tile", "plane"), pairs)

    own, other, shifts, conv_one, conv_two, packet = lax.optimization_barrier(
        (own, other, shifts, conv_one, conv_two, packet)
    )
    if sides == 2:
        before = after = swap_planes(shifts)
    else:
        before = lax.ppermute(shifts, "plane", [(i, i + 1) for i in range(sides - 1)])
        after = lax.ppermute(shifts, "plane", [(i + 1, i) for i in range(sides - 1)])

    def taps(kernel):
        flipped = jnp.flip(kernel, axis=2)
        return jnp.transpose(flipped, (3, 4, 1, 2, 0)).reshape(9 * GROUPS, 3 * GROUPS)

    both_taps = jnp.stack([taps(conv_one), taps(conv_two)])
    span = (planes + 4) * GROUPS * rows
    out_lanes = planes * GROUPS * rows
    late_rows = width - MAX_SHIFT
    high = views * (late_rows + 8) + 8
    *inner, match, first = pl.pallas_call(
        inner_body,
        out_shape=[
            shape((views, width, lanes), bf16),
            shape((width, lanes), bf16),
            shape((8, 128), jnp.int32),
            shape((8, span), f32),
            shape((256, out_lanes), bf16),
            shape((out_lanes, out_lanes), bf16),
            shape((4 * out_lanes, out_lanes), bf16),
            shape((3 * (span - out_lanes), span - out_lanes), bf16),
            shape((4 * out_lanes, out_lanes), bf16),
            shape((high, span), f32),
            shape((high, span), f32),
        ],
        in_specs=[whole(vmem)] * 12,
        out_specs=[whole(vmem)] * 11,
        scratch_shapes=[
            pltpu.VMEM((views, width + 16, lanes), f32),
            pltpu.VMEM((width + 8, lanes), f32),
        ],
        compiler_params=limit(24),
        cost_estimate=pl.CostEstimate(
            flops=3 * 10**9, bytes_accessed=10**6, transcendentals=10**5
        ),
        name="inner_columns",
    )(
        shifts,
        before,
        after,
        bias_one,
        bias_two,
        view_head,
        own,
        other,
        ref_feat,
        own_order,
        other_order,
        both_taps,
    )
    got, match, first, *inner = lax.optimization_barrier((got, match, first, *inner))
    if sides == 2:
        swapped = swap_planes(got)
    else:
        both = lax.all_gather(got, "plane", axis=0)
        got, swapped = both[0], both[1]
    late = pl.pallas_call(
        late_body,
        out_shape=shape((late_rows, out_lanes), bf16),
        in_specs=[whole(vmem)] * 5,
        out_specs=whole(vmem),
        compiler_params=limit(24),
        cost_estimate=pl.CostEstimate(
            flops=2 * 10**9, bytes_accessed=10**6, transcendentals=10**5
        ),
        name="late_columns",
    )(match, first, inner[3], inner[4], inner[8])
    high = views * (MAX_SHIFT + 16) + 8
    return pl.pallas_call(
        outer_body,
        out_shape=shape((GROUPS, planes, rows, width), bf16),
        in_specs=[whole(vmem)] * 12,
        out_specs=whole(vmem),
        scratch_shapes=[
            pltpu.VMEM((views, LEAD + width + EDGE, lanes), f32),
            pltpu.VMEM((EDGE + width + EDGE, lanes), f32),
            pltpu.VMEM((high, span), f32),
            pltpu.VMEM((high, span), f32),
            pltpu.VMEM((width, out_lanes), f32),
        ],
        compiler_params=limit(24),
        name="outer_columns",
    )(*inner, late, got, swapped)


def solution(mesh):
    placed = (
        P(None, None, "tile"),
        P(None, "plane", None, "tile"),
        P(None, "plane"),
        P(),
        P(),
        P(),
        P(),
        P(),
    )
    return jax.shard_map(
        per_device,
        mesh=mesh,
        in_specs=placed,
        out_specs=P(None, "plane", None, "tile"),
        check_vma=False,
    )
```

```python
import jax
import jax.numpy as jnp
from jax import lax
from jax.experimental import pallas as pl
from jax.experimental.pallas import tpu as pltpu
from jax.sharding import PartitionSpec as P

GROUPS = 8
MAX_SHIFT = 128
LEAD = MAX_SHIFT + 8
EDGE = 16
BATCH = 2
FAR = -3.0e38


def iota(shape, dim):
    return lax.broadcasted_iota(jnp.int32, shape, dim)


def dot(left, right):
    return jnp.dot(left, right, preferred_element_type=jnp.float32)


def dot_nt(left, right):
    return lax.dot_general(
        left, right, (((1,), (1,)), ((), ())), preferred_element_type=jnp.float32
    )


def position():
    tile, plane = lax.axis_index("tile"), lax.axis_index("plane")
    tiles, sides = lax.axis_size("tile"), lax.axis_size("plane")
    order = plane if sides == 2 else 0 * plane
    role = jnp.minimum(plane, 1)
    return role, order, tile == 0, tile == tiles - 1, plane == 0, plane == sides - 1


def columns_of(count, width, start):
    picked = iota((count, width), 0) + start == iota((count, width), 1)
    return picked.astype(jnp.bfloat16)


def lane_order(half, rows, side):
    lanes = 2 * half * rows
    inner = 2 * half // GROUPS
    at, to = iota((lanes, 2 * lanes), 0), iota((lanes, 2 * lanes), 1)
    k, g = (to // (GROUPS * rows)) % inner, (to // rows) % GROUPS
    channel = g * inner + k - half * side
    row = (to // lanes) * (half * rows) + channel * rows + to % rows
    held = (channel >= 0) & (channel < half) & (row == at)
    return held.astype(jnp.bfloat16)


def ref_order(lanes, rows):
    at, to = iota((lanes, lanes), 0), iota((lanes, lanes), 1)
    k, g, h = to // (GROUPS * rows), (to // rows) % GROUPS, to % rows
    return ((g * (lanes // (GROUPS * rows)) + k) * rows + h == at).astype(jnp.bfloat16)


def turned_half(half_ref, pick, order):
    views, half, rows, width = half_ref.shape
    lanes = 2 * half * rows
    block = half_ref[...].reshape(views * half * rows, width)
    columns = dot_nt(pick, block).astype(jnp.bfloat16)
    return [dot(columns[:, i : i + lanes], order) for i in range(0, columns.shape[1], lanes)]


def turned_ref(ref_ref, pick):
    channels, rows, width = ref_ref.shape
    lanes = channels * rows
    columns = dot_nt(pick, ref_ref[...].reshape(lanes, width)).astype(jnp.bfloat16)
    return dot(columns, ref_order(lanes, rows))


def edge_start(role, width, count):
    return jnp.where(role == 0, width - count, 0)


def stacked(pair, lanes):
    return jnp.concatenate([pair[:, 0:lanes], pair[:, lanes:]], axis=0)


def pack_own_body(*refs):
    count = (len(refs) - 5) // 2
    sources, targets = refs[:count], refs[count : 2 * count]
    part_ref, pick_ref, own_order_ref, other_order_ref, sems = refs[2 * count :]
    copies = [
        pltpu.make_async_copy(source, target, sems.at[i])
        for i, (source, target) in enumerate(zip(sources, targets))
    ]
    for copy in copies:
        copy.start()
    own_ref, ref_ref = targets[:2]
    views, half, rows, width = own_ref.shape
    lanes = part_ref.shape[1]
    role, order, *_ = position()
    pick_ref[...] = columns_of(LEAD, width, edge_start(role, width, LEAD))
    own_order_ref[...] = lane_order(half, rows, order)
    other_order_ref[...] = lane_order(half, rows, 1 - order)
    few = columns_of(EDGE, width, edge_start(role, width, EDGE))
    copies[0].wait()
    for i, pair in enumerate(turned_half(own_ref, pick_ref[...], own_order_ref[...])):
        at = 2 * i * LEAD
        part_ref[at : at + 2 * LEAD] = stacked(pair, lanes).astype(jnp.bfloat16)
    for copy in copies[1:]:
        copy.wait()
    part_ref[views * LEAD :] = turned_ref(ref_ref, few).astype(jnp.bfloat16)


def pack_other_body(part_ref, pick_ref, other_order_ref, other_ref, packet_ref):
    views = other_ref.shape[0]
    lanes = packet_ref.shape[1]
    for i, pair in enumerate(turned_half(other_ref, pick_ref[...], other_order_ref[...])):
        at = 2 * i * LEAD
        both = part_ref[at : at + 2 * LEAD].astype(jnp.float32) + stacked(pair, lanes)
        packet_ref[at : at + 2 * LEAD] = both.astype(jnp.bfloat16)
    packet_ref[views * LEAD :] = part_ref[views * LEAD :]


def lane_table(values_ref, rows, lane):
    which = lane // rows % GROUPS
    table = jnp.zeros(lane.shape, jnp.float32)
    for o in range(GROUPS):
        table = jnp.where(which == o, values_ref[o], table)
    return table


def base_blocks(taps_ref, which, rows, apart):
    block = GROUPS * rows
    slots = 128 // (4 * rows)
    at, lane = iota((3 * GROUPS, 128), 0), iota((3 * GROUPS, 128), 1)
    if apart:
        spreads = [
            (lane // (slots * rows) + t * 4 == at % GROUPS)
            & ((lane // rows) % slots == at // GROUPS)
            for t in range(2)
        ]
    else:
        spreads = [lane // rows == at]
    stretch = (iota((block, GROUPS), 0) // rows == iota((block, GROUPS), 1)).astype(jnp.bfloat16)
    gap = iota((block, 128), 0) % rows - iota((block, 128), 1) % rows + 1
    found = []
    for spread in spreads:
        wide = dot(taps_ref[which], spread.astype(jnp.bfloat16)).astype(jnp.bfloat16)
        for e in range(3):
            base = jnp.zeros((block, 128), jnp.float32)
            for b in range(3):
                at = (b * 3 + e) * GROUPS
                base = jnp.where(gap == b, dot(stretch, wide[at : at + GROUPS]), base)
            found.append(base)
    return [found[i : i + 3] for i in range(0, len(found), 3)]


def band_rows(e, j, block):
    per_tile = 128 // block
    whole = 2 * per_tile
    if j < whole:
        return (e * whole + j) * block
    return (3 * whole + 2 * e + j - whole) * block


def build_band_one(taps_ref, band_ref, rest_ref, rows):
    block = GROUPS * rows
    lane = iota((block, 128), 1)
    per_tile = 128 // block
    zero = jnp.zeros((block, 128), jnp.bfloat16)
    (bases,) = base_blocks(taps_ref, 0, rows, False)
    for e, base in enumerate(bases):
        low_parts, high_parts = [], []
        for turn in range(per_tile):
            moved = pltpu.roll(base, turn * block, 1) if turn else base
            high_parts.append(jnp.where(lane >= turn * block, moved, 0.0).astype(jnp.bfloat16))
            low_parts.append(jnp.where(lane < turn * block, moved, 0.0).astype(jnp.bfloat16))
        for j in range(2 * per_tile + 2):
            first, turn = (j - 2) // per_tile, (j - 2) % per_tile
            at = band_rows(e, j, block)
            for t in range(2):
                part = zero
                if t == first:
                    part = high_parts[turn]
                elif t == first + 1 and turn > per_tile - 3:
                    part = low_parts[turn]
                band_ref[at : at + block, t * 128 : (t + 1) * 128] = part
                if t == 0 and j < per_tile:
                    rest_ref[(e * per_tile + j) * block : (e * per_tile + j + 1) * block] = part
    for j in range(2):
        at = (3 * (2 * per_tile + 2) + j) * block
        band_ref[at : at + block] = jnp.zeros((block, 256), jnp.bfloat16)


def build_band_two(taps_ref, band_ref, rows):
    block = GROUPS * rows
    per_tile = 128 // block
    slots = 2 * per_tile
    plane = (iota((block, 128), 1) // rows) % slots
    for t, bases in enumerate(base_blocks(taps_ref, 1, rows, True)):
        for e, base in enumerate(bases):
            for j in range(slots + 2):
                turn = (j - 2) * rows % 128
                moved = pltpu.roll(base, turn, 1) if turn else base
                held = (plane >= j - 2) & (plane <= j)
                at = band_rows(e, j, block)
                band_ref[at : at + block, t * 128 : (t + 1) * 128] = jnp.where(
                    held, moved, 0.0
                ).astype(jnp.bfloat16)
    for j in range(2):
        at = (3 * (slots + 2) + j) * block
        band_ref[at : at + block] = jnp.zeros((block, 256), jnp.bfloat16)


def build_tables(planes, rows, inner, bias_one, bias_two, view_head, ends, table_ref, spread_ref, perm_ref):
    block = GROUPS * rows
    out_lanes = planes * block
    span = table_ref.shape[1]
    is_first_plane, is_last_plane = ends
    at = iota((1, span), 1)
    plane = at // block
    outside = ((plane < 2) & is_first_plane) | ((plane >= planes + 2) & is_last_plane)
    table_ref[0:1] = jnp.where(outside, 0.0, 1.0 / inner)
    outside = ((plane == 0) & is_first_plane) | ((plane == planes + 1) & is_last_plane)
    table_ref[1:2] = jnp.where(outside, FAR, lane_table(bias_one, rows, at))
    table_ref[2:3] = lane_table(bias_two, planes * rows, at)
    table_ref[3:4] = lane_table(view_head, planes * rows, at)
    row, lane = iota(spread_ref.shape, 0), iota(spread_ref.shape, 1)
    same = (row // rows % planes == lane // block) & (row % rows == lane % rows)
    spread_ref[...] = same.astype(jnp.bfloat16)
    to = iota(perm_ref.shape, 0)
    g, j, h = to // (planes * rows), (to // rows) % planes, to % rows
    perm = (j * GROUPS + g) * rows + h == iota(perm_ref.shape, 1)
    perm_ref[...] = perm.astype(jnp.bfloat16)


def fill(pieces, near, src, wide, match, table_ref, block):
    for at, src_at, wide_at, count in pieces:
        quarter = iota((count, 128), 1) // block
        lower, middle, even = quarter < 2, (quarter == 1) | (quarter == 2), quarter % 2 == 0
        here = wide[wide_at : wide_at + count]
        for q in range(match.shape[1] // 128):

            def product(j):
                return src[pl.ds(src_at - near[q * 4 + j], count)] * here

            a, c, b, d = (product(j) for j in range(4))
            x = jnp.where(lower, a, b) + pltpu.roll(jnp.where(lower, b, a), 64, 1)
            z = jnp.where(middle, c, d) + pltpu.roll(jnp.where(middle, d, c), 64, 1)
            y = jnp.where(even, x, z) + pltpu.roll(jnp.where(even, z, x), 96, 1)
            y = y * table_ref[0:1, q * 128 : (q + 1) * 128]
            y = y.astype(jnp.bfloat16).astype(jnp.float32)
            match[at : at + count, q * 128 : (q + 1) * 128] = y


def three_taps(volume, low, high, out_lanes):
    tile = volume.shape[1] - out_lanes
    parts = [volume[low + e : high + e] for e in range(3)]
    tails = [part[:, out_lanes:] for part in parts]
    near = iota((high - low, tile), 1) < tile // 2
    paired = jnp.where(near, tails[0], pltpu.roll(tails[1], tile // 2, 1))
    sides = [part[:, 0:out_lanes] for part in parts] + [paired, tails[2]]
    wide = jnp.concatenate([side.astype(jnp.bfloat16) for side in sides], axis=1)
    return wide, jnp.concatenate([tail.astype(jnp.bfloat16) for tail in tails], axis=1)


def convolve_first(low, high, planes, block, match, first, table_ref, band_one, rest_ref):
    out_lanes = planes * block
    wide, tails = three_taps(match, low, high, out_lanes)
    raw = dot(wide, band_one[...])
    main = jnp.maximum(raw + table_ref[1:2, 0:out_lanes], 0.0)
    raw = dot(tails, rest_ref[...])
    rest = jnp.maximum(raw + table_ref[1:2, out_lanes:], 0.0)

    def store():
        first[low:high, 0:out_lanes] = main
        first[low:high, out_lanes:] = rest

    return store


def convolve_second(low, high, planes, block, first, table_ref, band_two):
    out_lanes = planes * block
    wide, _ = three_taps(first, low, high, out_lanes)
    second = dot(wide, band_two[...])
    second = jnp.maximum(second + table_ref[2:3, 0:out_lanes], 0.0) * table_ref[3:4, 0:out_lanes]
    half = out_lanes // 2
    return second[:, 0:half] + second[:, half:]


def weights(second, spread_ref):
    upper = second.astype(jnp.bfloat16)
    under = (second - upper.astype(jnp.float32)).astype(jnp.bfloat16)
    score = dot(jnp.concatenate([upper, under], axis=1), spread_ref[...])
    return 1.0 / (1.0 + jnp.exp(-score))


def first_stage(
    views, tall, planes, block, filled, mend, match, first, table_ref, band_one, rest_ref
):
    store = None
    for v in range(views + 1):
        if v < views:
            filled(v)
        if store is not None:
            store()
            mend((v - 1) * tall)
        if v < views:
            low, high = v * tall, (v + 1) * tall
            store = convolve_first(
                low, high, planes, block, match, first, table_ref, band_one, rest_ref
            )


def second_stage(views, tall, planes, block, match, first, table_ref, band_two, spread_ref):
    out_lanes = planes * block
    total = weighted = 0.0
    steps = range(0, views, BATCH)
    seconds = [
        convolve_second(at * tall, (at + BATCH) * tall, planes, block, first, table_ref, band_two)
        for at in steps
    ]
    for at, second in zip(steps, seconds):
        weight = weights(second, spread_ref)
        for v in range(BATCH):
            part = weight[v * tall : (v + 1) * tall]
            row = (at + v) * tall + 2
            total = total + part
            weighted = weighted + part * match[row : row + tall, 2 * block : 2 * block + out_lanes]
    return weighted / total


def pack_shifts(shifts, before, after, word_ref):
    for row, ref in enumerate((before, shifts, after)):
        word = ref[0:1]
        for v in range(1, ref.shape[0]):
            word = word | (ref[v : v + 1] << (8 * v))
        word_ref[row : row + 1, 0 : word.shape[1]] = word


def read_shifts(views, planes, word_ref):
    at = [(0, planes - 2), (0, planes - 1)] + [(1, d) for d in range(planes)] + [(2, 0), (2, 1)]
    words = [word_ref[row, d] for row, d in at]
    return [[(word >> (8 * v)) & 255 for word in words] for v in range(views)]


def inner_body(
    shifts,
    before,
    after,
    bias_one,
    bias_two,
    view_head,
    own_ref,
    other_ref,
    ref_ref,
    own_order_ref,
    other_order_ref,
    taps_ref,
    cols_ref,
    ref_cols_ref,
    word_ref,
    table_ref,
    spread_ref,
    perm_ref,
    band_one,
    rest_ref,
    band_two,
    match,
    first,
    src,
    wide,
):
    views, half, rows, width = own_ref.shape
    planes = shifts.shape[1]
    lanes = 2 * half * rows
    inner = 2 * half // GROUPS
    block = GROUPS * rows
    _, _, _, _, *ends = position()
    pick = columns_of(width, width, 0)
    none = jnp.zeros((8, lanes), jnp.float32)
    columns = turned_ref(ref_ref, pick)
    ref_cols_ref[...] = columns.astype(jnp.bfloat16)
    wide[0:width] = columns
    wide[width:] = none
    pairs = zip(
        turned_half(own_ref, pick, own_order_ref[...]),
        turned_half(other_ref, pick, other_order_ref[...]),
    )
    for i, (low, high) in enumerate(pairs):
        columns = low + high
        for k in range(2):
            v = 2 * i + k
            part = columns[:, k * lanes : (k + 1) * lanes]
            cols_ref[v] = part.astype(jnp.bfloat16)
            src[v, 0:8] = none
            src[v, 8 : 8 + width] = part
            src[v, 8 + width :] = none
    build_tables(
        planes, rows, inner, bias_one, bias_two, view_head, ends, table_ref, spread_ref, perm_ref
    )
    build_band_one(taps_ref, band_one, rest_ref, rows)
    build_band_two(taps_ref, band_two, rows)
    pack_shifts(shifts, before, after, word_ref)
    near = read_shifts(views, planes, word_ref)
    out_rows = width - MAX_SHIFT
    tall = out_rows + 8
    base = MAX_SHIFT - 2

    def filled(v):
        pieces = [
            (v * tall + r, 8 + base + r, base + r, min(48, tall - r)) for r in range(0, tall, 48)
        ]
        fill(pieces, near[v], src.at[v], wide, match, table_ref, block)

    first_stage(
        views,
        tall,
        planes,
        block,
        filled,
        lambda row: None,
        match,
        first,
        table_ref,
        band_one,
        rest_ref,
    )
    for ref in (match, first):
        ref[views * tall :] = jnp.zeros((8, match.shape[1]), jnp.float32)


def late_body(match, first, table_ref, spread_ref, band_two, late_ref):
    out_rows, out_lanes = late_ref.shape
    block = (match.shape[1] - out_lanes) // 4
    views = match.shape[0] // (out_rows + 8)
    joined = second_stage(
        views, out_rows + 8, out_lanes // block, block, match, first, table_ref, band_two, spread_ref
    )
    late_ref[...] = joined[0:out_rows].astype(jnp.bfloat16)


def outer_body(
    cols_ref,
    ref_cols_ref,
    word_ref,
    table_ref,
    spread_ref,
    perm_ref,
    band_one,
    rest_ref,
    band_two,
    late_ref,
    got_ref,
    swapped_ref,
    out_ref,
    src,
    wide,
    match,
    first,
    joined,
    buffer,
    sems,
):
    views, width, lanes = cols_ref.shape
    groups, planes, rows, _ = out_ref.shape
    block = groups * rows
    _, order, is_first_tile, is_last_tile, *_ = position()

    near = read_shifts(views, planes, word_ref)
    left = jnp.where(order == 0, got_ref[...], swapped_ref[...])
    left = jnp.where(is_first_tile, jnp.zeros_like(left), left)
    right = jnp.where(order == 0, swapped_ref[...], got_ref[...])
    for v in range(0, views, 2):
        at = v * LEAD
        pair = left[at : at + 2 * LEAD].astype(jnp.float32)
        ends = right[at : at + LEAD + 24].astype(jnp.float32)
        for k in range(2):
            src[v + k, 0:LEAD] = pair[k * LEAD : (k + 1) * LEAD]
            src[v + k, LEAD : LEAD + width] = cols_ref[v + k].astype(jnp.float32)
            src[v + k, LEAD + width :] = ends[k * LEAD : k * LEAD + EDGE]
    wide[0:EDGE] = left[views * LEAD :].astype(jnp.float32)
    wide[EDGE : EDGE + width] = ref_cols_ref[...].astype(jnp.float32)
    wide[EDGE + width :] = jnp.where(is_last_tile, 0.0, right[views * LEAD :].astype(jnp.float32))
    main = MAX_SHIFT + 8
    tall = main + 8
    none = jnp.zeros((1, match.shape[1]), jnp.float32)

    def filled(v):
        at = v * tall
        pieces = [
            (at + r, LEAD - 2 + r, EDGE - 2 + r, min(48, main - r)) for r in range(0, main, 48)
        ]
        pieces += [(at + main, LEAD + width - 4, EDGE + width - 4, 8)]
        fill(pieces, near[v], src.at[v], wide, match, table_ref, block)

    def mend(row):
        for at, at_end in ((row, is_first_tile), (row + main + 3, is_last_tile)):
            first[at : at + 1] = jnp.where(at_end, none, first[at : at + 1])

    first_stage(
        views, tall, planes, block, filled, mend, match, first, table_ref, band_one, rest_ref
    )
    part = second_stage(
        views, tall, planes, block, match, first, table_ref, band_two, spread_ref
    )
    joined[0:MAX_SHIFT] = part[0:MAX_SHIFT]
    joined[MAX_SHIFT:] = late_ref[...].astype(jnp.float32)
    joined[MAX_SHIFT : MAX_SHIFT + 2] = part[MAX_SHIFT : MAX_SHIFT + 2]
    joined[width - 2 :] = part[main : main + 2]
    copies = []
    for half in range(2):
        at = half * (groups // 2)
        span = pl.ds(at, groups // 2)
        chosen = perm_ref[at * planes * rows : (at + groups // 2) * planes * rows]
        turned = dot_nt(chosen, joined[...].astype(jnp.bfloat16)).astype(jnp.bfloat16)
        buffer[at : at + groups // 2] = turned.reshape(groups // 2, planes, rows, width)
        copy = pltpu.make_async_copy(buffer.at[span], out_ref.at[span], sems.at[half])
        copy.start()
        copies.append(copy)
    for copy in copies:
        copy.wait()


def whole(memory):
    return pl.BlockSpec(memory_space=memory)


def limit(mebibytes):
    return pltpu.CompilerParams(vmem_limit_bytes=mebibytes * 1024 * 1024)


def swap_planes(value):
    return lax.ppermute(value, "plane", [(0, 1), (1, 0)])


def per_device(ref_feat, src_feat, shifts, conv_one, bias_one, conv_two, bias_two, view_head):
    views, _, rows, width = src_feat.shape
    planes = shifts.shape[1]
    lanes = ref_feat.shape[0] * rows
    tiles, sides = lax.axis_size("tile"), lax.axis_size("plane")
    bf16, f32 = jnp.bfloat16, jnp.float32
    vmem = pltpu.VMEM
    shape = jax.ShapeDtypeStruct
    if sides == 2:
        own, other = src_feat, swap_planes(src_feat)
    else:
        full = lax.all_gather(src_feat, "plane", axis=1, tiled=True)
        half = full.shape[1] // 2
        own, other = full[:, :half], full[:, half:]

    packet_shape = shape((views * LEAD + EDGE, lanes), bf16)
    order_shape = shape((lanes, 2 * lanes), bf16)
    staged = (own, ref_feat, shifts, bias_one, bias_two, view_head)
    *staged, part, pick, own_order, other_order = pl.pallas_call(
        pack_own_body,
        out_shape=[shape(x.shape, x.dtype) for x in staged]
        + [packet_shape, shape((LEAD, width), bf16), order_shape, order_shape],
        in_specs=[whole(pltpu.HBM)] * len(staged),
        out_specs=[whole(vmem)] * (len(staged) + 4),
        scratch_shapes=[pltpu.SemaphoreType.DMA((len(staged),))],
        compiler_params=limit(8),
        name="pack_own",
    )(*(pltpu.with_memory_space_constraint(x, pltpu.HBM) for x in staged))
    own, ref_feat, shifts, bias_one, bias_two, view_head = staged
    packet = pl.pallas_call(
        pack_other_body,
        out_shape=packet_shape,
        in_specs=[whole(vmem)] * 4,
        out_specs=whole(vmem),
        compiler_params=limit(8),
        name="pack_other",
    )(part, pick, other_order, other)

    pairs = [(sides * i, sides * (i + 1)) for i in range(tiles - 1)]
    pairs += [(sides * (i + 1) + 1, sides * i + 1) for i in range(tiles - 1)]
    pairs += [(sides * (tiles - 1), sides * (tiles - 1) + 1), (1, 0)]
    got = lax.ppermute(packet, ("tile", "plane"), pairs)

    own, other, shifts, conv_one, conv_two, packet = lax.optimization_barrier(
        (own, other, shifts, conv_one, conv_two, packet)
    )
    if sides == 2:
        before = after = swap_planes(shifts)
    else:
        before = lax.ppermute(shifts, "plane", [(i, i + 1) for i in range(sides - 1)])
        after = lax.ppermute(shifts, "plane", [(i + 1, i) for i in range(sides - 1)])

    def taps(kernel):
        flipped = jnp.flip(kernel, axis=2)
        return jnp.transpose(flipped, (3, 4, 1, 2, 0)).reshape(9 * GROUPS, 3 * GROUPS)

    both_taps = jnp.stack([taps(conv_one), taps(conv_two)])
    span = (planes + 4) * GROUPS * rows
    out_lanes = planes * GROUPS * rows
    late_rows = width - MAX_SHIFT
    high = views * (late_rows + 8) + 8
    *inner, match, first = pl.pallas_call(
        inner_body,
        out_shape=[
            shape((views, width, lanes), bf16),
            shape((width, lanes), bf16),
            shape((8, 128), jnp.int32),
            shape((8, span), f32),
            shape((256, out_lanes), bf16),
            shape((out_lanes, out_lanes), bf16),
            shape((4 * out_lanes, out_lanes), bf16),
            shape((3 * (span - out_lanes), span - out_lanes), bf16),
            shape((4 * out_lanes, out_lanes), bf16),
            shape((high, span), f32),
            shape((high, span), f32),
        ],
        in_specs=[whole(vmem)] * 12,
        out_specs=[whole(vmem)] * 11,
        scratch_shapes=[
            pltpu.VMEM((views, width + 16, lanes), f32),
            pltpu.VMEM((width + 8, lanes), f32),
        ],
        compiler_params=limit(24),
        cost_estimate=pl.CostEstimate(
            flops=3 * 10**9, bytes_accessed=10**6, transcendentals=10**5
        ),
        name="inner_columns",
    )(
        shifts,
        before,
        after,
        bias_one,
        bias_two,
        view_head,
        own,
        other,
        ref_feat,
        own_order,
        other_order,
        both_taps,
    )
    got, match, first, *inner = lax.optimization_barrier((got, match, first, *inner))
    if sides == 2:
        swapped = swap_planes(got)
    else:
        both = lax.all_gather(got, "plane", axis=0)
        got, swapped = both[0], both[1]
    late = pl.pallas_call(
        late_body,
        out_shape=shape((late_rows, out_lanes), bf16),
        in_specs=[whole(vmem)] * 5,
        out_specs=whole(vmem),
        compiler_params=limit(24),
        cost_estimate=pl.CostEstimate(
            flops=2 * 10**9, bytes_accessed=10**6, transcendentals=10**5
        ),
        name="late_columns",
    )(match, first, inner[3], inner[4], inner[8])
    high = views * (MAX_SHIFT + 16) + 8
    return pl.pallas_call(
        outer_body,
        out_shape=shape((GROUPS, planes, rows, width), bf16),
        in_specs=[whole(vmem)] * 12,
        out_specs=whole(pltpu.HBM),
        scratch_shapes=[
            pltpu.VMEM((views, LEAD + width + EDGE, lanes), f32),
            pltpu.VMEM((EDGE + width + EDGE, lanes), f32),
            pltpu.VMEM((high, span), f32),
            pltpu.VMEM((high, span), f32),
            pltpu.VMEM((width, out_lanes), f32),
            pltpu.VMEM((GROUPS, planes, rows, width), bf16),
            pltpu.SemaphoreType.DMA((2,)),
        ],
        compiler_params=limit(24),
        name="outer_columns",
    )(*inner, late, got, swapped)


def solution(mesh):
    placed = (
        P(None, None, "tile"),
        P(None, "plane", None, "tile"),
        P(None, "plane"),
        P(),
        P(),
        P(),
        P(),
        P(),
    )
    return jax.shard_map(
        per_device,
        mesh=mesh,
        in_specs=placed,
        out_specs=P(None, "plane", None, "tile"),
        check_vma=False,
    )
```

```python
import jax
import jax.numpy as jnp
from jax import lax
from jax.experimental import pallas as pl
from jax.experimental.pallas import tpu as pltpu
from jax.sharding import PartitionSpec as P

GROUPS = 8
MAX_SHIFT = 128
LEAD = MAX_SHIFT + 8
EDGE = 16
BATCH = 2
FAR = -3.0e38


def iota(shape, dim):
    return lax.broadcasted_iota(jnp.int32, shape, dim)


def dot(left, right):
    return jnp.dot(left, right, preferred_element_type=jnp.float32)


def dot_nt(left, right):
    return lax.dot_general(
        left, right, (((1,), (1,)), ((), ())), preferred_element_type=jnp.float32
    )


def position():
    tile, plane = lax.axis_index("tile"), lax.axis_index("plane")
    tiles, sides = lax.axis_size("tile"), lax.axis_size("plane")
    order = plane if sides == 2 else 0 * plane
    role = jnp.minimum(plane, 1)
    return role, order, tile == 0, tile == tiles - 1, plane == 0, plane == sides - 1


def columns_of(count, width, start):
    picked = iota((count, width), 0) + start == iota((count, width), 1)
    return picked.astype(jnp.bfloat16)


def lane_order(half, rows, side):
    lanes = 2 * half * rows
    inner = 2 * half // GROUPS
    at, to = iota((lanes, 2 * lanes), 0), iota((lanes, 2 * lanes), 1)
    k, g = (to // (GROUPS * rows)) % inner, (to // rows) % GROUPS
    channel = g * inner + k - half * side
    row = (to // lanes) * (half * rows) + channel * rows + to % rows
    held = (channel >= 0) & (channel < half) & (row == at)
    return held.astype(jnp.bfloat16)


def ref_order(lanes, rows):
    at, to = iota((lanes, lanes), 0), iota((lanes, lanes), 1)
    k, g, h = to // (GROUPS * rows), (to // rows) % GROUPS, to % rows
    return ((g * (lanes // (GROUPS * rows)) + k) * rows + h == at).astype(jnp.bfloat16)


def turned_half(half_ref, pick, order):
    views, half, rows, width = half_ref.shape
    lanes = 2 * half * rows
    block = half_ref[...].reshape(views * half * rows, width)
    columns = dot_nt(pick, block).astype(jnp.bfloat16)
    return [dot(columns[:, i : i + lanes], order) for i in range(0, columns.shape[1], lanes)]


def turned_ref(ref_ref, pick):
    channels, rows, width = ref_ref.shape
    lanes = channels * rows
    columns = dot_nt(pick, ref_ref[...].reshape(lanes, width)).astype(jnp.bfloat16)
    return dot(columns, ref_order(lanes, rows))


def edge_start(role, width, count):
    return jnp.where(role == 0, width - count, 0)


def stacked(pair, lanes):
    return jnp.concatenate([pair[:, 0:lanes], pair[:, lanes:]], axis=0)


def pack_own_body(*refs):
    count = (len(refs) - 5) // 2
    sources, targets = refs[:count], refs[count : 2 * count]
    part_ref, pick_ref, own_order_ref, other_order_ref, sems = refs[2 * count :]
    copies = [
        pltpu.make_async_copy(source, target, sems.at[i])
        for i, (source, target) in enumerate(zip(sources, targets))
    ]
    for copy in copies:
        copy.start()
    own_ref, ref_ref = targets[:2]
    views, half, rows, width = own_ref.shape
    lanes = part_ref.shape[1]
    role, order, *_ = position()
    pick_ref[...] = columns_of(LEAD, width, edge_start(role, width, LEAD))
    own_order_ref[...] = lane_order(half, rows, order)
    other_order_ref[...] = lane_order(half, rows, 1 - order)
    few = columns_of(EDGE, width, edge_start(role, width, EDGE))
    copies[0].wait()
    for i, pair in enumerate(turned_half(own_ref, pick_ref[...], own_order_ref[...])):
        at = 2 * i * LEAD
        part_ref[at : at + 2 * LEAD] = stacked(pair, lanes).astype(jnp.bfloat16)
    for copy in copies[1:]:
        copy.wait()
    part_ref[views * LEAD :] = turned_ref(ref_ref, few).astype(jnp.bfloat16)


def pack_other_body(part_ref, pick_ref, other_order_ref, other_ref, packet_ref):
    views = other_ref.shape[0]
    lanes = packet_ref.shape[1]
    for i, pair in enumerate(turned_half(other_ref, pick_ref[...], other_order_ref[...])):
        at = 2 * i * LEAD
        both = part_ref[at : at + 2 * LEAD].astype(jnp.float32) + stacked(pair, lanes)
        packet_ref[at : at + 2 * LEAD] = both.astype(jnp.bfloat16)
    packet_ref[views * LEAD :] = part_ref[views * LEAD :]


def lane_table(values_ref, rows, lane):
    which = lane // rows % GROUPS
    table = jnp.zeros(lane.shape, jnp.float32)
    for o in range(GROUPS):
        table = jnp.where(which == o, values_ref[o], table)
    return table


def base_blocks(taps_ref, which, rows, apart):
    block = GROUPS * rows
    slots = 128 // (4 * rows)
    at, lane = iota((3 * GROUPS, 128), 0), iota((3 * GROUPS, 128), 1)
    if apart:
        spreads = [
            (lane // (slots * rows) + t * 4 == at % GROUPS)
            & ((lane // rows) % slots == at // GROUPS)
            for t in range(2)
        ]
    else:
        spreads = [lane // rows == at]
    stretch = (iota((block, GROUPS), 0) // rows == iota((block, GROUPS), 1)).astype(jnp.bfloat16)
    gap = iota((block, 128), 0) % rows - iota((block, 128), 1) % rows + 1
    found = []
    for spread in spreads:
        wide = dot(taps_ref[which], spread.astype(jnp.bfloat16)).astype(jnp.bfloat16)
        for e in range(3):
            base = jnp.zeros((block, 128), jnp.float32)
            for b in range(3):
                at = (b * 3 + e) * GROUPS
                base = jnp.where(gap == b, dot(stretch, wide[at : at + GROUPS]), base)
            found.append(base)
    return [found[i : i + 3] for i in range(0, len(found), 3)]


def band_rows(e, j, block):
    per_tile = 128 // block
    whole = 2 * per_tile
    if j < whole:
        return (e * whole + j) * block
    return (3 * whole + 2 * e + j - whole) * block


def build_band_one(taps_ref, band_ref, rest_ref, rows):
    block = GROUPS * rows
    lane = iota((block, 128), 1)
    per_tile = 128 // block
    zero = jnp.zeros((block, 128), jnp.bfloat16)
    (bases,) = base_blocks(taps_ref, 0, rows, False)
    for e, base in enumerate(bases):
        low_parts, high_parts = [], []
        for turn in range(per_tile):
            moved = pltpu.roll(base, turn * block, 1) if turn else base
            high_parts.append(jnp.where(lane >= turn * block, moved, 0.0).astype(jnp.bfloat16))
            low_parts.append(jnp.where(lane < turn * block, moved, 0.0).astype(jnp.bfloat16))
        for j in range(2 * per_tile + 2):
            first, turn = (j - 2) // per_tile, (j - 2) % per_tile
            at = band_rows(e, j, block)
            for t in range(2):
                part = zero
                if t == first:
                    part = high_parts[turn]
                elif t == first + 1 and turn > per_tile - 3:
                    part = low_parts[turn]
                band_ref[at : at + block, t * 128 : (t + 1) * 128] = part
                if t == 0 and j < per_tile:
                    rest_ref[(e * per_tile + j) * block : (e * per_tile + j + 1) * block] = part
    for j in range(2):
        at = (3 * (2 * per_tile + 2) + j) * block
        band_ref[at : at + block] = jnp.zeros((block, 256), jnp.bfloat16)


def build_band_two(taps_ref, band_ref, rows):
    block = GROUPS * rows
    per_tile = 128 // block
    slots = 2 * per_tile
    plane = (iota((block, 128), 1) // rows) % slots
    for t, bases in enumerate(base_blocks(taps_ref, 1, rows, True)):
        for e, base in enumerate(bases):
            for j in range(slots + 2):
                turn = (j - 2) * rows % 128
                moved = pltpu.roll(base, turn, 1) if turn else base
                held = (plane >= j - 2) & (plane <= j)
                at = band_rows(e, j, block)
                band_ref[at : at + block, t * 128 : (t + 1) * 128] = jnp.where(
                    held, moved, 0.0
                ).astype(jnp.bfloat16)
    for j in range(2):
        at = (3 * (slots + 2) + j) * block
        band_ref[at : at + block] = jnp.zeros((block, 256), jnp.bfloat16)


def build_tables(planes, rows, inner, bias_one, bias_two, view_head, ends, table_ref, spread_ref, perm_ref):
    block = GROUPS * rows
    out_lanes = planes * block
    span = table_ref.shape[1]
    is_first_plane, is_last_plane = ends
    at = iota((1, span), 1)
    plane = at // block
    outside = ((plane < 2) & is_first_plane) | ((plane >= planes + 2) & is_last_plane)
    table_ref[0:1] = jnp.where(outside, 0.0, 1.0 / inner)
    outside = ((plane == 0) & is_first_plane) | ((plane == planes + 1) & is_last_plane)
    table_ref[1:2] = jnp.where(outside, FAR, lane_table(bias_one, rows, at))
    table_ref[2:3] = lane_table(bias_two, planes * rows, at)
    table_ref[3:4] = lane_table(view_head, planes * rows, at)
    row, lane = iota(spread_ref.shape, 0), iota(spread_ref.shape, 1)
    same = (row // rows % planes == lane // block) & (row % rows == lane % rows)
    spread_ref[...] = same.astype(jnp.bfloat16)
    to = iota(perm_ref.shape, 0)
    g, j, h = to // (planes * rows), (to // rows) % planes, to % rows
    perm = (j * GROUPS + g) * rows + h == iota(perm_ref.shape, 1)
    perm_ref[...] = perm.astype(jnp.bfloat16)


def fill(pieces, near, src, wide, match, table_ref, block):
    shared = lax.axis_size("plane") == 2
    last = len(near) - 2
    for at, src_at, wide_at, count in pieces:
        quarter = iota((count, 128), 1) // block
        lower, middle, even = quarter < 2, (quarter == 1) | (quarter == 2), quarter % 2 == 0
        here = wide[wide_at : wide_at + count]
        ready = {}

        def product(j):
            if shared and j >= last:
                j -= last
            if j not in ready:
                ready[j] = src[pl.ds(src_at - near[j], count)] * here
            return ready[j]

        tiles = match.shape[1] // 128
        for q in (0, *reversed(range(1, tiles))):
            a, c, b, d = (product(q * 4 + k) for k in range(4))
            x = jnp.where(lower, a, b) + pltpu.roll(jnp.where(lower, b, a), 64, 1)
            z = jnp.where(middle, c, d) + pltpu.roll(jnp.where(middle, d, c), 64, 1)
            y = jnp.where(even, x, z) + pltpu.roll(jnp.where(even, z, x), 96, 1)
            y = y * table_ref[0:1, q * 128 : (q + 1) * 128]
            y = y.astype(jnp.bfloat16).astype(jnp.float32)
            match[at : at + count, q * 128 : (q + 1) * 128] = y


def three_taps(volume, low, high, out_lanes):
    tile = volume.shape[1] - out_lanes
    parts = [volume[low + e : high + e] for e in range(3)]
    tails = [part[:, out_lanes:] for part in parts]
    near = iota((high - low, tile), 1) < tile // 2
    paired = jnp.where(near, tails[0], pltpu.roll(tails[1], tile // 2, 1))
    sides = [part[:, 0:out_lanes] for part in parts] + [paired, tails[2]]
    wide = jnp.concatenate([side.astype(jnp.bfloat16) for side in sides], axis=1)
    return wide, jnp.concatenate([tail.astype(jnp.bfloat16) for tail in tails], axis=1)


def convolve_first(low, high, planes, block, match, first, table_ref, band_one, rest_ref):
    out_lanes = planes * block
    wide, tails = three_taps(match, low, high, out_lanes)
    raw = dot(wide, band_one[...])
    main = jnp.maximum(raw + table_ref[1:2, 0:out_lanes], 0.0)
    raw = dot(tails, rest_ref[...])
    rest = jnp.maximum(raw + table_ref[1:2, out_lanes:], 0.0)

    def store():
        first[low:high, 0:out_lanes] = main
        first[low:high, out_lanes:] = rest

    return store


def convolve_second(low, high, planes, block, first, table_ref, band_two):
    out_lanes = planes * block
    wide, _ = three_taps(first, low, high, out_lanes)
    second = dot(wide, band_two[...])
    second = jnp.maximum(second + table_ref[2:3, 0:out_lanes], 0.0) * table_ref[3:4, 0:out_lanes]
    half = out_lanes // 2
    return second[:, 0:half] + second[:, half:]


def weights(second, spread_ref):
    upper = second.astype(jnp.bfloat16)
    under = (second - upper.astype(jnp.float32)).astype(jnp.bfloat16)
    score = dot(jnp.concatenate([upper, under], axis=1), spread_ref[...])
    return jax.nn.sigmoid(score)


def first_stage(
    views, tall, planes, block, filled, mend, match, first, table_ref, band_one, rest_ref
):
    store = None
    for v in range(views + 1):
        if v < views:
            filled(v)
        if store is not None:
            store()
            mend((v - 1) * tall)
        if v < views:
            low, high = v * tall, (v + 1) * tall
            store = convolve_first(
                low, high, planes, block, match, first, table_ref, band_one, rest_ref
            )


def second_stage(views, tall, planes, block, match, first, table_ref, band_two, spread_ref):
    out_lanes = planes * block
    total = weighted = 0.0
    steps = range(0, views, BATCH)
    seconds = [
        convolve_second(at * tall, (at + BATCH) * tall, planes, block, first, table_ref, band_two)
        for at in steps
    ]
    for at, second in zip(steps, seconds):
        weight = weights(second, spread_ref)
        for v in range(BATCH):
            part = weight[v * tall : (v + 1) * tall]
            row = (at + v) * tall + 2
            total = total + part
            weighted = weighted + part * match[row : row + tall, 2 * block : 2 * block + out_lanes]
    return weighted / total


def pack_shifts(shifts, before, after, word_ref):
    for row, ref in enumerate((before, shifts, after)):
        word = ref[0:1]
        for v in range(1, ref.shape[0]):
            word = word | (ref[v : v + 1] << (8 * v))
        word_ref[row : row + 1, 0 : word.shape[1]] = word


def read_shifts(views, planes, word_ref):
    at = [(0, planes - 2), (0, planes - 1)] + [(1, d) for d in range(planes)] + [(2, 0), (2, 1)]
    words = [word_ref[row, d] for row, d in at]
    if lax.axis_size("plane") == 2:
        _, _, _, _, is_first_plane, _ = position()
        for k in range(2):
            inside = jnp.where(is_first_plane, words[planes + 2 + k], words[k])
            words[k] = words[planes + 2 + k] = inside
    return [[(word >> (8 * v)) & 255 for word in words] for v in range(views)]


def inner_body(
    shifts,
    before,
    after,
    bias_one,
    bias_two,
    view_head,
    own_ref,
    other_ref,
    ref_ref,
    own_order_ref,
    other_order_ref,
    taps_ref,
    cols_ref,
    ref_cols_ref,
    word_ref,
    table_ref,
    spread_ref,
    perm_ref,
    band_one,
    rest_ref,
    band_two,
    match,
    first,
    src,
    wide,
):
    views, half, rows, width = own_ref.shape
    planes = shifts.shape[1]
    lanes = 2 * half * rows
    inner = 2 * half // GROUPS
    block = GROUPS * rows
    _, _, _, _, *ends = position()
    pick = columns_of(width, width, 0)
    none = jnp.zeros((8, lanes), jnp.float32)
    columns = turned_ref(ref_ref, pick)
    ref_cols_ref[...] = columns.astype(jnp.bfloat16)
    wide[0:width] = columns
    wide[width:] = none
    pairs = zip(
        turned_half(own_ref, pick, own_order_ref[...]),
        turned_half(other_ref, pick, other_order_ref[...]),
    )
    for i, (low, high) in enumerate(pairs):
        columns = low + high
        for k in range(2):
            v = 2 * i + k
            part = columns[:, k * lanes : (k + 1) * lanes]
            cols_ref[v] = part.astype(jnp.bfloat16)
            src[v, 0:8] = none
            src[v, 8 : 8 + width] = part
            src[v, 8 + width :] = none
    build_tables(
        planes, rows, inner, bias_one, bias_two, view_head, ends, table_ref, spread_ref, perm_ref
    )
    build_band_one(taps_ref, band_one, rest_ref, rows)
    build_band_two(taps_ref, band_two, rows)
    pack_shifts(shifts, before, after, word_ref)
    near = read_shifts(views, planes, word_ref)
    out_rows = width - MAX_SHIFT
    tall = out_rows + 8
    base = MAX_SHIFT - 2

    def filled(v):
        pieces = [
            (v * tall + r, 8 + base + r, base + r, min(48, tall - r)) for r in range(0, tall, 48)
        ]
        fill(pieces, near[v], src.at[v], wide, match, table_ref, block)

    first_stage(
        views,
        tall,
        planes,
        block,
        filled,
        lambda row: None,
        match,
        first,
        table_ref,
        band_one,
        rest_ref,
    )
    for ref in (match, first):
        ref[views * tall :] = jnp.zeros((8, match.shape[1]), jnp.float32)


def late_body(match, first, table_ref, spread_ref, band_two, late_ref):
    out_rows, out_lanes = late_ref.shape
    block = (match.shape[1] - out_lanes) // 4
    views = match.shape[0] // (out_rows + 8)
    joined = second_stage(
        views, out_rows + 8, out_lanes // block, block, match, first, table_ref, band_two, spread_ref
    )
    late_ref[...] = joined[0:out_rows].astype(jnp.bfloat16)


def outer_body(
    cols_ref,
    ref_cols_ref,
    word_ref,
    table_ref,
    spread_ref,
    perm_ref,
    band_one,
    rest_ref,
    band_two,
    late_ref,
    got_ref,
    swapped_ref,
    out_ref,
    src,
    wide,
    match,
    first,
    joined,
    buffer,
    sems,
):
    views, width, lanes = cols_ref.shape
    groups, planes, rows, _ = out_ref.shape
    block = groups * rows
    _, order, is_first_tile, is_last_tile, *_ = position()

    near = read_shifts(views, planes, word_ref)
    left = jnp.where(order == 0, got_ref[...], swapped_ref[...])
    left = jnp.where(is_first_tile, jnp.zeros_like(left), left)
    right = jnp.where(order == 0, swapped_ref[...], got_ref[...])
    for v in range(0, views, 2):
        at = v * LEAD
        pair = left[at : at + 2 * LEAD].astype(jnp.float32)
        ends = right[at : at + LEAD + 24].astype(jnp.float32)
        for k in range(2):
            src[v + k, 0:LEAD] = pair[k * LEAD : (k + 1) * LEAD]
            src[v + k, LEAD : LEAD + width] = cols_ref[v + k].astype(jnp.float32)
            src[v + k, LEAD + width :] = ends[k * LEAD : k * LEAD + EDGE]
    wide[0:EDGE] = left[views * LEAD :].astype(jnp.float32)
    wide[EDGE : EDGE + width] = ref_cols_ref[...].astype(jnp.float32)
    wide[EDGE + width :] = jnp.where(is_last_tile, 0.0, right[views * LEAD :].astype(jnp.float32))
    main = MAX_SHIFT + 8
    tall = main + 8
    none = jnp.zeros((1, match.shape[1]), jnp.float32)

    def filled(v):
        at = v * tall
        pieces = [
            (at + r, LEAD - 2 + r, EDGE - 2 + r, min(48, main - r)) for r in range(0, main, 48)
        ]
        pieces += [(at + main, LEAD + width - 4, EDGE + width - 4, 8)]
        fill(pieces, near[v], src.at[v], wide, match, table_ref, block)

    def mend(row):
        for at, at_end in ((row, is_first_tile), (row + main + 3, is_last_tile)):
            first[at : at + 1] = jnp.where(at_end, none, first[at : at + 1])

    first_stage(
        views, tall, planes, block, filled, mend, match, first, table_ref, band_one, rest_ref
    )
    part = second_stage(
        views, tall, planes, block, match, first, table_ref, band_two, spread_ref
    )
    joined[0:MAX_SHIFT] = part[0:MAX_SHIFT]
    joined[MAX_SHIFT:] = late_ref[...].astype(jnp.float32)
    joined[MAX_SHIFT : MAX_SHIFT + 2] = part[MAX_SHIFT : MAX_SHIFT + 2]
    joined[width - 2 :] = part[main : main + 2]
    copies = []
    for half in range(2):
        at = half * (groups // 2)
        span = pl.ds(at, groups // 2)
        chosen = perm_ref[at * planes * rows : (at + groups // 2) * planes * rows]
        turned = dot_nt(chosen, joined[...].astype(jnp.bfloat16)).astype(jnp.bfloat16)
        buffer[at : at + groups // 2] = turned.reshape(groups // 2, planes, rows, width)
        copy = pltpu.make_async_copy(buffer.at[span], out_ref.at[span], sems.at[half])
        copy.start()
        copies.append(copy)
    for copy in copies:
        copy.wait()


def whole(memory):
    return pl.BlockSpec(memory_space=memory)


def limit(mebibytes):
    return pltpu.CompilerParams(vmem_limit_bytes=mebibytes * 1024 * 1024)


def swap_planes(value):
    return lax.ppermute(value, "plane", [(0, 1), (1, 0)])


def per_device(ref_feat, src_feat, shifts, conv_one, bias_one, conv_two, bias_two, view_head):
    views, _, rows, width = src_feat.shape
    planes = shifts.shape[1]
    lanes = ref_feat.shape[0] * rows
    tiles, sides = lax.axis_size("tile"), lax.axis_size("plane")
    bf16, f32 = jnp.bfloat16, jnp.float32
    vmem = pltpu.VMEM
    shape = jax.ShapeDtypeStruct
    if sides == 2:
        own, other = src_feat, swap_planes(src_feat)
    else:
        full = lax.all_gather(src_feat, "plane", axis=1, tiled=True)
        half = full.shape[1] // 2
        own, other = full[:, :half], full[:, half:]

    packet_shape = shape((views * LEAD + EDGE, lanes), bf16)
    order_shape = shape((lanes, 2 * lanes), bf16)
    staged = (own, ref_feat, shifts, bias_one, bias_two, view_head)
    *staged, part, pick, own_order, other_order = pl.pallas_call(
        pack_own_body,
        out_shape=[shape(x.shape, x.dtype) for x in staged]
        + [packet_shape, shape((LEAD, width), bf16), order_shape, order_shape],
        in_specs=[whole(pltpu.HBM)] * len(staged),
        out_specs=[whole(vmem)] * (len(staged) + 4),
        scratch_shapes=[pltpu.SemaphoreType.DMA((len(staged),))],
        compiler_params=limit(8),
        name="pack_own",
    )(*(pltpu.with_memory_space_constraint(x, pltpu.HBM) for x in staged))
    own, ref_feat, shifts, bias_one, bias_two, view_head = staged
    packet = pl.pallas_call(
        pack_other_body,
        out_shape=packet_shape,
        in_specs=[whole(vmem)] * 4,
        out_specs=whole(vmem),
        compiler_params=limit(8),
        name="pack_other",
    )(part, pick, other_order, other)

    pairs = [(sides * i, sides * (i + 1)) for i in range(tiles - 1)]
    pairs += [(sides * (i + 1) + 1, sides * i + 1) for i in range(tiles - 1)]
    pairs += [(sides * (tiles - 1), sides * (tiles - 1) + 1), (1, 0)]
    got = lax.ppermute(packet, ("tile", "plane"), pairs)

    own, other, shifts, conv_one, conv_two, packet = lax.optimization_barrier(
        (own, other, shifts, conv_one, conv_two, packet)
    )
    if sides == 2:
        before = after = swap_planes(shifts)
    else:
        before = lax.ppermute(shifts, "plane", [(i, i + 1) for i in range(sides - 1)])
        after = lax.ppermute(shifts, "plane", [(i + 1, i) for i in range(sides - 1)])

    def taps(kernel):
        flipped = jnp.flip(kernel, axis=2)
        return jnp.transpose(flipped, (3, 4, 1, 2, 0)).reshape(9 * GROUPS, 3 * GROUPS)

    both_taps = jnp.stack([taps(conv_one), taps(conv_two)])
    span = (planes + 4) * GROUPS * rows
    out_lanes = planes * GROUPS * rows
    late_rows = width - MAX_SHIFT
    high = views * (late_rows + 8) + 8
    *inner, match, first = pl.pallas_call(
        inner_body,
        out_shape=[
            shape((views, width, lanes), bf16),
            shape((width, lanes), bf16),
            shape((8, 128), jnp.int32),
            shape((8, span), f32),
            shape((256, out_lanes), bf16),
            shape((out_lanes, out_lanes), bf16),
            shape((4 * out_lanes, out_lanes), bf16),
            shape((3 * (span - out_lanes), span - out_lanes), bf16),
            shape((4 * out_lanes, out_lanes), bf16),
            shape((high, span), f32),
            shape((high, span), f32),
        ],
        in_specs=[whole(vmem)] * 12,
        out_specs=[whole(vmem)] * 11,
        scratch_shapes=[
            pltpu.VMEM((views, width + 16, lanes), f32),
            pltpu.VMEM((width + 8, lanes), f32),
        ],
        compiler_params=limit(24),
        cost_estimate=pl.CostEstimate(
            flops=3 * 10**9, bytes_accessed=10**6, transcendentals=10**5
        ),
        name="inner_columns",
    )(
        shifts,
        before,
        after,
        bias_one,
        bias_two,
        view_head,
        own,
        other,
        ref_feat,
        own_order,
        other_order,
        both_taps,
    )
    got, match, first, *inner = lax.optimization_barrier((got, match, first, *inner))
    if sides == 2:
        swapped = swap_planes(got)
    else:
        both = lax.all_gather(got, "plane", axis=0)
        got, swapped = both[0], both[1]
    late = pl.pallas_call(
        late_body,
        out_shape=shape((late_rows, out_lanes), bf16),
        in_specs=[whole(vmem)] * 5,
        out_specs=whole(vmem),
        compiler_params=limit(24),
        cost_estimate=pl.CostEstimate(
            flops=2 * 10**9, bytes_accessed=10**6, transcendentals=10**5
        ),
        name="late_columns",
    )(match, first, inner[3], inner[4], inner[8])
    high = views * (MAX_SHIFT + 16) + 8
    return pl.pallas_call(
        outer_body,
        out_shape=shape((GROUPS, planes, rows, width), bf16),
        in_specs=[whole(vmem)] * 12,
        out_specs=whole(pltpu.HBM),
        scratch_shapes=[
            pltpu.VMEM((views, LEAD + width + EDGE, lanes), f32),
            pltpu.VMEM((EDGE + width + EDGE, lanes), f32),
            pltpu.VMEM((high, span), f32),
            pltpu.VMEM((high, span), f32),
            pltpu.VMEM((width, out_lanes), f32),
            pltpu.VMEM((GROUPS, planes, rows, width), bf16),
            pltpu.SemaphoreType.DMA((2,)),
        ],
        compiler_params=limit(24),
        name="outer_columns",
    )(*inner, late, got, swapped)


def solution(mesh):
    placed = (
        P(None, None, "tile"),
        P(None, "plane", None, "tile"),
        P(None, "plane"),
        P(),
        P(),
        P(),
        P(),
        P(),
    )
    return jax.shard_map(
        per_device,
        mesh=mesh,
        in_specs=placed,
        out_specs=P(None, "plane", None, "tile"),
        check_vma=False,
    )
```

```python
import jax
import jax.numpy as jnp
from jax import lax
from jax.experimental import pallas as pl
from jax.experimental.pallas import tpu as pltpu
from jax.sharding import PartitionSpec as P

GROUPS = 8
MAX_SHIFT = 128
LEAD = MAX_SHIFT + 8
EDGE = 16
SPOT = 4
BATCH = 2
FAR = -3.0e38


def iota(shape, dim):
    return lax.broadcasted_iota(jnp.int32, shape, dim)


def dot(left, right):
    return jnp.dot(left, right, preferred_element_type=jnp.float32)


def dot_nt(left, right):
    return lax.dot_general(
        left, right, (((1,), (1,)), ((), ())), preferred_element_type=jnp.float32
    )


def position():
    tile, plane = lax.axis_index("tile"), lax.axis_index("plane")
    tiles, sides = lax.axis_size("tile"), lax.axis_size("plane")
    order = plane if sides == 2 else 0 * plane
    role = jnp.minimum(plane, 1)
    return role, order, tile == 0, tile == tiles - 1, plane == 0, plane == sides - 1


def columns_of(count, width, start):
    picked = iota((count, width), 0) + start == iota((count, width), 1)
    return picked.astype(jnp.bfloat16)


def on_spot(count, width):
    row = iota((count, width), 0)
    return (row >= SPOT) & (row < SPOT + 2)


def lane_order(half, rows, side):
    lanes = 2 * half * rows
    inner = 2 * half // GROUPS
    at, to = iota((lanes, 2 * lanes), 0), iota((lanes, 2 * lanes), 1)
    k, g = (to // (GROUPS * rows)) % inner, (to // rows) % GROUPS
    channel = g * inner + k - half * side
    row = (to // lanes) * (half * rows) + channel * rows + to % rows
    held = (channel >= 0) & (channel < half) & (row == at)
    return held.astype(jnp.bfloat16)


def ref_order(lanes, rows):
    at, to = iota((lanes, lanes), 0), iota((lanes, lanes), 1)
    k, g, h = to // (GROUPS * rows), (to // rows) % GROUPS, to % rows
    return ((g * (lanes // (GROUPS * rows)) + k) * rows + h == at).astype(jnp.bfloat16)


def turned_half(half_ref, pick, order):
    views, half, rows, width = half_ref.shape
    lanes = 2 * half * rows
    block = half_ref[...].reshape(views * half * rows, width)
    columns = dot_nt(pick, block).astype(jnp.bfloat16)
    return [dot(columns[:, i : i + lanes], order) for i in range(0, columns.shape[1], lanes)]


def turned_ref(ref_ref, pick):
    channels, rows, width = ref_ref.shape
    lanes = channels * rows
    columns = dot_nt(pick, ref_ref[...].reshape(lanes, width)).astype(jnp.bfloat16)
    return dot(columns, ref_order(lanes, rows))


def edge_start(role, width, count):
    return jnp.where(role == 0, width - count, 0)


def stacked(pair, lanes):
    return jnp.concatenate([pair[:, 0:lanes], pair[:, lanes:]], axis=0)


def pack_own_body(*refs):
    count = (len(refs) - 5) // 2
    sources, targets = refs[:count], refs[count : 2 * count]
    part_ref, pick_ref, own_order_ref, other_order_ref, sems = refs[2 * count :]
    copies = [
        pltpu.make_async_copy(source, target, sems.at[i])
        for i, (source, target) in enumerate(zip(sources, targets))
    ]
    for copy in copies:
        copy.start()
    own_ref, ref_ref = targets[:2]
    views, half, rows, width = own_ref.shape
    lanes = part_ref.shape[1]
    role, order, *_ = position()
    pick = columns_of(LEAD, width, edge_start(role, width, LEAD))
    pick_ref[...] = jnp.where(on_spot(LEAD, width), 0.0, pick.astype(jnp.float32)).astype(jnp.bfloat16)
    own_order_ref[...] = lane_order(half, rows, order)
    other_order_ref[...] = lane_order(half, rows, 1 - order)
    few = columns_of(EDGE, width, edge_start(role, width, 2) - SPOT).astype(jnp.float32)
    few = jnp.where(on_spot(EDGE, width), few, 0.0).astype(jnp.bfloat16)
    copies[0].wait()
    for i, pair in enumerate(turned_half(own_ref, pick_ref[...], own_order_ref[...])):
        at = 2 * i * LEAD
        part_ref[at : at + 2 * LEAD] = stacked(pair, lanes).astype(jnp.bfloat16)
    for copy in copies[1:]:
        copy.wait()
    part_ref[0:EDGE] = part_ref[0:EDGE] + turned_ref(ref_ref, few).astype(jnp.bfloat16)


def pack_other_body(part_ref, pick_ref, other_order_ref, other_ref, packet_ref):
    lanes = packet_ref.shape[1]
    for i, pair in enumerate(turned_half(other_ref, pick_ref[...], other_order_ref[...])):
        at = 2 * i * LEAD
        both = part_ref[at : at + 2 * LEAD].astype(jnp.float32) + stacked(pair, lanes)
        packet_ref[at : at + 2 * LEAD] = both.astype(jnp.bfloat16)


def lane_table(values_ref, rows, lane):
    which = lane // rows % GROUPS
    table = jnp.zeros(lane.shape, jnp.float32)
    for o in range(GROUPS):
        table = jnp.where(which == o, values_ref[o], table)
    return table


def base_blocks(taps_ref, which, rows, apart):
    block = GROUPS * rows
    slots = 128 // (4 * rows)
    at, lane = iota((3 * GROUPS, 128), 0), iota((3 * GROUPS, 128), 1)
    if apart:
        spreads = [
            (lane // (slots * rows) + t * 4 == at % GROUPS)
            & ((lane // rows) % slots == at // GROUPS)
            for t in range(2)
        ]
    else:
        spreads = [lane // rows == at]
    stretch = (iota((block, GROUPS), 0) // rows == iota((block, GROUPS), 1)).astype(jnp.bfloat16)
    gap = iota((block, 128), 0) % rows - iota((block, 128), 1) % rows + 1
    found = []
    for spread in spreads:
        wide = dot(taps_ref[which], spread.astype(jnp.bfloat16)).astype(jnp.bfloat16)
        for e in range(3):
            base = jnp.zeros((block, 128), jnp.float32)
            for b in range(3):
                at = (b * 3 + e) * GROUPS
                base = jnp.where(gap == b, dot(stretch, wide[at : at + GROUPS]), base)
            found.append(base)
    return [found[i : i + 3] for i in range(0, len(found), 3)]


def band_rows(e, j, block):
    per_tile = 128 // block
    whole = 2 * per_tile
    if j < whole:
        return (e * whole + j) * block
    return (3 * whole + 2 * e + j - whole) * block


def build_band_one(taps_ref, band_ref, rest_ref, rows):
    block = GROUPS * rows
    lane = iota((block, 128), 1)
    per_tile = 128 // block
    zero = jnp.zeros((block, 128), jnp.bfloat16)
    (bases,) = base_blocks(taps_ref, 0, rows, False)
    for e, base in enumerate(bases):
        low_parts, high_parts = [], []
        for turn in range(per_tile):
            moved = pltpu.roll(base, turn * block, 1) if turn else base
            high_parts.append(jnp.where(lane >= turn * block, moved, 0.0).astype(jnp.bfloat16))
            low_parts.append(jnp.where(lane < turn * block, moved, 0.0).astype(jnp.bfloat16))
        for j in range(2 * per_tile + 2):
            first, turn = (j - 2) // per_tile, (j - 2) % per_tile
            at = band_rows(e, j, block)
            for t in range(2):
                part = zero
                if t == first:
                    part = high_parts[turn]
                elif t == first + 1 and turn > per_tile - 3:
                    part = low_parts[turn]
                band_ref[at : at + block, t * 128 : (t + 1) * 128] = part
                if t == 0 and j < per_tile:
                    rest_ref[(e * per_tile + j) * block : (e * per_tile + j + 1) * block] = part
    for j in range(2):
        at = (3 * (2 * per_tile + 2) + j) * block
        band_ref[at : at + block] = jnp.zeros((block, 256), jnp.bfloat16)


def build_band_two(taps_ref, band_ref, rows):
    block = GROUPS * rows
    per_tile = 128 // block
    slots = 2 * per_tile
    plane = (iota((block, 128), 1) // rows) % slots
    for t, bases in enumerate(base_blocks(taps_ref, 1, rows, True)):
        for e, base in enumerate(bases):
            for j in range(slots + 2):
                turn = (j - 2) * rows % 128
                moved = pltpu.roll(base, turn, 1) if turn else base
                held = (plane >= j - 2) & (plane <= j)
                at = band_rows(e, j, block)
                band_ref[at : at + block, t * 128 : (t + 1) * 128] = jnp.where(
                    held, moved, 0.0
                ).astype(jnp.bfloat16)
    for j in range(2):
        at = (3 * (slots + 2) + j) * block
        band_ref[at : at + block] = jnp.zeros((block, 256), jnp.bfloat16)


def build_tables(planes, rows, inner, bias_one, bias_two, view_head, ends, table_ref, spread_ref, perm_ref):
    block = GROUPS * rows
    out_lanes = planes * block
    span = table_ref.shape[1]
    is_first_plane, is_last_plane = ends
    at = iota((1, span), 1)
    plane = at // block
    outside = ((plane < 2) & is_first_plane) | ((plane >= planes + 2) & is_last_plane)
    table_ref[0:1] = jnp.where(outside, 0.0, 1.0 / inner)
    outside = ((plane == 0) & is_first_plane) | ((plane == planes + 1) & is_last_plane)
    table_ref[1:2] = jnp.where(outside, FAR, lane_table(bias_one, rows, at))
    table_ref[2:3] = lane_table(bias_two, planes * rows, at)
    table_ref[3:4] = lane_table(view_head, planes * rows, at)
    row, lane = iota(spread_ref.shape, 0), iota(spread_ref.shape, 1)
    same = (row // rows % planes == lane // block) & (row % rows == lane % rows)
    spread_ref[...] = same.astype(jnp.bfloat16)
    to = iota(perm_ref.shape, 0)
    g, j, h = to // (planes * rows), (to // rows) % planes, to % rows
    perm = (j * GROUPS + g) * rows + h == iota(perm_ref.shape, 1)
    perm_ref[...] = perm.astype(jnp.bfloat16)


def fill(pieces, near, src, wide, match, table_ref, block):
    shared = lax.axis_size("plane") == 2
    last = len(near) - 2
    for at, src_at, wide_at, count in pieces:
        quarter = iota((count, 128), 1) // block
        lower, middle, even = quarter < 2, (quarter == 1) | (quarter == 2), quarter % 2 == 0
        here = wide[wide_at : wide_at + count]
        ready = {}

        def product(j):
            if shared and j >= last:
                j -= last
            if j not in ready:
                ready[j] = src[pl.ds(src_at - near[j], count)] * here
            return ready[j]

        tiles = match.shape[1] // 128
        for q in (0, *reversed(range(1, tiles))):
            a, c, b, d = (product(q * 4 + k) for k in range(4))
            x = jnp.where(lower, a, b) + pltpu.roll(jnp.where(lower, b, a), 64, 1)
            z = jnp.where(middle, c, d) + pltpu.roll(jnp.where(middle, d, c), 64, 1)
            y = jnp.where(even, x, z) + pltpu.roll(jnp.where(even, z, x), 96, 1)
            y = y * table_ref[0:1, q * 128 : (q + 1) * 128]
            y = y.astype(jnp.bfloat16).astype(jnp.float32)
            match[at : at + count, q * 128 : (q + 1) * 128] = y


def three_taps(volume, low, high, out_lanes):
    tile = volume.shape[1] - out_lanes
    parts = [volume[low + e : high + e] for e in range(3)]
    tails = [part[:, out_lanes:] for part in parts]
    near = iota((high - low, tile), 1) < tile // 2
    paired = jnp.where(near, tails[0], pltpu.roll(tails[1], tile // 2, 1))
    sides = [part[:, 0:out_lanes] for part in parts] + [paired, tails[2]]
    wide = jnp.concatenate([side.astype(jnp.bfloat16) for side in sides], axis=1)
    return wide, jnp.concatenate([tail.astype(jnp.bfloat16) for tail in tails], axis=1)


def convolve_first(low, high, planes, block, match, first, table_ref, band_one, rest_ref):
    out_lanes = planes * block
    wide, tails = three_taps(match, low, high, out_lanes)
    raw = dot(wide, band_one[...])
    main = jnp.maximum(raw + table_ref[1:2, 0:out_lanes], 0.0)
    raw = dot(tails, rest_ref[...])
    rest = jnp.maximum(raw + table_ref[1:2, out_lanes:], 0.0)

    def store():
        first[low:high, 0:out_lanes] = main
        first[low:high, out_lanes:] = rest

    return store


def convolve_second(low, high, planes, block, first, table_ref, band_two):
    out_lanes = planes * block
    wide, _ = three_taps(first, low, high, out_lanes)
    second = dot(wide, band_two[...])
    second = jnp.maximum(second + table_ref[2:3, 0:out_lanes], 0.0) * table_ref[3:4, 0:out_lanes]
    half = out_lanes // 2
    return second[:, 0:half] + second[:, half:]


def weights(second, spread_ref):
    upper = second.astype(jnp.bfloat16)
    under = (second - upper.astype(jnp.float32)).astype(jnp.bfloat16)
    score = dot(jnp.concatenate([upper, under], axis=1), spread_ref[...])
    return jax.nn.sigmoid(score)


def first_stage(
    views, tall, planes, block, filled, mend, match, first, table_ref, band_one, rest_ref
):
    store = None
    for v in range(views + 1):
        if v < views:
            filled(v)
        if store is not None:
            store()
            mend((v - 1) * tall)
        if v < views:
            low, high = v * tall, (v + 1) * tall
            store = convolve_first(
                low, high, planes, block, match, first, table_ref, band_one, rest_ref
            )


def second_stage(views, tall, planes, block, match, first, table_ref, band_two, spread_ref):
    out_lanes = planes * block
    total = weighted = 0.0
    steps = range(0, views, BATCH)
    seconds = [
        convolve_second(at * tall, (at + BATCH) * tall, planes, block, first, table_ref, band_two)
        for at in steps
    ]
    for at, second in zip(steps, seconds):
        weight = weights(second, spread_ref)
        for v in range(BATCH):
            part = weight[v * tall : (v + 1) * tall]
            row = (at + v) * tall + 2
            total = total + part
            weighted = weighted + part * match[row : row + tall, 2 * block : 2 * block + out_lanes]
    return weighted / total


def pack_shifts(shifts, before, after, word_ref):
    for row, ref in enumerate((before, shifts, after)):
        word = ref[0:1]
        for v in range(1, ref.shape[0]):
            word = word | (ref[v : v + 1] << (8 * v))
        word_ref[row : row + 1, 0 : word.shape[1]] = word


def read_shifts(views, planes, word_ref):
    at = [(0, planes - 2), (0, planes - 1)] + [(1, d) for d in range(planes)] + [(2, 0), (2, 1)]
    words = [word_ref[row, d] for row, d in at]
    if lax.axis_size("plane") == 2:
        _, _, _, _, is_first_plane, _ = position()
        for k in range(2):
            inside = jnp.where(is_first_plane, words[planes + 2 + k], words[k])
            words[k] = words[planes + 2 + k] = inside
    return [[(word >> (8 * v)) & 255 for word in words] for v in range(views)]


def inner_body(
    shifts,
    before,
    after,
    bias_one,
    bias_two,
    view_head,
    own_ref,
    other_ref,
    ref_ref,
    own_order_ref,
    other_order_ref,
    taps_ref,
    cols_ref,
    ref_cols_ref,
    word_ref,
    table_ref,
    spread_ref,
    perm_ref,
    band_one,
    rest_ref,
    band_two,
    match,
    first,
    src,
    wide,
):
    views, half, rows, width = own_ref.shape
    planes = shifts.shape[1]
    lanes = 2 * half * rows
    inner = 2 * half // GROUPS
    block = GROUPS * rows
    _, _, _, _, *ends = position()
    pick = columns_of(width, width, 0)
    none = jnp.zeros((8, lanes), jnp.float32)
    columns = turned_ref(ref_ref, pick)
    ref_cols_ref[...] = columns.astype(jnp.bfloat16)
    wide[0:width] = columns
    wide[width:] = none
    pairs = zip(
        turned_half(own_ref, pick, own_order_ref[...]),
        turned_half(other_ref, pick, other_order_ref[...]),
    )
    for i, (low, high) in enumerate(pairs):
        columns = low + high
        for k in range(2):
            v = 2 * i + k
            part = columns[:, k * lanes : (k + 1) * lanes]
            cols_ref[v] = part.astype(jnp.bfloat16)
            src[v, 0:8] = none
            src[v, 8 : 8 + width] = part
            src[v, 8 + width :] = none
    build_tables(
        planes, rows, inner, bias_one, bias_two, view_head, ends, table_ref, spread_ref, perm_ref
    )
    build_band_one(taps_ref, band_one, rest_ref, rows)
    build_band_two(taps_ref, band_two, rows)
    pack_shifts(shifts, before, after, word_ref)
    near = read_shifts(views, planes, word_ref)
    out_rows = width - MAX_SHIFT
    tall = out_rows + 8
    base = MAX_SHIFT - 2

    def filled(v):
        pieces = [
            (v * tall + r, 8 + base + r, base + r, min(48, tall - r)) for r in range(0, tall, 48)
        ]
        fill(pieces, near[v], src.at[v], wide, match, table_ref, block)

    first_stage(
        views,
        tall,
        planes,
        block,
        filled,
        lambda row: None,
        match,
        first,
        table_ref,
        band_one,
        rest_ref,
    )
    for ref in (match, first):
        ref[views * tall :] = jnp.zeros((8, match.shape[1]), jnp.float32)


def late_body(match, first, table_ref, spread_ref, band_two, late_ref):
    out_rows, out_lanes = late_ref.shape
    block = (match.shape[1] - out_lanes) // 4
    views = match.shape[0] // (out_rows + 8)
    joined = second_stage(
        views, out_rows + 8, out_lanes // block, block, match, first, table_ref, band_two, spread_ref
    )
    late_ref[...] = joined[0:out_rows].astype(jnp.bfloat16)


def outer_body(
    cols_ref,
    ref_cols_ref,
    word_ref,
    table_ref,
    spread_ref,
    perm_ref,
    band_one,
    rest_ref,
    band_two,
    late_ref,
    got_ref,
    swapped_ref,
    out_ref,
    src,
    wide,
    match,
    first,
    joined,
    buffer,
    sems,
):
    views, width, lanes = cols_ref.shape
    groups, planes, rows, _ = out_ref.shape
    block = groups * rows
    _, order, is_first_tile, is_last_tile, *_ = position()

    near = read_shifts(views, planes, word_ref)
    left = jnp.where(order == 0, got_ref[...], swapped_ref[...])
    left = jnp.where(is_first_tile, jnp.zeros_like(left), left)
    right = jnp.where(order == 0, swapped_ref[...], got_ref[...])
    for v in range(0, views, 2):
        at = v * LEAD
        pair = left[at : at + 2 * LEAD].astype(jnp.float32)
        ends = right[at : at + LEAD + 24].astype(jnp.float32)
        for k in range(2):
            src[v + k, 0:LEAD] = pair[k * LEAD : (k + 1) * LEAD]
            src[v + k, LEAD : LEAD + width] = cols_ref[v + k].astype(jnp.float32)
            src[v + k, LEAD + width :] = ends[k * LEAD : k * LEAD + EDGE]
    wide[EDGE - 8 : EDGE] = pltpu.roll(left[0:EDGE].astype(jnp.float32)[0:8], 6 - SPOT, 0)
    wide[EDGE : EDGE + width] = ref_cols_ref[...].astype(jnp.float32)
    ends = pltpu.roll(right[0:EDGE].astype(jnp.float32)[0:8], 8 - SPOT, 0)
    wide[EDGE + width : EDGE + width + 8] = jnp.where(is_last_tile, 0.0, ends)
    main = MAX_SHIFT + 8
    tall = main + 8
    none = jnp.zeros((1, match.shape[1]), jnp.float32)

    def filled(v):
        at = v * tall
        pieces = [
            (at + r, LEAD - 2 + r, EDGE - 2 + r, min(48, main - r)) for r in range(0, main, 48)
        ]
        pieces += [(at + main, LEAD + width - 4, EDGE + width - 4, 8)]
        fill(pieces, near[v], src.at[v], wide, match, table_ref, block)

    def mend(row):
        for at, at_end in ((row, is_first_tile), (row + main + 3, is_last_tile)):
            first[at : at + 1] = jnp.where(at_end, none, first[at : at + 1])

    first_stage(
        views, tall, planes, block, filled, mend, match, first, table_ref, band_one, rest_ref
    )
    part = second_stage(
        views, tall, planes, block, match, first, table_ref, band_two, spread_ref
    )
    joined[0:MAX_SHIFT] = part[0:MAX_SHIFT]
    joined[MAX_SHIFT:] = late_ref[...].astype(jnp.float32)
    joined[MAX_SHIFT : MAX_SHIFT + 2] = part[MAX_SHIFT : MAX_SHIFT + 2]
    joined[width - 2 :] = part[main : main + 2]
    copies = []
    for half in range(2):
        at = half * (groups // 2)
        span = pl.ds(at, groups // 2)
        chosen = perm_ref[at * planes * rows : (at + groups // 2) * planes * rows]
        turned = dot_nt(chosen, joined[...].astype(jnp.bfloat16)).astype(jnp.bfloat16)
        buffer[at : at + groups // 2] = turned.reshape(groups // 2, planes, rows, width)
        copy = pltpu.make_async_copy(buffer.at[span], out_ref.at[span], sems.at[half])
        copy.start()
        copies.append(copy)
    for copy in copies:
        copy.wait()


def whole(memory):
    return pl.BlockSpec(memory_space=memory)


def limit(mebibytes):
    return pltpu.CompilerParams(vmem_limit_bytes=mebibytes * 1024 * 1024)


def swap_planes(value):
    return lax.ppermute(value, "plane", [(0, 1), (1, 0)])


def per_device(ref_feat, src_feat, shifts, conv_one, bias_one, conv_two, bias_two, view_head):
    views, _, rows, width = src_feat.shape
    planes = shifts.shape[1]
    lanes = ref_feat.shape[0] * rows
    tiles, sides = lax.axis_size("tile"), lax.axis_size("plane")
    bf16, f32 = jnp.bfloat16, jnp.float32
    vmem = pltpu.VMEM
    shape = jax.ShapeDtypeStruct
    if sides == 2:
        own, other = src_feat, swap_planes(src_feat)
    else:
        full = lax.all_gather(src_feat, "plane", axis=1, tiled=True)
        half = full.shape[1] // 2
        own, other = full[:, :half], full[:, half:]

    packet_shape = shape((views * LEAD, lanes), bf16)
    order_shape = shape((lanes, 2 * lanes), bf16)
    staged = (own, ref_feat, shifts, bias_one, bias_two, view_head)
    *staged, part, pick, own_order, other_order = pl.pallas_call(
        pack_own_body,
        out_shape=[shape(x.shape, x.dtype) for x in staged]
        + [packet_shape, shape((LEAD, width), bf16), order_shape, order_shape],
        in_specs=[whole(pltpu.HBM)] * len(staged),
        out_specs=[whole(vmem)] * (len(staged) + 4),
        scratch_shapes=[pltpu.SemaphoreType.DMA((len(staged),))],
        compiler_params=limit(8),
        name="pack_own",
    )(*(pltpu.with_memory_space_constraint(x, pltpu.HBM) for x in staged))
    own, ref_feat, shifts, bias_one, bias_two, view_head = staged
    packet = pl.pallas_call(
        pack_other_body,
        out_shape=packet_shape,
        in_specs=[whole(vmem)] * 4,
        out_specs=whole(vmem),
        compiler_params=limit(8),
        name="pack_other",
    )(part, pick, other_order, other)

    pairs = [(sides * i, sides * (i + 1)) for i in range(tiles - 1)]
    pairs += [(sides * (i + 1) + 1, sides * i + 1) for i in range(tiles - 1)]
    pairs += [(sides * (tiles - 1), sides * (tiles - 1) + 1), (1, 0)]
    got = lax.ppermute(packet, ("tile", "plane"), pairs)

    own, other, shifts, conv_one, conv_two, packet = lax.optimization_barrier(
        (own, other, shifts, conv_one, conv_two, packet)
    )
    if sides == 2:
        before = after = swap_planes(shifts)
    else:
        before = lax.ppermute(shifts, "plane", [(i, i + 1) for i in range(sides - 1)])
        after = lax.ppermute(shifts, "plane", [(i + 1, i) for i in range(sides - 1)])

    def taps(kernel):
        flipped = jnp.flip(kernel, axis=2)
        return jnp.transpose(flipped, (3, 4, 1, 2, 0)).reshape(9 * GROUPS, 3 * GROUPS)

    both_taps = jnp.stack([taps(conv_one), taps(conv_two)])
    span = (planes + 4) * GROUPS * rows
    out_lanes = planes * GROUPS * rows
    late_rows = width - MAX_SHIFT
    high = views * (late_rows + 8) + 8
    *inner, match, first = pl.pallas_call(
        inner_body,
        out_shape=[
            shape((views, width, lanes), bf16),
            shape((width, lanes), bf16),
            shape((8, 128), jnp.int32),
            shape((8, span), f32),
            shape((256, out_lanes), bf16),
            shape((out_lanes, out_lanes), bf16),
            shape((4 * out_lanes, out_lanes), bf16),
            shape((3 * (span - out_lanes), span - out_lanes), bf16),
            shape((4 * out_lanes, out_lanes), bf16),
            shape((high, span), f32),
            shape((high, span), f32),
        ],
        in_specs=[whole(vmem)] * 12,
        out_specs=[whole(vmem)] * 11,
        scratch_shapes=[
            pltpu.VMEM((views, width + 16, lanes), f32),
            pltpu.VMEM((width + 8, lanes), f32),
        ],
        compiler_params=limit(24),
        cost_estimate=pl.CostEstimate(
            flops=3 * 10**9, bytes_accessed=10**6, transcendentals=10**5
        ),
        name="inner_columns",
    )(
        shifts,
        before,
        after,
        bias_one,
        bias_two,
        view_head,
        own,
        other,
        ref_feat,
        own_order,
        other_order,
        both_taps,
    )
    got, match, first, *inner = lax.optimization_barrier((got, match, first, *inner))
    if sides == 2:
        swapped = swap_planes(got)
    else:
        both = lax.all_gather(got, "plane", axis=0)
        got, swapped = both[0], both[1]
    late = pl.pallas_call(
        late_body,
        out_shape=shape((late_rows, out_lanes), bf16),
        in_specs=[whole(vmem)] * 5,
        out_specs=whole(vmem),
        compiler_params=limit(24),
        cost_estimate=pl.CostEstimate(
            flops=2 * 10**9, bytes_accessed=10**6, transcendentals=10**5
        ),
        name="late_columns",
    )(match, first, inner[3], inner[4], inner[8])
    high = views * (MAX_SHIFT + 16) + 8
    return pl.pallas_call(
        outer_body,
        out_shape=shape((GROUPS, planes, rows, width), bf16),
        in_specs=[whole(vmem)] * 12,
        out_specs=whole(pltpu.HBM),
        scratch_shapes=[
            pltpu.VMEM((views, LEAD + width + EDGE, lanes), f32),
            pltpu.VMEM((EDGE + width + EDGE, lanes), f32),
            pltpu.VMEM((high, span), f32),
            pltpu.VMEM((high, span), f32),
            pltpu.VMEM((width, out_lanes), f32),
            pltpu.VMEM((GROUPS, planes, rows, width), bf16),
            pltpu.SemaphoreType.DMA((2,)),
        ],
        compiler_params=limit(24),
        name="outer_columns",
    )(*inner, late, got, swapped)


def solution(mesh):
    placed = (
        P(None, None, "tile"),
        P(None, "plane", None, "tile"),
        P(None, "plane"),
        P(),
        P(),
        P(),
        P(),
        P(),
    )
    return jax.shard_map(
        per_device,
        mesh=mesh,
        in_specs=placed,
        out_specs=P(None, "plane", None, "tile"),
        check_vma=False,
    )
```

```python
import jax
import jax.numpy as jnp
from jax import lax
from jax.experimental import pallas as pl
from jax.experimental.pallas import tpu as pltpu
from jax.sharding import PartitionSpec as P

GROUPS = 8
MAX_SHIFT = 128
LEAD = MAX_SHIFT + 8
EDGE = 16
BATCH = 2
FAR = -3.0e38


def iota(shape, dim):
    return lax.broadcasted_iota(jnp.int32, shape, dim)


def dot(left, right):
    return jnp.dot(left, right, preferred_element_type=jnp.float32)


def dot_nt(left, right):
    return lax.dot_general(
        left, right, (((1,), (1,)), ((), ())), preferred_element_type=jnp.float32
    )


def position():
    tile, plane = lax.axis_index("tile"), lax.axis_index("plane")
    tiles, sides = lax.axis_size("tile"), lax.axis_size("plane")
    order = plane if sides == 2 else 0 * plane
    role = jnp.minimum(plane, 1)
    return role, order, tile == 0, tile == tiles - 1, plane == 0, plane == sides - 1


def columns_of(count, width, start):
    picked = iota((count, width), 0) + start == iota((count, width), 1)
    return picked.astype(jnp.bfloat16)


def edge_columns(width, role):
    row = iota((LEAD, width), 0)
    base = edge_start(role, width, MAX_SHIFT)
    column = jnp.where(row < MAX_SHIFT, base + row, base - 4 + row % 4)
    column = jnp.where((row >= MAX_SHIFT) & (row % 4 < 2), -1, column)
    return (column == iota((LEAD, width), 1)).astype(jnp.bfloat16)


def laid_out(pairs, lanes):
    blocks, tails = [], []
    for pair in pairs:
        a, b = pair[:, 0:lanes], pair[:, lanes:]
        blocks += [a[0:MAX_SHIFT], b[0:MAX_SHIFT]]
        tails.append(jnp.where(iota((8, lanes), 0) < 4, a[MAX_SHIFT:], b[MAX_SHIFT:]))
    return blocks, jnp.concatenate(tails, axis=0)


def lane_order(half, rows, side):
    lanes = 2 * half * rows
    inner = 2 * half // GROUPS
    at, to = iota((lanes, 2 * lanes), 0), iota((lanes, 2 * lanes), 1)
    k, g = (to // (GROUPS * rows)) % inner, (to // rows) % GROUPS
    channel = g * inner + k - half * side
    row = (to // lanes) * (half * rows) + channel * rows + to % rows
    held = (channel >= 0) & (channel < half) & (row == at)
    return held.astype(jnp.bfloat16)


def ref_order(lanes, rows):
    at, to = iota((lanes, lanes), 0), iota((lanes, lanes), 1)
    k, g, h = to // (GROUPS * rows), (to // rows) % GROUPS, to % rows
    return ((g * (lanes // (GROUPS * rows)) + k) * rows + h == at).astype(jnp.bfloat16)


def turned_half(half_ref, pick, order):
    views, half, rows, width = half_ref.shape
    lanes = 2 * half * rows
    block = half_ref[...].reshape(views * half * rows, width)
    columns = dot_nt(pick, block).astype(jnp.bfloat16)
    return [dot(columns[:, i : i + lanes], order) for i in range(0, columns.shape[1], lanes)]


def turned_ref(ref_ref, pick):
    channels, rows, width = ref_ref.shape
    lanes = channels * rows
    columns = dot_nt(pick, ref_ref[...].reshape(lanes, width)).astype(jnp.bfloat16)
    return dot(columns, ref_order(lanes, rows))


def edge_start(role, width, count):
    return jnp.where(role == 0, width - count, 0)


def pack_own_body(*refs):
    count = (len(refs) - 5) // 2
    sources, targets = refs[:count], refs[count : 2 * count]
    part_ref, pick_ref, own_order_ref, other_order_ref, sems = refs[2 * count :]
    copies = [
        pltpu.make_async_copy(source, target, sems.at[i])
        for i, (source, target) in enumerate(zip(sources, targets))
    ]
    for copy in copies:
        copy.start()
    own_ref, ref_ref = targets[:2]
    views, half, rows, width = own_ref.shape
    lanes = part_ref.shape[1]
    role, order, *_ = position()
    pick_ref[...] = edge_columns(width, role)
    own_order_ref[...] = lane_order(half, rows, order)
    other_order_ref[...] = lane_order(half, rows, 1 - order)
    few = columns_of(EDGE, width, edge_start(role, width, 2)).astype(jnp.float32)
    few = jnp.where(iota((EDGE, width), 0) < 2, few, 0.0).astype(jnp.bfloat16)
    copies[0].wait()
    pairs = turned_half(own_ref, pick_ref[...], own_order_ref[...])
    blocks, tails = laid_out(pairs, lanes)
    for v, block in enumerate(blocks):
        part_ref[v * MAX_SHIFT : (v + 1) * MAX_SHIFT] = block.astype(jnp.bfloat16)
    for copy in copies[1:]:
        copy.wait()
    extra = turned_ref(ref_ref, few)[0:8]
    tails = jnp.concatenate([tails[0:8] + extra, tails[8:]], axis=0)
    part_ref[views * MAX_SHIFT :] = tails.astype(jnp.bfloat16)


def pack_other_body(part_ref, pick_ref, other_order_ref, other_ref, packet_ref):
    lanes = packet_ref.shape[1]
    pairs = turned_half(other_ref, pick_ref[...], other_order_ref[...])
    blocks, tails = laid_out(pairs, lanes)
    for v, block in enumerate(blocks):
        rows = pl.ds(v * MAX_SHIFT, MAX_SHIFT)
        packet_ref[rows] = (part_ref[rows].astype(jnp.float32) + block).astype(jnp.bfloat16)
    at = len(blocks) * MAX_SHIFT
    packet_ref[at:] = (part_ref[at:].astype(jnp.float32) + tails).astype(jnp.bfloat16)


def lane_table(values_ref, rows, lane):
    which = lane // rows % GROUPS
    table = jnp.zeros(lane.shape, jnp.float32)
    for o in range(GROUPS):
        table = jnp.where(which == o, values_ref[o], table)
    return table


def base_blocks(taps_ref, which, rows, apart):
    block = GROUPS * rows
    slots = 128 // (4 * rows)
    at, lane = iota((3 * GROUPS, 128), 0), iota((3 * GROUPS, 128), 1)
    if apart:
        spreads = [
            (lane // (slots * rows) + t * 4 == at % GROUPS)
            & ((lane // rows) % slots == at // GROUPS)
            for t in range(2)
        ]
    else:
        spreads = [lane // rows == at]
    stretch = (iota((block, GROUPS), 0) // rows == iota((block, GROUPS), 1)).astype(jnp.bfloat16)
    gap = iota((block, 128), 0) % rows - iota((block, 128), 1) % rows + 1
    found = []
    for spread in spreads:
        wide = dot(taps_ref[which], spread.astype(jnp.bfloat16)).astype(jnp.bfloat16)
        for e in range(3):
            base = jnp.zeros((block, 128), jnp.float32)
            for b in range(3):
                at = (b * 3 + e) * GROUPS
                base = jnp.where(gap == b, dot(stretch, wide[at : at + GROUPS]), base)
            found.append(base)
    return [found[i : i + 3] for i in range(0, len(found), 3)]


def band_rows(e, j, block):
    per_tile = 128 // block
    whole = 2 * per_tile
    if j < whole:
        return (e * whole + j) * block
    return (3 * whole + 2 * e + j - whole) * block


def build_band_one(taps_ref, band_ref, rest_ref, rows):
    block = GROUPS * rows
    lane = iota((block, 128), 1)
    per_tile = 128 // block
    zero = jnp.zeros((block, 128), jnp.bfloat16)
    (bases,) = base_blocks(taps_ref, 0, rows, False)
    for e, base in enumerate(bases):
        low_parts, high_parts = [], []
        for turn in range(per_tile):
            moved = pltpu.roll(base, turn * block, 1) if turn else base
            high_parts.append(jnp.where(lane >= turn * block, moved, 0.0).astype(jnp.bfloat16))
            low_parts.append(jnp.where(lane < turn * block, moved, 0.0).astype(jnp.bfloat16))
        for j in range(2 * per_tile + 2):
            first, turn = (j - 2) // per_tile, (j - 2) % per_tile
            at = band_rows(e, j, block)
            for t in range(2):
                part = zero
                if t == first:
                    part = high_parts[turn]
                elif t == first + 1 and turn > per_tile - 3:
                    part = low_parts[turn]
                band_ref[at : at + block, t * 128 : (t + 1) * 128] = part
                if t == 0 and j < per_tile:
                    rest_ref[(e * per_tile + j) * block : (e * per_tile + j + 1) * block] = part
    for j in range(2):
        at = (3 * (2 * per_tile + 2) + j) * block
        band_ref[at : at + block] = jnp.zeros((block, 256), jnp.bfloat16)


def build_band_two(taps_ref, band_ref, rows):
    block = GROUPS * rows
    per_tile = 128 // block
    slots = 2 * per_tile
    plane = (iota((block, 128), 1) // rows) % slots
    for t, bases in enumerate(base_blocks(taps_ref, 1, rows, True)):
        for e, base in enumerate(bases):
            for j in range(slots + 2):
                turn = (j - 2) * rows % 128
                moved = pltpu.roll(base, turn, 1) if turn else base
                held = (plane >= j - 2) & (plane <= j)
                at = band_rows(e, j, block)
                band_ref[at : at + block, t * 128 : (t + 1) * 128] = jnp.where(
                    held, moved, 0.0
                ).astype(jnp.bfloat16)
    for j in range(2):
        at = (3 * (slots + 2) + j) * block
        band_ref[at : at + block] = jnp.zeros((block, 256), jnp.bfloat16)


def build_tables(planes, rows, inner, bias_one, bias_two, view_head, ends, table_ref, spread_ref, perm_ref):
    block = GROUPS * rows
    out_lanes = planes * block
    span = table_ref.shape[1]
    is_first_plane, is_last_plane = ends
    at = iota((1, span), 1)
    plane = at // block
    outside = ((plane < 2) & is_first_plane) | ((plane >= planes + 2) & is_last_plane)
    table_ref[0:1] = jnp.where(outside, 0.0, 1.0 / inner)
    outside = ((plane == 0) & is_first_plane) | ((plane == planes + 1) & is_last_plane)
    table_ref[1:2] = jnp.where(outside, FAR, lane_table(bias_one, rows, at))
    table_ref[2:3] = lane_table(bias_two, planes * rows, at)
    table_ref[3:4] = lane_table(view_head, planes * rows, at)
    row, lane = iota(spread_ref.shape, 0), iota(spread_ref.shape, 1)
    same = (row // rows % planes == lane // block) & (row % rows == lane % rows)
    spread_ref[...] = same.astype(jnp.bfloat16)
    to = iota(perm_ref.shape, 0)
    g, j, h = to // (planes * rows), (to // rows) % planes, to % rows
    perm = (j * GROUPS + g) * rows + h == iota(perm_ref.shape, 1)
    perm_ref[...] = perm.astype(jnp.bfloat16)


def fill(pieces, near, src, wide, match, table_ref, block):
    shared = lax.axis_size("plane") == 2
    last = len(near) - 2
    for at, src_at, wide_at, count in pieces:
        quarter = iota((count, 128), 1) // block
        lower, middle, even = quarter < 2, (quarter == 1) | (quarter == 2), quarter % 2 == 0
        here = wide[wide_at : wide_at + count]
        ready = {}

        def product(j):
            if shared and j >= last:
                j -= last
            if j not in ready:
                ready[j] = src[pl.ds(src_at - near[j], count)] * here
            return ready[j]

        tiles = match.shape[1] // 128
        for q in (0, *reversed(range(1, tiles))):
            a, c, b, d = (product(q * 4 + k) for k in range(4))
            x = jnp.where(lower, a, b) + pltpu.roll(jnp.where(lower, b, a), 64, 1)
            z = jnp.where(middle, c, d) + pltpu.roll(jnp.where(middle, d, c), 64, 1)
            y = jnp.where(even, x, z) + pltpu.roll(jnp.where(even, z, x), 96, 1)
            y = y * table_ref[0:1, q * 128 : (q + 1) * 128]
            y = y.astype(jnp.bfloat16).astype(jnp.float32)
            match[at : at + count, q * 128 : (q + 1) * 128] = y


def three_taps(volume, low, high, out_lanes):
    tile = volume.shape[1] - out_lanes
    parts = [volume[low + e : high + e] for e in range(3)]
    tails = [part[:, out_lanes:] for part in parts]
    near = iota((high - low, tile), 1) < tile // 2
    paired = jnp.where(near, tails[0], pltpu.roll(tails[1], tile // 2, 1))
    sides = [part[:, 0:out_lanes] for part in parts] + [paired, tails[2]]
    wide = jnp.concatenate([side.astype(jnp.bfloat16) for side in sides], axis=1)
    return wide, jnp.concatenate([tail.astype(jnp.bfloat16) for tail in tails], axis=1)


def convolve_first(low, high, planes, block, match, first, table_ref, band_one, rest_ref):
    out_lanes = planes * block
    wide, tails = three_taps(match, low, high, out_lanes)
    raw = dot(wide, band_one[...])
    main = jnp.maximum(raw + table_ref[1:2, 0:out_lanes], 0.0)
    raw = dot(tails, rest_ref[...])
    rest = jnp.maximum(raw + table_ref[1:2, out_lanes:], 0.0)

    def store():
        first[low:high, 0:out_lanes] = main
        first[low:high, out_lanes:] = rest

    return store


def convolve_second(low, high, planes, block, first, table_ref, band_two):
    out_lanes = planes * block
    wide, _ = three_taps(first, low, high, out_lanes)
    second = dot(wide, band_two[...])
    second = jnp.maximum(second + table_ref[2:3, 0:out_lanes], 0.0) * table_ref[3:4, 0:out_lanes]
    half = out_lanes // 2
    return second[:, 0:half] + second[:, half:]


def weights(second, spread_ref):
    upper = second.astype(jnp.bfloat16)
    under = (second - upper.astype(jnp.float32)).astype(jnp.bfloat16)
    score = dot(jnp.concatenate([upper, under], axis=1), spread_ref[...])
    return jax.nn.sigmoid(score)


def first_stage(
    views, tall, planes, block, filled, mend, match, first, table_ref, band_one, rest_ref
):
    store = None
    for v in range(views + 1):
        if v < views:
            filled(v)
        if store is not None:
            store()
            mend((v - 1) * tall)
        if v < views:
            low, high = v * tall, (v + 1) * tall
            store = convolve_first(
                low, high, planes, block, match, first, table_ref, band_one, rest_ref
            )


def second_stage(views, tall, planes, block, match, first, table_ref, band_two, spread_ref):
    out_lanes = planes * block
    total = weighted = 0.0
    steps = range(0, views, BATCH)
    seconds = [
        convolve_second(at * tall, (at + BATCH) * tall, planes, block, first, table_ref, band_two)
        for at in steps
    ]
    for at, second in zip(steps, seconds):
        weight = weights(second, spread_ref)
        for v in range(BATCH):
            part = weight[v * tall : (v + 1) * tall]
            row = (at + v) * tall + 2
            total = total + part
            weighted = weighted + part * match[row : row + tall, 2 * block : 2 * block + out_lanes]
    return weighted / total


def pack_shifts(shifts, before, after, word_ref):
    for row, ref in enumerate((before, shifts, after)):
        word = ref[0:1]
        for v in range(1, ref.shape[0]):
            word = word | (ref[v : v + 1] << (8 * v))
        word_ref[row : row + 1, 0 : word.shape[1]] = word


def read_shifts(views, planes, word_ref):
    at = [(0, planes - 2), (0, planes - 1)] + [(1, d) for d in range(planes)] + [(2, 0), (2, 1)]
    words = [word_ref[row, d] for row, d in at]
    if lax.axis_size("plane") == 2:
        _, _, _, _, is_first_plane, _ = position()
        for k in range(2):
            inside = jnp.where(is_first_plane, words[planes + 2 + k], words[k])
            words[k] = words[planes + 2 + k] = inside
    return [[(word >> (8 * v)) & 255 for word in words] for v in range(views)]


def inner_body(
    shifts,
    before,
    after,
    bias_one,
    bias_two,
    view_head,
    own_ref,
    other_ref,
    ref_ref,
    own_order_ref,
    other_order_ref,
    taps_ref,
    cols_ref,
    ref_cols_ref,
    word_ref,
    table_ref,
    spread_ref,
    perm_ref,
    band_one,
    rest_ref,
    band_two,
    match,
    first,
    src,
    wide,
):
    views, half, rows, width = own_ref.shape
    planes = shifts.shape[1]
    lanes = 2 * half * rows
    inner = 2 * half // GROUPS
    block = GROUPS * rows
    _, _, _, _, *ends = position()
    pick = columns_of(width, width, 0)
    none = jnp.zeros((8, lanes), jnp.float32)
    columns = turned_ref(ref_ref, pick)
    ref_cols_ref[...] = columns.astype(jnp.bfloat16)
    wide[0:width] = columns
    wide[width:] = none
    pairs = zip(
        turned_half(own_ref, pick, own_order_ref[...]),
        turned_half(other_ref, pick, other_order_ref[...]),
    )
    for i, (low, high) in enumerate(pairs):
        columns = low + high
        for k in range(2):
            v = 2 * i + k
            part = columns[:, k * lanes : (k + 1) * lanes]
            cols_ref[v] = part.astype(jnp.bfloat16)
            src[v, 0:8] = none
            src[v, 8 : 8 + width] = part
            src[v, 8 + width :] = none
    build_tables(
        planes, rows, inner, bias_one, bias_two, view_head, ends, table_ref, spread_ref, perm_ref
    )
    build_band_one(taps_ref, band_one, rest_ref, rows)
    build_band_two(taps_ref, band_two, rows)
    pack_shifts(shifts, before, after, word_ref)
    near = read_shifts(views, planes, word_ref)
    out_rows = width - MAX_SHIFT
    tall = out_rows + 8
    base = MAX_SHIFT - 2

    def filled(v):
        pieces = [
            (v * tall + r, 8 + base + r, base + r, min(48, tall - r)) for r in range(0, tall, 48)
        ]
        fill(pieces, near[v], src.at[v], wide, match, table_ref, block)

    first_stage(
        views,
        tall,
        planes,
        block,
        filled,
        lambda row: None,
        match,
        first,
        table_ref,
        band_one,
        rest_ref,
    )
    for ref in (match, first):
        ref[views * tall :] = jnp.zeros((8, match.shape[1]), jnp.float32)


def late_body(match, first, table_ref, spread_ref, band_two, late_ref):
    out_rows, out_lanes = late_ref.shape
    block = (match.shape[1] - out_lanes) // 4
    views = match.shape[0] // (out_rows + 8)
    joined = second_stage(
        views, out_rows + 8, out_lanes // block, block, match, first, table_ref, band_two, spread_ref
    )
    late_ref[...] = joined[0:out_rows].astype(jnp.bfloat16)


def outer_body(
    cols_ref,
    ref_cols_ref,
    word_ref,
    table_ref,
    spread_ref,
    perm_ref,
    band_one,
    rest_ref,
    band_two,
    late_ref,
    got_ref,
    swapped_ref,
    out_ref,
    src,
    wide,
    match,
    first,
    joined,
    buffer,
    sems,
):
    views, width, lanes = cols_ref.shape
    groups, planes, rows, _ = out_ref.shape
    block = groups * rows
    _, order, is_first_tile, is_last_tile, *_ = position()

    near = read_shifts(views, planes, word_ref)
    left = jnp.where(order == 0, got_ref[...], swapped_ref[...])
    left = jnp.where(is_first_tile, jnp.zeros_like(left), left)
    right = jnp.where(order == 0, swapped_ref[...], got_ref[...])
    left_tails = left[views * MAX_SHIFT :].astype(jnp.float32)
    right_tails = right[views * MAX_SHIFT :].astype(jnp.float32)
    for v in range(views):
        at = v * MAX_SHIFT
        tail = left_tails[v // 2 * 8 : v // 2 * 8 + 8]
        src[v, 0:8] = tail if v % 2 else pltpu.roll(tail, 4, 0)
        src[v, 8:LEAD] = left[at : at + MAX_SHIFT].astype(jnp.float32)
        src[v, LEAD : LEAD + width] = cols_ref[v].astype(jnp.float32)
        src[v, LEAD + width :] = right[at : at + EDGE].astype(jnp.float32)
    wide[EDGE - 8 : EDGE] = pltpu.roll(left_tails[0:8], 6, 0)
    wide[EDGE : EDGE + width] = ref_cols_ref[...].astype(jnp.float32)
    wide[EDGE + width : EDGE + width + 8] = jnp.where(is_last_tile, 0.0, right_tails[0:8])
    main = MAX_SHIFT + 8
    tall = main + 8
    none = jnp.zeros((1, match.shape[1]), jnp.float32)

    def filled(v):
        at = v * tall
        pieces = [
            (at + r, LEAD - 2 + r, EDGE - 2 + r, min(48, main - r)) for r in range(0, main, 48)
        ]
        pieces += [(at + main, LEAD + width - 4, EDGE + width - 4, 8)]
        fill(pieces, near[v], src.at[v], wide, match, table_ref, block)

    def mend(row):
        for at, at_end in ((row, is_first_tile), (row + main + 3, is_last_tile)):
            first[at : at + 1] = jnp.where(at_end, none, first[at : at + 1])

    first_stage(
        views, tall, planes, block, filled, mend, match, first, table_ref, band_one, rest_ref
    )
    part = second_stage(
        views, tall, planes, block, match, first, table_ref, band_two, spread_ref
    )
    joined[0:MAX_SHIFT] = part[0:MAX_SHIFT]
    joined[MAX_SHIFT:] = late_ref[...].astype(jnp.float32)
    joined[MAX_SHIFT : MAX_SHIFT + 2] = part[MAX_SHIFT : MAX_SHIFT + 2]
    joined[width - 2 :] = part[main : main + 2]
    copies = []
    for half in range(2):
        at = half * (groups // 2)
        span = pl.ds(at, groups // 2)
        chosen = perm_ref[at * planes * rows : (at + groups // 2) * planes * rows]
        turned = dot_nt(chosen, joined[...].astype(jnp.bfloat16)).astype(jnp.bfloat16)
        buffer[at : at + groups // 2] = turned.reshape(groups // 2, planes, rows, width)
        copy = pltpu.make_async_copy(buffer.at[span], out_ref.at[span], sems.at[half])
        copy.start()
        copies.append(copy)
    for copy in copies:
        copy.wait()


def whole(memory):
    return pl.BlockSpec(memory_space=memory)


def limit(mebibytes):
    return pltpu.CompilerParams(vmem_limit_bytes=mebibytes * 1024 * 1024)


def swap_planes(value):
    return lax.ppermute(value, "plane", [(0, 1), (1, 0)])


def per_device(ref_feat, src_feat, shifts, conv_one, bias_one, conv_two, bias_two, view_head):
    views, _, rows, width = src_feat.shape
    planes = shifts.shape[1]
    lanes = ref_feat.shape[0] * rows
    tiles, sides = lax.axis_size("tile"), lax.axis_size("plane")
    bf16, f32 = jnp.bfloat16, jnp.float32
    vmem = pltpu.VMEM
    shape = jax.ShapeDtypeStruct
    if sides == 2:
        own, other = src_feat, swap_planes(src_feat)
    else:
        full = lax.all_gather(src_feat, "plane", axis=1, tiled=True)
        half = full.shape[1] // 2
        own, other = full[:, :half], full[:, half:]

    packet_shape = shape((views * MAX_SHIFT + views * 4, lanes), bf16)
    order_shape = shape((lanes, 2 * lanes), bf16)
    staged = (own, ref_feat, shifts, bias_one, bias_two, view_head)
    *staged, part, pick, own_order, other_order = pl.pallas_call(
        pack_own_body,
        out_shape=[shape(x.shape, x.dtype) for x in staged]
        + [packet_shape, shape((LEAD, width), bf16), order_shape, order_shape],
        in_specs=[whole(pltpu.HBM)] * len(staged),
        out_specs=[whole(vmem)] * (len(staged) + 4),
        scratch_shapes=[pltpu.SemaphoreType.DMA((len(staged),))],
        compiler_params=limit(8),
        name="pack_own",
    )(*(pltpu.with_memory_space_constraint(x, pltpu.HBM) for x in staged))
    own, ref_feat, shifts, bias_one, bias_two, view_head = staged
    packet = pl.pallas_call(
        pack_other_body,
        out_shape=packet_shape,
        in_specs=[whole(vmem)] * 4,
        out_specs=whole(vmem),
        compiler_params=limit(8),
        name="pack_other",
    )(part, pick, other_order, other)

    pairs = [(sides * i, sides * (i + 1)) for i in range(tiles - 1)]
    pairs += [(sides * (i + 1) + 1, sides * i + 1) for i in range(tiles - 1)]
    pairs += [(sides * (tiles - 1), sides * (tiles - 1) + 1), (1, 0)]
    got = lax.ppermute(packet, ("tile", "plane"), pairs)

    own, other, shifts, conv_one, conv_two, packet = lax.optimization_barrier(
        (own, other, shifts, conv_one, conv_two, packet)
    )
    if sides == 2:
        before = after = swap_planes(shifts)
    else:
        before = lax.ppermute(shifts, "plane", [(i, i + 1) for i in range(sides - 1)])
        after = lax.ppermute(shifts, "plane", [(i + 1, i) for i in range(sides - 1)])

    def taps(kernel):
        flipped = jnp.flip(kernel, axis=2)
        return jnp.transpose(flipped, (3, 4, 1, 2, 0)).reshape(9 * GROUPS, 3 * GROUPS)

    both_taps = jnp.stack([taps(conv_one), taps(conv_two)])
    span = (planes + 4) * GROUPS * rows
    out_lanes = planes * GROUPS * rows
    late_rows = width - MAX_SHIFT
    high = views * (late_rows + 8) + 8
    *inner, match, first = pl.pallas_call(
        inner_body,
        out_shape=[
            shape((views, width, lanes), bf16),
            shape((width, lanes), bf16),
            shape((8, 128), jnp.int32),
            shape((8, span), f32),
            shape((256, out_lanes), bf16),
            shape((out_lanes, out_lanes), bf16),
            shape((4 * out_lanes, out_lanes), bf16),
            shape((3 * (span - out_lanes), span - out_lanes), bf16),
            shape((4 * out_lanes, out_lanes), bf16),
            shape((high, span), f32),
            shape((high, span), f32),
        ],
        in_specs=[whole(vmem)] * 12,
        out_specs=[whole(vmem)] * 11,
        scratch_shapes=[
            pltpu.VMEM((views, width + 16, lanes), f32),
            pltpu.VMEM((width + 8, lanes), f32),
        ],
        compiler_params=limit(24),
        cost_estimate=pl.CostEstimate(
            flops=3 * 10**9, bytes_accessed=10**6, transcendentals=10**5
        ),
        name="inner_columns",
    )(
        shifts,
        before,
        after,
        bias_one,
        bias_two,
        view_head,
        own,
        other,
        ref_feat,
        own_order,
        other_order,
        both_taps,
    )
    got, match, first, *inner = lax.optimization_barrier((got, match, first, *inner))
    if sides == 2:
        swapped = swap_planes(got)
    else:
        both = lax.all_gather(got, "plane", axis=0)
        got, swapped = both[0], both[1]
    late = pl.pallas_call(
        late_body,
        out_shape=shape((late_rows, out_lanes), bf16),
        in_specs=[whole(vmem)] * 5,
        out_specs=whole(vmem),
        compiler_params=limit(24),
        cost_estimate=pl.CostEstimate(
            flops=2 * 10**9, bytes_accessed=10**6, transcendentals=10**5
        ),
        name="late_columns",
    )(match, first, inner[3], inner[4], inner[8])
    high = views * (MAX_SHIFT + 16) + 8
    return pl.pallas_call(
        outer_body,
        out_shape=shape((GROUPS, planes, rows, width), bf16),
        in_specs=[whole(vmem)] * 12,
        out_specs=whole(pltpu.HBM),
        scratch_shapes=[
            pltpu.VMEM((views, LEAD + width + EDGE, lanes), f32),
            pltpu.VMEM((EDGE + width + EDGE, lanes), f32),
            pltpu.VMEM((high, span), f32),
            pltpu.VMEM((high, span), f32),
            pltpu.VMEM((width, out_lanes), f32),
            pltpu.VMEM((GROUPS, planes, rows, width), bf16),
            pltpu.SemaphoreType.DMA((2,)),
        ],
        compiler_params=limit(24),
        name="outer_columns",
    )(*inner, late, got, swapped)


def solution(mesh):
    placed = (
        P(None, None, "tile"),
        P(None, "plane", None, "tile"),
        P(None, "plane"),
        P(),
        P(),
        P(),
        P(),
        P(),
    )
    return jax.shard_map(
        per_device,
        mesh=mesh,
        in_specs=placed,
        out_specs=P(None, "plane", None, "tile"),
        check_vma=False,
    )
```

```python
import jax
import jax.numpy as jnp
from jax import lax
from jax.experimental import pallas as pl
from jax.experimental.pallas import tpu as pltpu
from jax.sharding import PartitionSpec as P

GROUPS = 8
MAX_SHIFT = 128
LEAD = MAX_SHIFT + 8
EDGE = 16
BATCH = 1
FAR = -3.0e38


def iota(shape, dim):
    return lax.broadcasted_iota(jnp.int32, shape, dim)


def dot(left, right):
    return jnp.dot(left, right, preferred_element_type=jnp.float32)


def dot_nt(left, right):
    return lax.dot_general(
        left, right, (((1,), (1,)), ((), ())), preferred_element_type=jnp.float32
    )


def position():
    tile, plane = lax.axis_index("tile"), lax.axis_index("plane")
    tiles, sides = lax.axis_size("tile"), lax.axis_size("plane")
    order = plane if sides == 2 else 0 * plane
    role = jnp.minimum(plane, 1)
    return role, order, tile == 0, tile == tiles - 1, plane == 0, plane == sides - 1


def columns_of(count, width, start):
    picked = iota((count, width), 0) + start == iota((count, width), 1)
    return picked.astype(jnp.bfloat16)


def edge_columns(width, role, dropped):
    row = iota((LEAD, width), 0)
    base = edge_start(role, width, MAX_SHIFT)
    column = jnp.where(row < MAX_SHIFT, base + row, base - 4 + row % 4)
    column = jnp.where(((row >= MAX_SHIFT) & (row % 4 < 2)) | dropped, -1, column)
    return (column == iota((LEAD, width), 1)).astype(jnp.bfloat16)


def laid_out(pairs, lanes):
    blocks, tails = [], []
    for pair in pairs:
        a, b = pair[:, 0:lanes], pair[:, lanes:]
        blocks += [a[0:MAX_SHIFT], b[0:MAX_SHIFT]]
        tails.append(jnp.where(iota((8, lanes), 0) < 4, a[MAX_SHIFT:], b[MAX_SHIFT:]))
    return blocks, jnp.concatenate(tails, axis=0)


def lane_order(half, rows, side):
    lanes = 2 * half * rows
    inner = 2 * half // GROUPS
    at, to = iota((lanes, 2 * lanes), 0), iota((lanes, 2 * lanes), 1)
    k, g = (to // (GROUPS * rows)) % inner, (to // rows) % GROUPS
    channel = g * inner + k - half * side
    row = (to // lanes) * (half * rows) + channel * rows + to % rows
    held = (channel >= 0) & (channel < half) & (row == at)
    return held.astype(jnp.bfloat16)


def ref_order(lanes, rows):
    at, to = iota((lanes, lanes), 0), iota((lanes, lanes), 1)
    k, g, h = to // (GROUPS * rows), (to // rows) % GROUPS, to % rows
    return ((g * (lanes // (GROUPS * rows)) + k) * rows + h == at).astype(jnp.bfloat16)


def turned_half(half_ref, pick, order):
    views, half, rows, width = half_ref.shape
    lanes = 2 * half * rows
    block = half_ref[...].reshape(views * half * rows, width)
    columns = dot_nt(pick, block).astype(jnp.bfloat16)
    return [dot(columns[:, i : i + lanes], order) for i in range(0, columns.shape[1], lanes)]


def turned_ref(ref_ref, pick):
    channels, rows, width = ref_ref.shape
    lanes = channels * rows
    columns = dot_nt(pick, ref_ref[...].reshape(lanes, width)).astype(jnp.bfloat16)
    return dot(columns, ref_order(lanes, rows))


def edge_start(role, width, count):
    return jnp.where(role == 0, width - count, 0)


def pack_own_body(*refs):
    count = (len(refs) - 5) // 2
    sources, targets = refs[:count], refs[count : 2 * count]
    part_ref, pick_ref, own_order_ref, other_order_ref, sems = refs[2 * count :]
    copies = [
        pltpu.make_async_copy(source, target, sems.at[i])
        for i, (source, target) in enumerate(zip(sources, targets))
    ]
    for copy in copies:
        copy.start()
    own_ref, ref_ref = targets[:2]
    views, half, rows, width = own_ref.shape
    lanes = part_ref.shape[1]
    role, order, is_first_tile, is_last_tile, *_ = position()
    dropped = (is_first_tile & (role != 0)) | (is_last_tile & (role == 0))
    pick_ref[...] = edge_columns(width, role, dropped)
    own_order_ref[...] = lane_order(half, rows, order)
    other_order_ref[...] = lane_order(half, rows, 1 - order)
    few = columns_of(EDGE, width, edge_start(role, width, 2)).astype(jnp.float32)
    kept = (iota((EDGE, width), 0) < 2) & ~dropped
    few = jnp.where(kept, few, 0.0).astype(jnp.bfloat16)
    copies[0].wait()
    pairs = turned_half(own_ref, pick_ref[...], own_order_ref[...])
    blocks, tails = laid_out(pairs, lanes)
    for v, block in enumerate(blocks):
        part_ref[v * MAX_SHIFT : (v + 1) * MAX_SHIFT] = block.astype(jnp.bfloat16)
    for copy in copies[1:]:
        copy.wait()
    extra = turned_ref(ref_ref, few)[0:8]
    tails = jnp.concatenate([tails[0:8] + extra, tails[8:]], axis=0)
    part_ref[views * MAX_SHIFT :] = tails.astype(jnp.bfloat16)


def pack_other_body(part_ref, pick_ref, other_order_ref, other_ref, packet_ref):
    lanes = packet_ref.shape[1]
    pairs = turned_half(other_ref, pick_ref[...], other_order_ref[...])
    blocks, tails = laid_out(pairs, lanes)
    for v, block in enumerate(blocks):
        rows = pl.ds(v * MAX_SHIFT, MAX_SHIFT)
        packet_ref[rows] = (part_ref[rows].astype(jnp.float32) + block).astype(jnp.bfloat16)
    at = len(blocks) * MAX_SHIFT
    packet_ref[at:] = (part_ref[at:].astype(jnp.float32) + tails).astype(jnp.bfloat16)


def lane_table(values_ref, rows, lane):
    which = lane // rows % GROUPS
    table = jnp.zeros(lane.shape, jnp.float32)
    for o in range(GROUPS):
        table = jnp.where(which == o, values_ref[o], table)
    return table


def base_blocks(taps_ref, which, rows, apart):
    block = GROUPS * rows
    slots = 128 // (4 * rows)
    at, lane = iota((3 * GROUPS, 128), 0), iota((3 * GROUPS, 128), 1)
    if apart:
        spreads = [
            (lane // (slots * rows) + t * 4 == at % GROUPS)
            & ((lane // rows) % slots == at // GROUPS)
            for t in range(2)
        ]
    else:
        spreads = [lane // rows == at]
    stretch = (iota((block, GROUPS), 0) // rows == iota((block, GROUPS), 1)).astype(jnp.bfloat16)
    gap = iota((block, 128), 0) % rows - iota((block, 128), 1) % rows + 1
    found = []
    for spread in spreads:
        wide = dot(taps_ref[which], spread.astype(jnp.bfloat16)).astype(jnp.bfloat16)
        for e in range(3):
            base = jnp.zeros((block, 128), jnp.float32)
            for b in range(3):
                at = (b * 3 + e) * GROUPS
                base = jnp.where(gap == b, dot(stretch, wide[at : at + GROUPS]), base)
            found.append(base)
    return [found[i : i + 3] for i in range(0, len(found), 3)]


def band_rows(e, j, block):
    per_tile = 128 // block
    whole = 2 * per_tile
    if j < whole:
        return (e * whole + j) * block
    return (3 * whole + 2 * e + j - whole) * block


def build_band_one(taps_ref, band_ref, rest_ref, rows):
    block = GROUPS * rows
    lane = iota((block, 128), 1)
    per_tile = 128 // block
    zero = jnp.zeros((block, 128), jnp.bfloat16)
    (bases,) = base_blocks(taps_ref, 0, rows, False)
    for e, base in enumerate(bases):
        low_parts, high_parts = [], []
        for turn in range(per_tile):
            moved = pltpu.roll(base, turn * block, 1) if turn else base
            high_parts.append(jnp.where(lane >= turn * block, moved, 0.0).astype(jnp.bfloat16))
            low_parts.append(jnp.where(lane < turn * block, moved, 0.0).astype(jnp.bfloat16))
        for j in range(2 * per_tile + 2):
            first, turn = (j - 2) // per_tile, (j - 2) % per_tile
            at = band_rows(e, j, block)
            for t in range(2):
                part = zero
                if t == first:
                    part = high_parts[turn]
                elif t == first + 1 and turn > per_tile - 3:
                    part = low_parts[turn]
                band_ref[at : at + block, t * 128 : (t + 1) * 128] = part
                if t == 0 and j < per_tile:
                    rest_ref[(e * per_tile + j) * block : (e * per_tile + j + 1) * block] = part
    for j in range(2):
        at = (3 * (2 * per_tile + 2) + j) * block
        band_ref[at : at + block] = jnp.zeros((block, 256), jnp.bfloat16)


def build_band_two(taps_ref, band_ref, rows):
    block = GROUPS * rows
    per_tile = 128 // block
    slots = 2 * per_tile
    plane = (iota((block, 128), 1) // rows) % slots
    for t, bases in enumerate(base_blocks(taps_ref, 1, rows, True)):
        for e, base in enumerate(bases):
            for j in range(slots + 2):
                turn = (j - 2) * rows % 128
                moved = pltpu.roll(base, turn, 1) if turn else base
                held = (plane >= j - 2) & (plane <= j)
                at = band_rows(e, j, block)
                band_ref[at : at + block, t * 128 : (t + 1) * 128] = jnp.where(
                    held, moved, 0.0
                ).astype(jnp.bfloat16)
    for j in range(2):
        at = (3 * (slots + 2) + j) * block
        band_ref[at : at + block] = jnp.zeros((block, 256), jnp.bfloat16)


def build_tables(planes, rows, inner, bias_one, bias_two, view_head, ends, table_ref, spread_ref, perm_ref):
    block = GROUPS * rows
    out_lanes = planes * block
    span = table_ref.shape[1]
    is_first_plane, is_last_plane = ends
    at = iota((1, span), 1)
    plane = at // block
    outside = ((plane < 2) & is_first_plane) | ((plane >= planes + 2) & is_last_plane)
    table_ref[0:1] = jnp.where(outside, 0.0, 1.0 / inner)
    outside = ((plane == 0) & is_first_plane) | ((plane == planes + 1) & is_last_plane)
    table_ref[1:2] = jnp.where(outside, FAR, lane_table(bias_one, rows, at))
    table_ref[2:3] = lane_table(bias_two, planes * rows, at)
    table_ref[3:4] = lane_table(view_head, planes * rows, at)
    row, lane = iota(spread_ref.shape, 0), iota(spread_ref.shape, 1)
    same = (row // rows % planes == lane // block) & (row % rows == lane % rows)
    spread_ref[...] = same.astype(jnp.bfloat16)
    to = iota(perm_ref.shape, 0)
    g, j, h = to // (planes * rows), (to // rows) % planes, to % rows
    perm = (j * GROUPS + g) * rows + h == iota(perm_ref.shape, 1)
    perm_ref[...] = perm.astype(jnp.bfloat16)


def fill(pieces, near, src, wide, match, table_ref, block):
    shared = lax.axis_size("plane") == 2
    last = len(near) - 2
    for at, src_at, wide_at, count in pieces:
        quarter = iota((count, 128), 1) // block
        lower, middle, even = quarter < 2, (quarter == 1) | (quarter == 2), quarter % 2 == 0
        here = wide[wide_at : wide_at + count]
        ready = {}

        def product(j):
            if shared and j >= last:
                j -= last
            if j not in ready:
                ready[j] = src[pl.ds(src_at - near[j], count)] * here
            return ready[j]

        tiles = match.shape[1] // 128
        for q in (0, *reversed(range(1, tiles))):
            a, c, b, d = (product(q * 4 + k) for k in range(4))
            x = jnp.where(lower, a, b) + pltpu.roll(jnp.where(lower, b, a), 64, 1)
            z = jnp.where(middle, c, d) + pltpu.roll(jnp.where(middle, d, c), 64, 1)
            y = jnp.where(even, x, z) + pltpu.roll(jnp.where(even, z, x), 96, 1)
            y = y * table_ref[0:1, q * 128 : (q + 1) * 128]
            y = y.astype(jnp.bfloat16).astype(jnp.float32)
            match[at : at + count, q * 128 : (q + 1) * 128] = y


def three_taps(volume, low, high, out_lanes):
    tile = volume.shape[1] - out_lanes
    parts = [volume[low + e : high + e] for e in range(3)]
    tails = [part[:, out_lanes:] for part in parts]
    near = iota((high - low, tile), 1) < tile // 2
    paired = jnp.where(near, tails[0], pltpu.roll(tails[1], tile // 2, 1))
    sides = [part[:, 0:out_lanes] for part in parts] + [paired, tails[2]]
    wide = jnp.concatenate([side.astype(jnp.bfloat16) for side in sides], axis=1)
    return wide, jnp.concatenate([tail.astype(jnp.bfloat16) for tail in tails], axis=1)


def convolve_first(low, high, planes, block, match, first, table_ref, band_one, rest_ref):
    out_lanes = planes * block
    wide, tails = three_taps(match, low, high, out_lanes)
    raw = dot(wide, band_one[...])
    main = jnp.maximum(raw + table_ref[1:2, 0:out_lanes], 0.0)
    raw = dot(tails, rest_ref[...])
    rest = jnp.maximum(raw + table_ref[1:2, out_lanes:], 0.0)

    def store():
        first[low:high, 0:out_lanes] = main
        first[low:high, out_lanes:] = rest

    return store


def convolve_second(low, high, planes, block, first, table_ref, band_two):
    out_lanes = planes * block
    wide, _ = three_taps(first, low, high, out_lanes)
    second = dot(wide, band_two[...])
    second = jnp.maximum(second + table_ref[2:3, 0:out_lanes], 0.0) * table_ref[3:4, 0:out_lanes]
    half = out_lanes // 2
    return second[:, 0:half] + second[:, half:]


def weights(second, spread_ref):
    upper = second.astype(jnp.bfloat16)
    under = (second - upper.astype(jnp.float32)).astype(jnp.bfloat16)
    score = dot(jnp.concatenate([upper, under], axis=1), spread_ref[...])
    return jax.nn.sigmoid(score)


def first_stage(
    views, tall, planes, block, filled, mend, match, first, table_ref, band_one, rest_ref
):
    store = None
    for v in range(views + 1):
        if v < views:
            filled(v)
        if store is not None:
            store()
            mend((v - 1) * tall)
        if v < views:
            low, high = v * tall, (v + 1) * tall
            store = convolve_first(
                low, high, planes, block, match, first, table_ref, band_one, rest_ref
            )


def second_stage(views, tall, planes, block, match, first, table_ref, band_two, spread_ref):
    out_lanes = planes * block
    total = weighted = 0.0
    steps = range(0, views, BATCH)
    seconds = [
        convolve_second(at * tall, (at + BATCH) * tall, planes, block, first, table_ref, band_two)
        for at in steps
    ]
    for at, second in zip(steps, seconds):
        weight = weights(second, spread_ref)
        for v in range(BATCH):
            part = weight[v * tall : (v + 1) * tall]
            row = (at + v) * tall + 2
            total = total + part
            weighted = weighted + part * match[row : row + tall, 2 * block : 2 * block + out_lanes]
    return weighted / total


def pack_shifts(shifts, before, after, word_ref):
    for row, ref in enumerate((before, shifts, after)):
        word = ref[0:1]
        for v in range(1, ref.shape[0]):
            word = word | (ref[v : v + 1] << (8 * v))
        word_ref[row : row + 1, 0 : word.shape[1]] = word


def read_shifts(views, planes, word_ref):
    at = [(0, planes - 2), (0, planes - 1)] + [(1, d) for d in range(planes)] + [(2, 0), (2, 1)]
    words = [word_ref[row, d] for row, d in at]
    if lax.axis_size("plane") == 2:
        _, _, _, _, is_first_plane, _ = position()
        for k in range(2):
            inside = jnp.where(is_first_plane, words[planes + 2 + k], words[k])
            words[k] = words[planes + 2 + k] = inside
    return [[(word >> (8 * v)) & 255 for word in words] for v in range(views)]


def inner_body(
    shifts,
    before,
    after,
    bias_one,
    bias_two,
    view_head,
    own_ref,
    other_ref,
    ref_ref,
    own_order_ref,
    other_order_ref,
    taps_ref,
    cols_ref,
    ref_cols_ref,
    word_ref,
    table_ref,
    spread_ref,
    perm_ref,
    band_one,
    rest_ref,
    band_two,
    match,
    first,
    src,
    wide,
):
    views, half, rows, width = own_ref.shape
    planes = shifts.shape[1]
    lanes = 2 * half * rows
    inner = 2 * half // GROUPS
    block = GROUPS * rows
    _, _, _, _, *ends = position()
    pick = columns_of(width, width, 0)
    none = jnp.zeros((8, lanes), jnp.float32)
    columns = turned_ref(ref_ref, pick)
    ref_cols_ref[...] = columns.astype(jnp.bfloat16)
    wide[0:width] = columns
    wide[width:] = none
    pairs = zip(
        turned_half(own_ref, pick, own_order_ref[...]),
        turned_half(other_ref, pick, other_order_ref[...]),
    )
    for i, (low, high) in enumerate(pairs):
        columns = low + high
        for k in range(2):
            v = 2 * i + k
            part = columns[:, k * lanes : (k + 1) * lanes]
            cols_ref[v] = part.astype(jnp.bfloat16)
            src[v, 0:8] = none
            src[v, 8 : 8 + width] = part
            src[v, 8 + width :] = none
    build_tables(
        planes, rows, inner, bias_one, bias_two, view_head, ends, table_ref, spread_ref, perm_ref
    )
    build_band_one(taps_ref, band_one, rest_ref, rows)
    build_band_two(taps_ref, band_two, rows)
    pack_shifts(shifts, before, after, word_ref)
    near = read_shifts(views, planes, word_ref)
    out_rows = width - MAX_SHIFT
    tall = out_rows + 8
    base = MAX_SHIFT - 2

    def filled(v):
        pieces = [
            (v * tall + r, 8 + base + r, base + r, min(48, tall - r)) for r in range(0, tall, 48)
        ]
        fill(pieces, near[v], src.at[v], wide, match, table_ref, block)

    first_stage(
        views,
        tall,
        planes,
        block,
        filled,
        lambda row: None,
        match,
        first,
        table_ref,
        band_one,
        rest_ref,
    )
    for ref in (match, first):
        ref[views * tall :] = jnp.zeros((8, match.shape[1]), jnp.float32)


def late_body(match, first, table_ref, spread_ref, band_two, late_ref):
    out_rows, out_lanes = late_ref.shape
    block = (match.shape[1] - out_lanes) // 4
    views = match.shape[0] // (out_rows + 8)
    joined = second_stage(
        views, out_rows + 8, out_lanes // block, block, match, first, table_ref, band_two, spread_ref
    )
    late_ref[...] = joined[0:out_rows].astype(jnp.bfloat16)


def outer_body(
    cols_ref,
    ref_cols_ref,
    word_ref,
    table_ref,
    spread_ref,
    perm_ref,
    band_one,
    rest_ref,
    band_two,
    late_ref,
    got_ref,
    swapped_ref,
    out_ref,
    src,
    wide,
    match,
    first,
    joined,
    buffer,
    sems,
):
    views, width, lanes = cols_ref.shape
    groups, planes, rows, _ = out_ref.shape
    block = groups * rows
    _, order, is_first_tile, is_last_tile, *_ = position()

    near = read_shifts(views, planes, word_ref)
    left = jnp.where(order == 0, got_ref[...], swapped_ref[...])
    right = jnp.where(order == 0, swapped_ref[...], got_ref[...])
    left_tails = left[views * MAX_SHIFT :].astype(jnp.float32)
    right_tails = right[views * MAX_SHIFT :].astype(jnp.float32)
    for v in range(views):
        at = v * MAX_SHIFT
        tail = left_tails[v // 2 * 8 : v // 2 * 8 + 8]
        src[v, 0:8] = tail if v % 2 else pltpu.roll(tail, 4, 0)
        src[v, 8:LEAD] = left[at : at + MAX_SHIFT].astype(jnp.float32)
        src[v, LEAD : LEAD + width] = cols_ref[v].astype(jnp.float32)
        src[v, LEAD + width :] = right[at : at + EDGE].astype(jnp.float32)
    wide[EDGE - 8 : EDGE] = pltpu.roll(left_tails[0:8], 6, 0)
    wide[EDGE : EDGE + width] = ref_cols_ref[...].astype(jnp.float32)
    wide[EDGE + width : EDGE + width + 8] = right_tails[0:8]
    main = MAX_SHIFT + 8
    tall = main + 8
    none = jnp.zeros((1, match.shape[1]), jnp.float32)

    def filled(v):
        at = v * tall
        pieces = [
            (at + r, LEAD - 2 + r, EDGE - 2 + r, min(48, main - r)) for r in range(0, main, 48)
        ]
        pieces += [(at + main, LEAD + width - 4, EDGE + width - 4, 8)]
        fill(pieces, near[v], src.at[v], wide, match, table_ref, block)

    def mend(row):
        for at, at_end in ((row, is_first_tile), (row + main + 3, is_last_tile)):
            first[at : at + 1] = jnp.where(at_end, none, first[at : at + 1])

    first_stage(
        views, tall, planes, block, filled, mend, match, first, table_ref, band_one, rest_ref
    )
    part = second_stage(
        views, tall, planes, block, match, first, table_ref, band_two, spread_ref
    )
    joined[0:MAX_SHIFT] = part[0:MAX_SHIFT]
    joined[MAX_SHIFT:] = late_ref[...].astype(jnp.float32)
    joined[MAX_SHIFT : MAX_SHIFT + 2] = part[MAX_SHIFT : MAX_SHIFT + 2]
    joined[width - 2 :] = part[main : main + 2]
    copies = []
    for half in range(2):
        at = half * (groups // 2)
        span = pl.ds(at, groups // 2)
        chosen = perm_ref[at * planes * rows : (at + groups // 2) * planes * rows]
        turned = dot_nt(chosen, joined[...].astype(jnp.bfloat16)).astype(jnp.bfloat16)
        buffer[at : at + groups // 2] = turned.reshape(groups // 2, planes, rows, width)
        copy = pltpu.make_async_copy(buffer.at[span], out_ref.at[span], sems.at[half])
        copy.start()
        copies.append(copy)
    for copy in copies:
        copy.wait()


def whole(memory):
    return pl.BlockSpec(memory_space=memory)


def limit(mebibytes):
    return pltpu.CompilerParams(vmem_limit_bytes=mebibytes * 1024 * 1024)


def swap_planes(value):
    return lax.ppermute(value, "plane", [(0, 1), (1, 0)])


def per_device(ref_feat, src_feat, shifts, conv_one, bias_one, conv_two, bias_two, view_head):
    views, _, rows, width = src_feat.shape
    planes = shifts.shape[1]
    lanes = ref_feat.shape[0] * rows
    tiles, sides = lax.axis_size("tile"), lax.axis_size("plane")
    bf16, f32 = jnp.bfloat16, jnp.float32
    vmem = pltpu.VMEM
    shape = jax.ShapeDtypeStruct
    if sides == 2:
        own, other = src_feat, swap_planes(src_feat)
    else:
        full = lax.all_gather(src_feat, "plane", axis=1, tiled=True)
        half = full.shape[1] // 2
        own, other = full[:, :half], full[:, half:]

    packet_shape = shape((views * MAX_SHIFT + views * 4, lanes), bf16)
    order_shape = shape((lanes, 2 * lanes), bf16)
    staged = (own, ref_feat, shifts, bias_one, bias_two, view_head)
    *staged, part, pick, own_order, other_order = pl.pallas_call(
        pack_own_body,
        out_shape=[shape(x.shape, x.dtype) for x in staged]
        + [packet_shape, shape((LEAD, width), bf16), order_shape, order_shape],
        in_specs=[whole(pltpu.HBM)] * len(staged),
        out_specs=[whole(vmem)] * (len(staged) + 4),
        scratch_shapes=[pltpu.SemaphoreType.DMA((len(staged),))],
        compiler_params=limit(8),
        name="pack_own",
    )(*(pltpu.with_memory_space_constraint(x, pltpu.HBM) for x in staged))
    own, ref_feat, shifts, bias_one, bias_two, view_head = staged
    packet = pl.pallas_call(
        pack_other_body,
        out_shape=packet_shape,
        in_specs=[whole(vmem)] * 4,
        out_specs=whole(vmem),
        compiler_params=limit(8),
        name="pack_other",
    )(part, pick, other_order, other)

    pairs = [(sides * i, sides * (i + 1)) for i in range(tiles - 1)]
    pairs += [(sides * (i + 1) + 1, sides * i + 1) for i in range(tiles - 1)]
    pairs += [(sides * (tiles - 1), sides * (tiles - 1) + 1), (1, 0)]
    got = lax.ppermute(packet, ("tile", "plane"), pairs)

    own, other, shifts, conv_one, conv_two, packet = lax.optimization_barrier(
        (own, other, shifts, conv_one, conv_two, packet)
    )
    if sides == 2:
        before = after = swap_planes(shifts)
    else:
        before = lax.ppermute(shifts, "plane", [(i, i + 1) for i in range(sides - 1)])
        after = lax.ppermute(shifts, "plane", [(i + 1, i) for i in range(sides - 1)])

    def taps(kernel):
        flipped = jnp.flip(kernel, axis=2)
        return jnp.transpose(flipped, (3, 4, 1, 2, 0)).reshape(9 * GROUPS, 3 * GROUPS)

    both_taps = jnp.stack([taps(conv_one), taps(conv_two)])
    span = (planes + 4) * GROUPS * rows
    out_lanes = planes * GROUPS * rows
    late_rows = width - MAX_SHIFT
    high = views * (late_rows + 8) + 8
    *inner, match, first = pl.pallas_call(
        inner_body,
        out_shape=[
            shape((views, width, lanes), bf16),
            shape((width, lanes), bf16),
            shape((8, 128), jnp.int32),
            shape((8, span), f32),
            shape((256, out_lanes), bf16),
            shape((out_lanes, out_lanes), bf16),
            shape((4 * out_lanes, out_lanes), bf16),
            shape((3 * (span - out_lanes), span - out_lanes), bf16),
            shape((4 * out_lanes, out_lanes), bf16),
            shape((high, span), f32),
            shape((high, span), f32),
        ],
        in_specs=[whole(vmem)] * 12,
        out_specs=[whole(vmem)] * 11,
        scratch_shapes=[
            pltpu.VMEM((views, width + 16, lanes), f32),
            pltpu.VMEM((width + 8, lanes), f32),
        ],
        compiler_params=limit(24),
        cost_estimate=pl.CostEstimate(
            flops=3 * 10**9, bytes_accessed=10**6, transcendentals=10**5
        ),
        name="inner_columns",
    )(
        shifts,
        before,
        after,
        bias_one,
        bias_two,
        view_head,
        own,
        other,
        ref_feat,
        own_order,
        other_order,
        both_taps,
    )
    got, match, first, *inner = lax.optimization_barrier((got, match, first, *inner))
    if sides == 2:
        swapped = swap_planes(got)
    else:
        both = lax.all_gather(got, "plane", axis=0)
        got, swapped = both[0], both[1]
    late = pl.pallas_call(
        late_body,
        out_shape=shape((late_rows, out_lanes), bf16),
        in_specs=[whole(vmem)] * 5,
        out_specs=whole(vmem),
        compiler_params=limit(24),
        cost_estimate=pl.CostEstimate(
            flops=2 * 10**9, bytes_accessed=10**6, transcendentals=10**5
        ),
        name="late_columns",
    )(match, first, inner[3], inner[4], inner[8])
    high = views * (MAX_SHIFT + 16) + 8
    return pl.pallas_call(
        outer_body,
        out_shape=shape((GROUPS, planes, rows, width), bf16),
        in_specs=[whole(vmem)] * 12,
        out_specs=whole(pltpu.HBM),
        scratch_shapes=[
            pltpu.VMEM((views, LEAD + width + EDGE, lanes), f32),
            pltpu.VMEM((EDGE + width + EDGE, lanes), f32),
            pltpu.VMEM((high, span), f32),
            pltpu.VMEM((high, span), f32),
            pltpu.VMEM((width, out_lanes), f32),
            pltpu.VMEM((GROUPS, planes, rows, width), bf16),
            pltpu.SemaphoreType.DMA((2,)),
        ],
        compiler_params=limit(24),
        name="outer_columns",
    )(*inner, late, got, swapped)


def solution(mesh):
    placed = (
        P(None, None, "tile"),
        P(None, "plane", None, "tile"),
        P(None, "plane"),
        P(),
        P(),
        P(),
        P(),
        P(),
    )
    return jax.shard_map(
        per_device,
        mesh=mesh,
        in_specs=placed,
        out_specs=P(None, "plane", None, "tile"),
        check_vma=False,
    )
```

```python
import jax
import jax.numpy as jnp
from jax import lax
from jax.experimental import pallas as pl
from jax.experimental.pallas import tpu as pltpu
from jax.sharding import PartitionSpec as P

GROUPS = 8
MAX_SHIFT = 128
LEAD = MAX_SHIFT + 8
EDGE = 16
BATCH = 2
FAR = -3.0e38


def iota(shape, dim):
    return lax.broadcasted_iota(jnp.int32, shape, dim)


def dot(left, right):
    return jnp.dot(left, right, preferred_element_type=jnp.float32)


def dot_nt(left, right):
    return lax.dot_general(
        left, right, (((1,), (1,)), ((), ())), preferred_element_type=jnp.float32
    )


def position():
    tile, plane = lax.axis_index("tile"), lax.axis_index("plane")
    tiles, sides = lax.axis_size("tile"), lax.axis_size("plane")
    order = plane if sides == 2 else 0 * plane
    role = jnp.minimum(plane, 1)
    return role, order, tile == 0, tile == tiles - 1, plane == 0, plane == sides - 1


def columns_of(count, width, start):
    picked = iota((count, width), 0) + start == iota((count, width), 1)
    return picked.astype(jnp.bfloat16)


def edge_columns(width, role):
    row = iota((LEAD, width), 0)
    base = edge_start(role, width, MAX_SHIFT)
    column = jnp.where(row < MAX_SHIFT, base + row, base - 4 + row % 4)
    column = jnp.where((row >= MAX_SHIFT) & (row % 4 < 2), -1, column)
    return (column == iota((LEAD, width), 1)).astype(jnp.bfloat16)


def laid_out(pairs, lanes):
    blocks, tails = [], []
    for pair in pairs:
        a, b = pair[:, 0:lanes], pair[:, lanes:]
        blocks += [a[0:MAX_SHIFT], b[0:MAX_SHIFT]]
        tails.append(jnp.where(iota((8, lanes), 0) < 4, a[MAX_SHIFT:], b[MAX_SHIFT:]))
    return blocks, jnp.concatenate(tails, axis=0)


def lane_order(half, rows, side):
    lanes = 2 * half * rows
    inner = 2 * half // GROUPS
    at, to = iota((lanes, 2 * lanes), 0), iota((lanes, 2 * lanes), 1)
    k, g = (to // (GROUPS * rows)) % inner, (to // rows) % GROUPS
    channel = g * inner + k - half * side
    row = (to // lanes) * (half * rows) + channel * rows + to % rows
    held = (channel >= 0) & (channel < half) & (row == at)
    return held.astype(jnp.bfloat16)


def ref_order(lanes, rows):
    at, to = iota((lanes, lanes), 0), iota((lanes, lanes), 1)
    k, g, h = to // (GROUPS * rows), (to // rows) % GROUPS, to % rows
    return ((g * (lanes // (GROUPS * rows)) + k) * rows + h == at).astype(jnp.bfloat16)


def turned_half(half_ref, pick, order):
    views, half, rows, width = half_ref.shape
    lanes = 2 * half * rows
    block = half_ref[...].reshape(views * half * rows, width)
    columns = dot_nt(pick, block).astype(jnp.bfloat16)
    return [dot(columns[:, i : i + lanes], order) for i in range(0, columns.shape[1], lanes)]


def turned_ref(ref_ref, pick):
    channels, rows, width = ref_ref.shape
    lanes = channels * rows
    columns = dot_nt(pick, ref_ref[...].reshape(lanes, width)).astype(jnp.bfloat16)
    return dot(columns, ref_order(lanes, rows))


def edge_start(role, width, count):
    return jnp.where(role == 0, width - count, 0)


def pack_own_body(*refs):
    count = (len(refs) - 5) // 2
    sources, targets = refs[:count], refs[count : 2 * count]
    part_ref, pick_ref, own_order_ref, other_order_ref, sems = refs[2 * count :]
    copies = [
        pltpu.make_async_copy(source, target, sems.at[i])
        for i, (source, target) in enumerate(zip(sources, targets))
    ]
    for copy in copies:
        copy.start()
    own_ref, ref_ref = targets[:2]
    views, half, rows, width = own_ref.shape
    lanes = part_ref.shape[1]
    role, order, *_ = position()
    pick_ref[...] = edge_columns(width, role)
    own_order_ref[...] = lane_order(half, rows, order)
    other_order_ref[...] = lane_order(half, rows, 1 - order)
    few = columns_of(EDGE, width, edge_start(role, width, 2)).astype(jnp.float32)
    few = jnp.where(iota((EDGE, width), 0) < 2, few, 0.0).astype(jnp.bfloat16)
    copies[0].wait()
    pairs = turned_half(own_ref, pick_ref[...], own_order_ref[...])
    blocks, tails = laid_out(pairs, lanes)
    for v, block in enumerate(blocks):
        part_ref[v * MAX_SHIFT : (v + 1) * MAX_SHIFT] = block.astype(jnp.bfloat16)
    copies[1].wait()
    extra = turned_ref(ref_ref, few)[0:8]
    tails = jnp.concatenate([tails[0:8] + extra, tails[8:]], axis=0)
    part_ref[views * MAX_SHIFT :] = tails.astype(jnp.bfloat16)
    for copy in copies[2:]:
        copy.wait()


def pack_other_body(part_ref, pick_ref, other_order_ref, other_ref, packet_ref):
    lanes = packet_ref.shape[1]
    pairs = turned_half(other_ref, pick_ref[...], other_order_ref[...])
    blocks, tails = laid_out(pairs, lanes)
    for v, block in enumerate(blocks):
        rows = pl.ds(v * MAX_SHIFT, MAX_SHIFT)
        packet_ref[rows] = (part_ref[rows].astype(jnp.float32) + block).astype(jnp.bfloat16)
    at = len(blocks) * MAX_SHIFT
    packet_ref[at:] = (part_ref[at:].astype(jnp.float32) + tails).astype(jnp.bfloat16)


def lane_table(values_ref, rows, lane):
    which = lane // rows % GROUPS
    table = jnp.zeros(lane.shape, jnp.float32)
    for o in range(GROUPS):
        table = jnp.where(which == o, values_ref[o], table)
    return table


def base_blocks(taps_ref, which, rows, apart):
    block = GROUPS * rows
    slots = 128 // (4 * rows)
    at, lane = iota((3 * GROUPS, 128), 0), iota((3 * GROUPS, 128), 1)
    if apart:
        spreads = [
            (lane // (slots * rows) + t * 4 == at % GROUPS)
            & ((lane // rows) % slots == at // GROUPS)
            for t in range(2)
        ]
    else:
        spreads = [lane // rows == at]
    stretch = (iota((block, GROUPS), 0) // rows == iota((block, GROUPS), 1)).astype(jnp.bfloat16)
    gap = iota((block, 128), 0) % rows - iota((block, 128), 1) % rows + 1
    found = []
    for spread in spreads:
        wide = dot(taps_ref[which], spread.astype(jnp.bfloat16)).astype(jnp.bfloat16)
        for e in range(3):
            base = jnp.zeros((block, 128), jnp.float32)
            for b in range(3):
                at = (b * 3 + e) * GROUPS
                base = jnp.where(gap == b, dot(stretch, wide[at : at + GROUPS]), base)
            found.append(base)
    return [found[i : i + 3] for i in range(0, len(found), 3)]


def band_rows(e, j, block):
    per_tile = 128 // block
    whole = 2 * per_tile
    if j < whole:
        return (e * whole + j) * block
    return (3 * whole + 2 * e + j - whole) * block


def build_band_one(taps_ref, band_ref, rest_ref, rows):
    block = GROUPS * rows
    lane = iota((block, 128), 1)
    per_tile = 128 // block
    zero = jnp.zeros((block, 128), jnp.bfloat16)
    (bases,) = base_blocks(taps_ref, 0, rows, False)
    for e, base in enumerate(bases):
        low_parts, high_parts = [], []
        for turn in range(per_tile):
            moved = pltpu.roll(base, turn * block, 1) if turn else base
            high_parts.append(jnp.where(lane >= turn * block, moved, 0.0).astype(jnp.bfloat16))
            low_parts.append(jnp.where(lane < turn * block, moved, 0.0).astype(jnp.bfloat16))
        for j in range(2 * per_tile + 2):
            first, turn = (j - 2) // per_tile, (j - 2) % per_tile
            at = band_rows(e, j, block)
            for t in range(2):
                part = zero
                if t == first:
                    part = high_parts[turn]
                elif t == first + 1 and turn > per_tile - 3:
                    part = low_parts[turn]
                band_ref[at : at + block, t * 128 : (t + 1) * 128] = part
                if t == 0 and j < per_tile:
                    rest_ref[(e * per_tile + j) * block : (e * per_tile + j + 1) * block] = part
    for j in range(2):
        at = (3 * (2 * per_tile + 2) + j) * block
        band_ref[at : at + block] = jnp.zeros((block, 256), jnp.bfloat16)


def build_band_two(taps_ref, band_ref, rows):
    block = GROUPS * rows
    per_tile = 128 // block
    slots = 2 * per_tile
    plane = (iota((block, 128), 1) // rows) % slots
    for t, bases in enumerate(base_blocks(taps_ref, 1, rows, True)):
        for e, base in enumerate(bases):
            for j in range(slots + 2):
                turn = (j - 2) * rows % 128
                moved = pltpu.roll(base, turn, 1) if turn else base
                held = (plane >= j - 2) & (plane <= j)
                at = band_rows(e, j, block)
                band_ref[at : at + block, t * 128 : (t + 1) * 128] = jnp.where(
                    held, moved, 0.0
                ).astype(jnp.bfloat16)
    for j in range(2):
        at = (3 * (slots + 2) + j) * block
        band_ref[at : at + block] = jnp.zeros((block, 256), jnp.bfloat16)


def build_tables(planes, rows, inner, bias_one, bias_two, view_head, ends, table_ref, spread_ref, perm_ref):
    block = GROUPS * rows
    out_lanes = planes * block
    span = table_ref.shape[1]
    is_first_plane, is_last_plane = ends
    at = iota((1, span), 1)
    plane = at // block
    outside = ((plane < 2) & is_first_plane) | ((plane >= planes + 2) & is_last_plane)
    table_ref[0:1] = jnp.where(outside, 0.0, 1.0 / inner)
    outside = ((plane == 0) & is_first_plane) | ((plane == planes + 1) & is_last_plane)
    table_ref[1:2] = jnp.where(outside, FAR, lane_table(bias_one, rows, at))
    table_ref[2:3] = lane_table(bias_two, planes * rows, at)
    table_ref[3:4] = lane_table(view_head, planes * rows, at)
    row, lane = iota(spread_ref.shape, 0), iota(spread_ref.shape, 1)
    same = (row // rows % planes == lane // block) & (row % rows == lane % rows)
    spread_ref[...] = same.astype(jnp.bfloat16)
    to = iota(perm_ref.shape, 0)
    g, j, h = to // (planes * rows), (to // rows) % planes, to % rows
    perm = (j * GROUPS + g) * rows + h == iota(perm_ref.shape, 1)
    perm_ref[...] = perm.astype(jnp.bfloat16)


def fill(pieces, near, src, wide, match, table_ref, block):
    shared = lax.axis_size("plane") == 2
    last = len(near) - 2
    for at, src_at, wide_at, count in pieces:
        quarter = iota((count, 128), 1) // block
        lower, middle, even = quarter < 2, (quarter == 1) | (quarter == 2), quarter % 2 == 0
        here = wide[wide_at : wide_at + count]
        ready = {}

        def product(j):
            if shared and j >= last:
                j -= last
            if j not in ready:
                ready[j] = src[pl.ds(src_at - near[j], count)] * here
            return ready[j]

        tiles = match.shape[1] // 128
        for q in (0, *reversed(range(1, tiles))):
            a, c, b, d = (product(q * 4 + k) for k in range(4))
            x = jnp.where(lower, a, b) + pltpu.roll(jnp.where(lower, b, a), 64, 1)
            z = jnp.where(middle, c, d) + pltpu.roll(jnp.where(middle, d, c), 64, 1)
            y = jnp.where(even, x, z) + pltpu.roll(jnp.where(even, z, x), 96, 1)
            y = y * table_ref[0:1, q * 128 : (q + 1) * 128]
            y = y.astype(jnp.bfloat16).astype(jnp.float32)
            match[at : at + count, q * 128 : (q + 1) * 128] = y


def three_taps(volume, low, high, out_lanes):
    tile = volume.shape[1] - out_lanes
    parts = [volume[low + e : high + e] for e in range(3)]
    tails = [part[:, out_lanes:] for part in parts]
    near = iota((high - low, tile), 1) < tile // 2
    paired = jnp.where(near, tails[0], pltpu.roll(tails[1], tile // 2, 1))
    sides = [part[:, 0:out_lanes] for part in parts] + [paired, tails[2]]
    wide = jnp.concatenate([side.astype(jnp.bfloat16) for side in sides], axis=1)
    return wide, jnp.concatenate([tail.astype(jnp.bfloat16) for tail in tails], axis=1)


def convolve_first(low, high, planes, block, match, first, table_ref, band_one, rest_ref):
    out_lanes = planes * block
    wide, tails = three_taps(match, low, high, out_lanes)
    raw = dot(wide, band_one[...])
    main = jnp.maximum(raw + table_ref[1:2, 0:out_lanes], 0.0)
    raw = dot(tails, rest_ref[...])
    rest = jnp.maximum(raw + table_ref[1:2, out_lanes:], 0.0)

    def store():
        first[low:high, 0:out_lanes] = main
        first[low:high, out_lanes:] = rest

    return store


def convolve_second(low, high, planes, block, first, table_ref, band_two):
    out_lanes = planes * block
    wide, _ = three_taps(first, low, high, out_lanes)
    second = dot(wide, band_two[...])
    second = jnp.maximum(second + table_ref[2:3, 0:out_lanes], 0.0) * table_ref[3:4, 0:out_lanes]
    half = out_lanes // 2
    return second[:, 0:half] + second[:, half:]


def weights(second, spread_ref):
    upper = second.astype(jnp.bfloat16)
    under = (second - upper.astype(jnp.float32)).astype(jnp.bfloat16)
    score = dot(jnp.concatenate([upper, under], axis=1), spread_ref[...])
    return jax.nn.sigmoid(score)


def first_stage(
    views, tall, planes, block, filled, mend, match, first, table_ref, band_one, rest_ref
):
    store = None
    for v in range(views + 1):
        if v < views:
            filled(v)
        if store is not None:
            store()
            mend((v - 1) * tall)
        if v < views:
            low, high = v * tall, (v + 1) * tall
            store = convolve_first(
                low, high, planes, block, match, first, table_ref, band_one, rest_ref
            )


def second_stage(views, tall, planes, block, match, first, table_ref, band_two, spread_ref):
    out_lanes = planes * block
    total = weighted = 0.0
    steps = range(0, views, BATCH)
    seconds = [
        convolve_second(at * tall, (at + BATCH) * tall, planes, block, first, table_ref, band_two)
        for at in steps
    ]
    for at, second in zip(steps, seconds):
        weight = weights(second, spread_ref)
        for v in range(BATCH):
            part = weight[v * tall : (v + 1) * tall]
            row = (at + v) * tall + 2
            total = total + part
            weighted = weighted + part * match[row : row + tall, 2 * block : 2 * block + out_lanes]
    return weighted / total


def pack_shifts(shifts, before, after, word_ref):
    for row, ref in enumerate((before, shifts, after)):
        word = ref[0:1]
        for v in range(1, ref.shape[0]):
            word = word | (ref[v : v + 1] << (8 * v))
        word_ref[row : row + 1, 0 : word.shape[1]] = word


def read_shifts(views, planes, word_ref):
    at = [(0, planes - 2), (0, planes - 1)] + [(1, d) for d in range(planes)] + [(2, 0), (2, 1)]
    words = [word_ref[row, d] for row, d in at]
    if lax.axis_size("plane") == 2:
        _, _, _, _, is_first_plane, _ = position()
        for k in range(2):
            inside = jnp.where(is_first_plane, words[planes + 2 + k], words[k])
            words[k] = words[planes + 2 + k] = inside
    return [[(word >> (8 * v)) & 255 for word in words] for v in range(views)]


def inner_body(
    shifts,
    before,
    after,
    bias_one,
    bias_two,
    view_head,
    own_ref,
    other_ref,
    ref_ref,
    own_order_ref,
    other_order_ref,
    taps_ref,
    cols_ref,
    ref_cols_ref,
    word_ref,
    table_ref,
    spread_ref,
    perm_ref,
    band_one,
    rest_ref,
    band_two,
    match,
    first,
    src,
    wide,
):
    views, half, rows, width = own_ref.shape
    planes = shifts.shape[1]
    lanes = 2 * half * rows
    inner = 2 * half // GROUPS
    block = GROUPS * rows
    _, _, _, _, *ends = position()
    pick = columns_of(width, width, 0)
    none = jnp.zeros((8, lanes), jnp.float32)
    columns = turned_ref(ref_ref, pick)
    ref_cols_ref[...] = columns.astype(jnp.bfloat16)
    wide[0:width] = columns
    wide[width:] = none
    pairs = zip(
        turned_half(own_ref, pick, own_order_ref[...]),
        turned_half(other_ref, pick, other_order_ref[...]),
    )
    for i, (low, high) in enumerate(pairs):
        columns = low + high
        for k in range(2):
            v = 2 * i + k
            part = columns[:, k * lanes : (k + 1) * lanes]
            cols_ref[v] = part.astype(jnp.bfloat16)
            src[v, 0:8] = none
            src[v, 8 : 8 + width] = part
            src[v, 8 + width :] = none
    build_tables(
        planes, rows, inner, bias_one, bias_two, view_head, ends, table_ref, spread_ref, perm_ref
    )
    build_band_one(taps_ref, band_one, rest_ref, rows)
    build_band_two(taps_ref, band_two, rows)
    pack_shifts(shifts, before, after, word_ref)
    near = read_shifts(views, planes, word_ref)
    out_rows = width - MAX_SHIFT
    tall = out_rows + 8
    base = MAX_SHIFT - 2

    def filled(v):
        pieces = [
            (v * tall + r, 8 + base + r, base + r, min(48, tall - r)) for r in range(0, tall, 48)
        ]
        fill(pieces, near[v], src.at[v], wide, match, table_ref, block)

    first_stage(
        views,
        tall,
        planes,
        block,
        filled,
        lambda row: None,
        match,
        first,
        table_ref,
        band_one,
        rest_ref,
    )
    for ref in (match, first):
        ref[views * tall :] = jnp.zeros((8, match.shape[1]), jnp.float32)


def late_body(match, first, table_ref, spread_ref, band_two, late_ref):
    out_rows, out_lanes = late_ref.shape
    block = (match.shape[1] - out_lanes) // 4
    views = match.shape[0] // (out_rows + 8)
    joined = second_stage(
        views, out_rows + 8, out_lanes // block, block, match, first, table_ref, band_two, spread_ref
    )
    late_ref[...] = joined[0:out_rows].astype(jnp.bfloat16)


def outer_body(
    cols_ref,
    ref_cols_ref,
    word_ref,
    table_ref,
    spread_ref,
    perm_ref,
    band_one,
    rest_ref,
    band_two,
    late_ref,
    got_ref,
    swapped_ref,
    out_ref,
    src,
    wide,
    match,
    first,
    joined,
    buffer,
    sems,
):
    views, width, lanes = cols_ref.shape
    groups, planes, rows, _ = out_ref.shape
    block = groups * rows
    _, order, is_first_tile, is_last_tile, *_ = position()

    near = read_shifts(views, planes, word_ref)
    left = jnp.where(order == 0, got_ref[...], swapped_ref[...])
    left = jnp.where(is_first_tile, jnp.zeros_like(left), left)
    right = jnp.where(order == 0, swapped_ref[...], got_ref[...])
    left_tails = left[views * MAX_SHIFT :].astype(jnp.float32)
    right_tails = right[views * MAX_SHIFT :].astype(jnp.float32)
    for v in range(views):
        at = v * MAX_SHIFT
        tail = left_tails[v // 2 * 8 : v // 2 * 8 + 8]
        src[v, 0:8] = tail if v % 2 else pltpu.roll(tail, 4, 0)
        src[v, 8:LEAD] = left[at : at + MAX_SHIFT].astype(jnp.float32)
        src[v, LEAD : LEAD + width] = cols_ref[v].astype(jnp.float32)
        src[v, LEAD + width :] = right[at : at + EDGE].astype(jnp.float32)
    wide[EDGE - 8 : EDGE] = pltpu.roll(left_tails[0:8], 6, 0)
    wide[EDGE : EDGE + width] = ref_cols_ref[...].astype(jnp.float32)
    wide[EDGE + width : EDGE + width + 8] = jnp.where(is_last_tile, 0.0, right_tails[0:8])
    main = MAX_SHIFT + 8
    tall = main + 8
    none = jnp.zeros((1, match.shape[1]), jnp.float32)

    def filled(v):
        at = v * tall
        pieces = [
            (at + r, LEAD - 2 + r, EDGE - 2 + r, min(48, main - r)) for r in range(0, main, 48)
        ]
        pieces += [(at + main, LEAD + width - 4, EDGE + width - 4, 8)]
        fill(pieces, near[v], src.at[v], wide, match, table_ref, block)

    def mend(row):
        for at, at_end in ((row, is_first_tile), (row + main + 3, is_last_tile)):
            first[at : at + 1] = jnp.where(at_end, none, first[at : at + 1])

    first_stage(
        views, tall, planes, block, filled, mend, match, first, table_ref, band_one, rest_ref
    )
    part = second_stage(
        views, tall, planes, block, match, first, table_ref, band_two, spread_ref
    )
    joined[0:MAX_SHIFT] = part[0:MAX_SHIFT]
    joined[MAX_SHIFT:] = late_ref[...].astype(jnp.float32)
    joined[MAX_SHIFT : MAX_SHIFT + 2] = part[MAX_SHIFT : MAX_SHIFT + 2]
    joined[width - 2 :] = part[main : main + 2]
    copies = []
    for half in range(2):
        at = half * (groups // 2)
        span = pl.ds(at, groups // 2)
        chosen = perm_ref[at * planes * rows : (at + groups // 2) * planes * rows]
        turned = dot_nt(chosen, joined[...].astype(jnp.bfloat16)).astype(jnp.bfloat16)
        buffer[at : at + groups // 2] = turned.reshape(groups // 2, planes, rows, width)
        copy = pltpu.make_async_copy(buffer.at[span], out_ref.at[span], sems.at[half])
        copy.start()
        copies.append(copy)
    for copy in copies:
        copy.wait()


def whole(memory):
    return pl.BlockSpec(memory_space=memory)


def limit(mebibytes):
    return pltpu.CompilerParams(vmem_limit_bytes=mebibytes * 1024 * 1024)


def swap_planes(value):
    return lax.ppermute(value, "plane", [(0, 1), (1, 0)])


def per_device(ref_feat, src_feat, shifts, conv_one, bias_one, conv_two, bias_two, view_head):
    views, _, rows, width = src_feat.shape
    planes = shifts.shape[1]
    lanes = ref_feat.shape[0] * rows
    tiles, sides = lax.axis_size("tile"), lax.axis_size("plane")
    bf16, f32 = jnp.bfloat16, jnp.float32
    vmem = pltpu.VMEM
    shape = jax.ShapeDtypeStruct
    if sides == 2:
        own, other = src_feat, swap_planes(src_feat)
    else:
        full = lax.all_gather(src_feat, "plane", axis=1, tiled=True)
        half = full.shape[1] // 2
        own, other = full[:, :half], full[:, half:]

    packet_shape = shape((views * MAX_SHIFT + views * 4, lanes), bf16)
    order_shape = shape((lanes, 2 * lanes), bf16)
    staged = (own, ref_feat, shifts, bias_one, bias_two, view_head)
    *staged, part, pick, own_order, other_order = pl.pallas_call(
        pack_own_body,
        out_shape=[shape(x.shape, x.dtype) for x in staged]
        + [packet_shape, shape((LEAD, width), bf16), order_shape, order_shape],
        in_specs=[whole(pltpu.HBM)] * len(staged),
        out_specs=[whole(vmem)] * (len(staged) + 4),
        scratch_shapes=[pltpu.SemaphoreType.DMA((len(staged),))],
        compiler_params=limit(8),
        name="pack_own",
    )(*(pltpu.with_memory_space_constraint(x, pltpu.HBM) for x in staged))
    own, ref_feat, shifts, bias_one, bias_two, view_head = staged
    packet = pl.pallas_call(
        pack_other_body,
        out_shape=packet_shape,
        in_specs=[whole(vmem)] * 4,
        out_specs=whole(vmem),
        compiler_params=limit(8),
        name="pack_other",
    )(part, pick, other_order, other)

    pairs = [(sides * i, sides * (i + 1)) for i in range(tiles - 1)]
    pairs += [(sides * (i + 1) + 1, sides * i + 1) for i in range(tiles - 1)]
    pairs += [(sides * (tiles - 1), sides * (tiles - 1) + 1), (1, 0)]
    got = lax.ppermute(packet, ("tile", "plane"), pairs)

    own, other, shifts, conv_one, conv_two, packet = lax.optimization_barrier(
        (own, other, shifts, conv_one, conv_two, packet)
    )
    if sides == 2:
        before = after = swap_planes(shifts)
    else:
        before = lax.ppermute(shifts, "plane", [(i, i + 1) for i in range(sides - 1)])
        after = lax.ppermute(shifts, "plane", [(i + 1, i) for i in range(sides - 1)])

    def taps(kernel):
        flipped = jnp.flip(kernel, axis=2)
        return jnp.transpose(flipped, (3, 4, 1, 2, 0)).reshape(9 * GROUPS, 3 * GROUPS)

    both_taps = jnp.stack([taps(conv_one), taps(conv_two)])
    span = (planes + 4) * GROUPS * rows
    out_lanes = planes * GROUPS * rows
    late_rows = width - MAX_SHIFT
    high = views * (late_rows + 8) + 8
    *inner, match, first = pl.pallas_call(
        inner_body,
        out_shape=[
            shape((views, width, lanes), bf16),
            shape((width, lanes), bf16),
            shape((8, 128), jnp.int32),
            shape((8, span), f32),
            shape((256, out_lanes), bf16),
            shape((out_lanes, out_lanes), bf16),
            shape((4 * out_lanes, out_lanes), bf16),
            shape((3 * (span - out_lanes), span - out_lanes), bf16),
            shape((4 * out_lanes, out_lanes), bf16),
            shape((high, span), f32),
            shape((high, span), f32),
        ],
        in_specs=[whole(vmem)] * 12,
        out_specs=[whole(vmem)] * 11,
        scratch_shapes=[
            pltpu.VMEM((views, width + 16, lanes), f32),
            pltpu.VMEM((width + 8, lanes), f32),
        ],
        compiler_params=limit(24),
        cost_estimate=pl.CostEstimate(
            flops=3 * 10**9, bytes_accessed=10**6, transcendentals=10**5
        ),
        name="inner_columns",
    )(
        shifts,
        before,
        after,
        bias_one,
        bias_two,
        view_head,
        own,
        other,
        ref_feat,
        own_order,
        other_order,
        both_taps,
    )
    got, match, first, *inner = lax.optimization_barrier((got, match, first, *inner))
    if sides == 2:
        swapped = swap_planes(got)
    else:
        both = lax.all_gather(got, "plane", axis=0)
        got, swapped = both[0], both[1]
    late = pl.pallas_call(
        late_body,
        out_shape=shape((late_rows, out_lanes), bf16),
        in_specs=[whole(vmem)] * 5,
        out_specs=whole(vmem),
        compiler_params=limit(24),
        cost_estimate=pl.CostEstimate(
            flops=2 * 10**9, bytes_accessed=10**6, transcendentals=10**5
        ),
        name="late_columns",
    )(match, first, inner[3], inner[4], inner[8])
    high = views * (MAX_SHIFT + 16) + 8
    return pl.pallas_call(
        outer_body,
        out_shape=shape((GROUPS, planes, rows, width), bf16),
        in_specs=[whole(vmem)] * 12,
        out_specs=whole(pltpu.HBM),
        scratch_shapes=[
            pltpu.VMEM((views, LEAD + width + EDGE, lanes), f32),
            pltpu.VMEM((EDGE + width + EDGE, lanes), f32),
            pltpu.VMEM((high, span), f32),
            pltpu.VMEM((high, span), f32),
            pltpu.VMEM((width, out_lanes), f32),
            pltpu.VMEM((GROUPS, planes, rows, width), bf16),
            pltpu.SemaphoreType.DMA((2,)),
        ],
        compiler_params=limit(24),
        name="outer_columns",
    )(*inner, late, got, swapped)


def solution(mesh):
    placed = (
        P(None, None, "tile"),
        P(None, "plane", None, "tile"),
        P(None, "plane"),
        P(),
        P(),
        P(),
        P(),
        P(),
    )
    return jax.shard_map(
        per_device,
        mesh=mesh,
        in_specs=placed,
        out_specs=P(None, "plane", None, "tile"),
        check_vma=False,
    )
```

```python
import jax
import jax.numpy as jnp
from jax import lax
from jax.experimental import pallas as pl
from jax.experimental.pallas import tpu as pltpu
from jax.sharding import PartitionSpec as P

GROUPS = 8
MAX_SHIFT = 128
LEAD = MAX_SHIFT + 8
EDGE = 16
BATCH = 2
FAR = -3.0e38


def iota(shape, dim):
    return lax.broadcasted_iota(jnp.int32, shape, dim)


def dot(left, right):
    return jnp.dot(left, right, preferred_element_type=jnp.float32)


def dot_nt(left, right):
    return lax.dot_general(
        left, right, (((1,), (1,)), ((), ())), preferred_element_type=jnp.float32
    )


def position():
    tile, plane = lax.axis_index("tile"), lax.axis_index("plane")
    tiles, sides = lax.axis_size("tile"), lax.axis_size("plane")
    order = plane if sides == 2 else 0 * plane
    role = jnp.minimum(plane, 1)
    return role, order, tile == 0, tile == tiles - 1, plane == 0, plane == sides - 1


def columns_of(count, width, start):
    picked = iota((count, width), 0) + start == iota((count, width), 1)
    return picked.astype(jnp.bfloat16)


def edge_columns(width, role):
    row = iota((LEAD, width), 0)
    base = edge_start(role, width, MAX_SHIFT)
    column = jnp.where(row < MAX_SHIFT, base + row, base - 4 + row % 4)
    column = jnp.where((row >= MAX_SHIFT) & (row % 4 < 2), -1, column)
    return (column == iota((LEAD, width), 1)).astype(jnp.bfloat16)


def laid_out(pairs, lanes):
    blocks, tails = [], []
    for pair in pairs:
        a, b = pair[:, 0:lanes], pair[:, lanes:]
        blocks += [a[0:MAX_SHIFT], b[0:MAX_SHIFT]]
        tails.append(jnp.where(iota((8, lanes), 0) < 4, a[MAX_SHIFT:], b[MAX_SHIFT:]))
    return blocks, jnp.concatenate(tails, axis=0)


def lane_order(half, rows, side):
    lanes = 2 * half * rows
    inner = 2 * half // GROUPS
    at, to = iota((lanes, 2 * lanes), 0), iota((lanes, 2 * lanes), 1)
    k, g = (to // (GROUPS * rows)) % inner, (to // rows) % GROUPS
    channel = g * inner + k - half * side
    row = (to // lanes) * (half * rows) + channel * rows + to % rows
    held = (channel >= 0) & (channel < half) & (row == at)
    return held.astype(jnp.bfloat16)


def ref_order(lanes, rows):
    at, to = iota((lanes, lanes), 0), iota((lanes, lanes), 1)
    k, g, h = to // (GROUPS * rows), (to // rows) % GROUPS, to % rows
    return ((g * (lanes // (GROUPS * rows)) + k) * rows + h == at).astype(jnp.bfloat16)


def turned_half(half_ref, pick, order):
    views, half, rows, width = half_ref.shape
    lanes = 2 * half * rows
    block = half_ref[...].reshape(views * half * rows, width)
    columns = dot_nt(pick, block).astype(jnp.bfloat16)
    return [dot(columns[:, i : i + lanes], order) for i in range(0, columns.shape[1], lanes)]


def turned_ref(ref_ref, pick):
    channels, rows, width = ref_ref.shape
    lanes = channels * rows
    columns = dot_nt(pick, ref_ref[...].reshape(lanes, width)).astype(jnp.bfloat16)
    return dot(columns, ref_order(lanes, rows))


def edge_start(role, width, count):
    return jnp.where(role == 0, width - count, 0)


def pack_own_body(*refs):
    count = (len(refs) - 5) // 2
    sources, targets = refs[:count], refs[count : 2 * count]
    part_ref, pick_ref, own_order_ref, other_order_ref, sems = refs[2 * count :]
    copies = [
        pltpu.make_async_copy(source, target, sems.at[i])
        for i, (source, target) in enumerate(zip(sources, targets))
    ]
    for copy in copies:
        copy.start()
    own_ref, ref_ref = targets[:2]
    views, half, rows, width = own_ref.shape
    lanes = part_ref.shape[1]
    role, order, *_ = position()
    pick_ref[...] = edge_columns(width, role)
    own_order_ref[...] = lane_order(half, rows, order)
    other_order_ref[...] = lane_order(half, rows, 1 - order)
    few = columns_of(EDGE, width, edge_start(role, width, 2)).astype(jnp.float32)
    few = jnp.where(iota((EDGE, width), 0) < 2, few, 0.0).astype(jnp.bfloat16)
    copies[0].wait()
    pairs = turned_half(own_ref, pick_ref[...], own_order_ref[...])
    blocks, tails = laid_out(pairs, lanes)
    for v, block in enumerate(blocks):
        part_ref[v * MAX_SHIFT : (v + 1) * MAX_SHIFT] = block.astype(jnp.bfloat16)
    for copy in copies[1:]:
        copy.wait()
    extra = turned_ref(ref_ref, few)[0:8]
    tails = jnp.concatenate([tails[0:8] + extra, tails[8:]], axis=0)
    part_ref[views * MAX_SHIFT :] = tails.astype(jnp.bfloat16)


def pack_other_body(part_ref, pick_ref, other_order_ref, other_ref, packet_ref):
    lanes = packet_ref.shape[1]
    pairs = turned_half(other_ref, pick_ref[...], other_order_ref[...])
    blocks, tails = laid_out(pairs, lanes)
    for v, block in enumerate(blocks):
        rows = pl.ds(v * MAX_SHIFT, MAX_SHIFT)
        packet_ref[rows] = (part_ref[rows].astype(jnp.float32) + block).astype(jnp.bfloat16)
    at = len(blocks) * MAX_SHIFT
    packet_ref[at:] = (part_ref[at:].astype(jnp.float32) + tails).astype(jnp.bfloat16)


def lane_table(values_ref, rows, lane):
    which = lane // rows % GROUPS
    table = jnp.zeros(lane.shape, jnp.float32)
    for o in range(GROUPS):
        table = jnp.where(which == o, values_ref[o], table)
    return table


def base_blocks(taps_ref, which, rows, apart):
    block = GROUPS * rows
    slots = 128 // (4 * rows)
    at, lane = iota((3 * GROUPS, 128), 0), iota((3 * GROUPS, 128), 1)
    if apart:
        spreads = [
            (lane // (slots * rows) + t * 4 == at % GROUPS)
            & ((lane // rows) % slots == at // GROUPS)
            for t in range(2)
        ]
    else:
        spreads = [lane // rows == at]
    stretch = (iota((block, GROUPS), 0) // rows == iota((block, GROUPS), 1)).astype(jnp.bfloat16)
    gap = iota((block, 128), 0) % rows - iota((block, 128), 1) % rows + 1
    found = []
    for spread in spreads:
        wide = dot(taps_ref[which], spread.astype(jnp.bfloat16)).astype(jnp.bfloat16)
        for e in range(3):
            base = jnp.zeros((block, 128), jnp.float32)
            for b in range(3):
                at = (b * 3 + e) * GROUPS
                base = jnp.where(gap == b, dot(stretch, wide[at : at + GROUPS]), base)
            found.append(base)
    return [found[i : i + 3] for i in range(0, len(found), 3)]


def band_rows(e, j, block):
    per_tile = 128 // block
    whole = 2 * per_tile
    if j < whole:
        return (e * whole + j) * block
    return (3 * whole + 2 * e + j - whole) * block


def build_band_one(taps_ref, band_ref, rest_ref, rows):
    block = GROUPS * rows
    lane = iota((block, 128), 1)
    per_tile = 128 // block
    zero = jnp.zeros((block, 128), jnp.bfloat16)
    (bases,) = base_blocks(taps_ref, 0, rows, False)
    for e, base in enumerate(bases):
        low_parts, high_parts = [], []
        for turn in range(per_tile):
            moved = pltpu.roll(base, turn * block, 1) if turn else base
            high_parts.append(jnp.where(lane >= turn * block, moved, 0.0).astype(jnp.bfloat16))
            low_parts.append(jnp.where(lane < turn * block, moved, 0.0).astype(jnp.bfloat16))
        for j in range(2 * per_tile + 2):
            first, turn = (j - 2) // per_tile, (j - 2) % per_tile
            at = band_rows(e, j, block)
            for t in range(2):
                part = zero
                if t == first:
                    part = high_parts[turn]
                elif t == first + 1 and turn > per_tile - 3:
                    part = low_parts[turn]
                band_ref[at : at + block, t * 128 : (t + 1) * 128] = part
                if t == 0 and j < per_tile:
                    rest_ref[(e * per_tile + j) * block : (e * per_tile + j + 1) * block] = part
    for j in range(2):
        at = (3 * (2 * per_tile + 2) + j) * block
        band_ref[at : at + block] = jnp.zeros((block, 256), jnp.bfloat16)


def build_band_two(taps_ref, band_ref, rows):
    block = GROUPS * rows
    per_tile = 128 // block
    slots = 2 * per_tile
    plane = (iota((block, 128), 1) // rows) % slots
    for t, bases in enumerate(base_blocks(taps_ref, 1, rows, True)):
        for e, base in enumerate(bases):
            for j in range(slots + 2):
                turn = (j - 2) * rows % 128
                moved = pltpu.roll(base, turn, 1) if turn else base
                held = (plane >= j - 2) & (plane <= j)
                at = band_rows(e, j, block)
                band_ref[at : at + block, t * 128 : (t + 1) * 128] = jnp.where(
                    held, moved, 0.0
                ).astype(jnp.bfloat16)
    for j in range(2):
        at = (3 * (slots + 2) + j) * block
        band_ref[at : at + block] = jnp.zeros((block, 256), jnp.bfloat16)


def build_tables(planes, rows, inner, bias_one, bias_two, view_head, ends, table_ref, spread_ref, perm_ref):
    block = GROUPS * rows
    out_lanes = planes * block
    span = table_ref.shape[1]
    is_first_plane, is_last_plane = ends
    at = iota((1, span), 1)
    plane = at // block
    outside = ((plane < 2) & is_first_plane) | ((plane >= planes + 2) & is_last_plane)
    table_ref[0:1] = jnp.where(outside, 0.0, 1.0 / inner)
    outside = ((plane == 0) & is_first_plane) | ((plane == planes + 1) & is_last_plane)
    table_ref[1:2] = jnp.where(outside, FAR, lane_table(bias_one, rows, at))
    table_ref[2:3] = lane_table(bias_two, planes * rows, at)
    table_ref[3:4] = lane_table(view_head, planes * rows, at)
    row, lane = iota(spread_ref.shape, 0), iota(spread_ref.shape, 1)
    same = (row // rows % planes == lane // block) & (row % rows == lane % rows)
    spread_ref[...] = same.astype(jnp.bfloat16)
    to = iota(perm_ref.shape, 0)
    g, j, h = to // (planes * rows), (to // rows) % planes, to % rows
    perm = (j * GROUPS + g) * rows + h == iota(perm_ref.shape, 1)
    perm_ref[...] = perm.astype(jnp.bfloat16)


def fill(pieces, near, src, wide, match, table_ref, block):
    shared = lax.axis_size("plane") == 2
    last = len(near) - 2
    for at, src_at, wide_at, count in pieces:
        quarter = iota((count, 128), 1) // block
        lower, middle, even = quarter < 2, (quarter == 1) | (quarter == 2), quarter % 2 == 0
        here = wide[wide_at : wide_at + count]
        ready = {}

        def product(j):
            if shared and j >= last:
                j -= last
            if j not in ready:
                ready[j] = src[pl.ds(src_at - near[j], count)] * here
            return ready[j]

        tiles = match.shape[1] // 128
        for q in (0, *reversed(range(1, tiles))):
            a, c, b, d = (product(q * 4 + k) for k in range(4))
            x = jnp.where(lower, a, b) + pltpu.roll(jnp.where(lower, b, a), 64, 1)
            z = jnp.where(middle, c, d) + pltpu.roll(jnp.where(middle, d, c), 64, 1)
            y = jnp.where(even, x, z) + pltpu.roll(jnp.where(even, z, x), 96, 1)
            y = y * table_ref[0:1, q * 128 : (q + 1) * 128]
            y = y.astype(jnp.bfloat16).astype(jnp.float32)
            match[at : at + count, q * 128 : (q + 1) * 128] = y


def three_taps(volume, low, high, out_lanes):
    tile = volume.shape[1] - out_lanes
    parts = [volume[low + e : high + e] for e in range(3)]
    tails = [part[:, out_lanes:] for part in parts]
    near = iota((high - low, tile), 1) < tile // 2
    paired = jnp.where(near, tails[0], pltpu.roll(tails[1], tile // 2, 1))
    sides = [part[:, 0:out_lanes] for part in parts] + [paired, tails[2]]
    wide = jnp.concatenate([side.astype(jnp.bfloat16) for side in sides], axis=1)
    return wide, jnp.concatenate([tail.astype(jnp.bfloat16) for tail in tails], axis=1)


def convolve_first(low, high, planes, block, match, first, table_ref, band_one, rest_ref):
    out_lanes = planes * block
    wide, tails = three_taps(match, low, high, out_lanes)
    raw = dot(wide, band_one[...])
    main = jnp.maximum(raw + table_ref[1:2, 0:out_lanes], 0.0)
    raw = dot(tails, rest_ref[...])
    rest = jnp.maximum(raw + table_ref[1:2, out_lanes:], 0.0)

    def store():
        first[low:high, 0:out_lanes] = main
        first[low:high, out_lanes:] = rest

    return store


def convolve_second(low, high, planes, block, first, table_ref, band_two):
    out_lanes = planes * block
    wide, _ = three_taps(first, low, high, out_lanes)
    second = dot(wide, band_two[...])
    second = jnp.maximum(second + table_ref[2:3, 0:out_lanes], 0.0) * table_ref[3:4, 0:out_lanes]
    half = out_lanes // 2
    return second[:, 0:half] + second[:, half:]


def weights(second, spread_ref):
    upper = second.astype(jnp.bfloat16)
    under = (second - upper.astype(jnp.float32)).astype(jnp.bfloat16)
    score = dot(jnp.concatenate([upper, under], axis=1), spread_ref[...])
    return jax.nn.sigmoid(score)


def first_stage(
    views, tall, planes, block, filled, mend, match, first, table_ref, band_one, rest_ref
):
    store = None
    for v in range(views + 1):
        if v < views:
            filled(v)
        if store is not None:
            store()
            mend((v - 1) * tall)
        if v < views:
            low, high = v * tall, (v + 1) * tall
            store = convolve_first(
                low, high, planes, block, match, first, table_ref, band_one, rest_ref
            )


def second_stage(views, tall, planes, block, match, first, table_ref, band_two, spread_ref):
    out_lanes = planes * block
    total = weighted = 0.0
    steps = range(0, views, BATCH)
    seconds = [
        convolve_second(at * tall, (at + BATCH) * tall, planes, block, first, table_ref, band_two)
        for at in steps
    ]
    for at, second in zip(steps, seconds):
        weight = weights(second, spread_ref)
        for v in range(BATCH):
            part = weight[v * tall : (v + 1) * tall]
            row = (at + v) * tall + 2
            total = total + part
            weighted = weighted + part * match[row : row + tall, 2 * block : 2 * block + out_lanes]
    return weighted / total


def pack_shifts(shifts, before, after, word_ref):
    for row, ref in enumerate((before, shifts, after)):
        word = ref[0:1]
        for v in range(1, ref.shape[0]):
            word = word | (ref[v : v + 1] << (8 * v))
        word_ref[row : row + 1, 0 : word.shape[1]] = word


def read_shifts(views, planes, word_ref):
    at = [(0, planes - 2), (0, planes - 1)] + [(1, d) for d in range(planes)] + [(2, 0), (2, 1)]
    words = [word_ref[row, d] for row, d in at]
    if lax.axis_size("plane") == 2:
        _, _, _, _, is_first_plane, _ = position()
        for k in range(2):
            inside = jnp.where(is_first_plane, words[planes + 2 + k], words[k])
            words[k] = words[planes + 2 + k] = inside
    return [[(word >> (8 * v)) & 255 for word in words] for v in range(views)]


def inner_body(
    shifts,
    before,
    after,
    bias_one,
    bias_two,
    view_head,
    own_ref,
    other_ref,
    ref_ref,
    own_order_ref,
    other_order_ref,
    taps_ref,
    cols_ref,
    ref_cols_ref,
    word_ref,
    table_ref,
    spread_ref,
    perm_ref,
    band_one,
    rest_ref,
    band_two,
    match,
    first,
    src,
    wide,
):
    views, half, rows, width = own_ref.shape
    planes = shifts.shape[1]
    lanes = 2 * half * rows
    inner = 2 * half // GROUPS
    block = GROUPS * rows
    _, _, _, _, *ends = position()
    pick = columns_of(width, width, 0)
    none = jnp.zeros((8, lanes), jnp.float32)
    columns = turned_ref(ref_ref, pick)
    ref_cols_ref[...] = columns.astype(jnp.bfloat16)
    wide[0:width] = columns
    wide[width:] = none
    pairs = zip(
        turned_half(own_ref, pick, own_order_ref[...]),
        turned_half(other_ref, pick, other_order_ref[...]),
    )
    for i, (low, high) in enumerate(pairs):
        columns = low + high
        for k in range(2):
            v = 2 * i + k
            part = columns[:, k * lanes : (k + 1) * lanes]
            cols_ref[v] = part.astype(jnp.bfloat16)
            src[v, 0:8] = none
            src[v, 8 : 8 + width] = part
            src[v, 8 + width :] = none
    build_tables(
        planes, rows, inner, bias_one, bias_two, view_head, ends, table_ref, spread_ref, perm_ref
    )
    build_band_one(taps_ref, band_one, rest_ref, rows)
    build_band_two(taps_ref, band_two, rows)
    pack_shifts(shifts, before, after, word_ref)
    near = read_shifts(views, planes, word_ref)
    out_rows = width - MAX_SHIFT
    tall = out_rows + 8
    base = MAX_SHIFT - 2

    def filled(v):
        pieces = [
            (v * tall + r, 8 + base + r, base + r, min(48, tall - r)) for r in range(0, tall, 48)
        ]
        fill(pieces, near[v], src.at[v], wide, match, table_ref, block)

    first_stage(
        views,
        tall,
        planes,
        block,
        filled,
        lambda row: None,
        match,
        first,
        table_ref,
        band_one,
        rest_ref,
    )
    for ref in (match, first):
        ref[views * tall :] = jnp.zeros((8, match.shape[1]), jnp.float32)


def late_body(match, first, table_ref, spread_ref, band_two, late_ref):
    out_rows, out_lanes = late_ref.shape
    block = (match.shape[1] - out_lanes) // 4
    views = match.shape[0] // (out_rows + 8)
    joined = second_stage(
        views, out_rows + 8, out_lanes // block, block, match, first, table_ref, band_two, spread_ref
    )
    late_ref[...] = joined[0:out_rows].astype(jnp.bfloat16)


def outer_body(
    cols_ref,
    ref_cols_ref,
    word_ref,
    table_ref,
    spread_ref,
    perm_ref,
    band_one,
    rest_ref,
    band_two,
    late_ref,
    got_ref,
    swapped_ref,
    out_ref,
    src,
    wide,
    match,
    first,
    joined,
    buffer,
    sems,
):
    views, width, lanes = cols_ref.shape
    groups, planes, rows, _ = out_ref.shape
    block = groups * rows
    _, order, is_first_tile, is_last_tile, *_ = position()

    near = read_shifts(views, planes, word_ref)
    left = jnp.where(order == 0, got_ref[...], swapped_ref[...])
    left = jnp.where(is_first_tile, jnp.zeros_like(left), left)
    right = jnp.where(order == 0, swapped_ref[...], got_ref[...])
    left_tails = left[views * MAX_SHIFT :].astype(jnp.float32)
    right_tails = right[views * MAX_SHIFT :].astype(jnp.float32)
    for v in range(views):
        at = v * MAX_SHIFT
        tail = left_tails[v // 2 * 8 : v // 2 * 8 + 8]
        src[v, 0:8] = tail if v % 2 else pltpu.roll(tail, 4, 0)
        src[v, 8:LEAD] = left[at : at + MAX_SHIFT].astype(jnp.float32)
        src[v, LEAD : LEAD + width] = cols_ref[v].astype(jnp.float32)
        src[v, LEAD + width :] = right[at : at + EDGE].astype(jnp.float32)
    wide[EDGE - 8 : EDGE] = pltpu.roll(left_tails[0:8], 6, 0)
    wide[EDGE : EDGE + width] = ref_cols_ref[...].astype(jnp.float32)
    wide[EDGE + width : EDGE + width + 8] = jnp.where(is_last_tile, 0.0, right_tails[0:8])
    main = MAX_SHIFT + 8
    tall = main + 8
    none = jnp.zeros((1, match.shape[1]), jnp.float32)

    def filled(v):
        at = v * tall
        pieces = [
            (at + r, LEAD - 2 + r, EDGE - 2 + r, min(24, main - r)) for r in range(0, main, 24)
        ]
        pieces += [(at + main, LEAD + width - 4, EDGE + width - 4, 8)]
        fill(pieces, near[v], src.at[v], wide, match, table_ref, block)

    def mend(row):
        for at, at_end in ((row, is_first_tile), (row + main + 3, is_last_tile)):
            first[at : at + 1] = jnp.where(at_end, none, first[at : at + 1])

    first_stage(
        views, tall, planes, block, filled, mend, match, first, table_ref, band_one, rest_ref
    )
    part = second_stage(
        views, tall, planes, block, match, first, table_ref, band_two, spread_ref
    )
    joined[0:MAX_SHIFT] = part[0:MAX_SHIFT]
    joined[MAX_SHIFT:] = late_ref[...].astype(jnp.float32)
    joined[MAX_SHIFT : MAX_SHIFT + 2] = part[MAX_SHIFT : MAX_SHIFT + 2]
    joined[width - 2 :] = part[main : main + 2]
    copies = []
    for half in range(2):
        at = half * (groups // 2)
        span = pl.ds(at, groups // 2)
        chosen = perm_ref[at * planes * rows : (at + groups // 2) * planes * rows]
        turned = dot_nt(chosen, joined[...].astype(jnp.bfloat16)).astype(jnp.bfloat16)
        buffer[at : at + groups // 2] = turned.reshape(groups // 2, planes, rows, width)
        copy = pltpu.make_async_copy(buffer.at[span], out_ref.at[span], sems.at[half])
        copy.start()
        copies.append(copy)
    for copy in copies:
        copy.wait()


def whole(memory):
    return pl.BlockSpec(memory_space=memory)


def limit(mebibytes):
    return pltpu.CompilerParams(vmem_limit_bytes=mebibytes * 1024 * 1024)


def swap_planes(value):
    return lax.ppermute(value, "plane", [(0, 1), (1, 0)])


def per_device(ref_feat, src_feat, shifts, conv_one, bias_one, conv_two, bias_two, view_head):
    views, _, rows, width = src_feat.shape
    planes = shifts.shape[1]
    lanes = ref_feat.shape[0] * rows
    tiles, sides = lax.axis_size("tile"), lax.axis_size("plane")
    bf16, f32 = jnp.bfloat16, jnp.float32
    vmem = pltpu.VMEM
    shape = jax.ShapeDtypeStruct
    if sides == 2:
        own, other = src_feat, swap_planes(src_feat)
    else:
        full = lax.all_gather(src_feat, "plane", axis=1, tiled=True)
        half = full.shape[1] // 2
        own, other = full[:, :half], full[:, half:]

    packet_shape = shape((views * MAX_SHIFT + views * 4, lanes), bf16)
    order_shape = shape((lanes, 2 * lanes), bf16)
    staged = (own, ref_feat, shifts, bias_one, bias_two, view_head)
    *staged, part, pick, own_order, other_order = pl.pallas_call(
        pack_own_body,
        out_shape=[shape(x.shape, x.dtype) for x in staged]
        + [packet_shape, shape((LEAD, width), bf16), order_shape, order_shape],
        in_specs=[whole(pltpu.HBM)] * len(staged),
        out_specs=[whole(vmem)] * (len(staged) + 4),
        scratch_shapes=[pltpu.SemaphoreType.DMA((len(staged),))],
        compiler_params=limit(8),
        name="pack_own",
    )(*(pltpu.with_memory_space_constraint(x, pltpu.HBM) for x in staged))
    own, ref_feat, shifts, bias_one, bias_two, view_head = staged
    packet = pl.pallas_call(
        pack_other_body,
        out_shape=packet_shape,
        in_specs=[whole(vmem)] * 4,
        out_specs=whole(vmem),
        compiler_params=limit(8),
        name="pack_other",
    )(part, pick, other_order, other)

    pairs = [(sides * i, sides * (i + 1)) for i in range(tiles - 1)]
    pairs += [(sides * (i + 1) + 1, sides * i + 1) for i in range(tiles - 1)]
    pairs += [(sides * (tiles - 1), sides * (tiles - 1) + 1), (1, 0)]
    got = lax.ppermute(packet, ("tile", "plane"), pairs)

    own, other, shifts, conv_one, conv_two, packet = lax.optimization_barrier(
        (own, other, shifts, conv_one, conv_two, packet)
    )
    if sides == 2:
        before = after = swap_planes(shifts)
    else:
        before = lax.ppermute(shifts, "plane", [(i, i + 1) for i in range(sides - 1)])
        after = lax.ppermute(shifts, "plane", [(i + 1, i) for i in range(sides - 1)])

    def taps(kernel):
        flipped = jnp.flip(kernel, axis=2)
        return jnp.transpose(flipped, (3, 4, 1, 2, 0)).reshape(9 * GROUPS, 3 * GROUPS)

    both_taps = jnp.stack([taps(conv_one), taps(conv_two)])
    span = (planes + 4) * GROUPS * rows
    out_lanes = planes * GROUPS * rows
    late_rows = width - MAX_SHIFT
    high = views * (late_rows + 8) + 8
    *inner, match, first = pl.pallas_call(
        inner_body,
        out_shape=[
            shape((views, width, lanes), bf16),
            shape((width, lanes), bf16),
            shape((8, 128), jnp.int32),
            shape((8, span), f32),
            shape((256, out_lanes), bf16),
            shape((out_lanes, out_lanes), bf16),
            shape((4 * out_lanes, out_lanes), bf16),
            shape((3 * (span - out_lanes), span - out_lanes), bf16),
            shape((4 * out_lanes, out_lanes), bf16),
            shape((high, span), f32),
            shape((high, span), f32),
        ],
        in_specs=[whole(vmem)] * 12,
        out_specs=[whole(vmem)] * 11,
        scratch_shapes=[
            pltpu.VMEM((views, width + 16, lanes), f32),
            pltpu.VMEM((width + 8, lanes), f32),
        ],
        compiler_params=limit(24),
        cost_estimate=pl.CostEstimate(
            flops=3 * 10**9, bytes_accessed=10**6, transcendentals=10**5
        ),
        name="inner_columns",
    )(
        shifts,
        before,
        after,
        bias_one,
        bias_two,
        view_head,
        own,
        other,
        ref_feat,
        own_order,
        other_order,
        both_taps,
    )
    got, match, first, *inner = lax.optimization_barrier((got, match, first, *inner))
    if sides == 2:
        swapped = swap_planes(got)
    else:
        both = lax.all_gather(got, "plane", axis=0)
        got, swapped = both[0], both[1]
    late = pl.pallas_call(
        late_body,
        out_shape=shape((late_rows, out_lanes), bf16),
        in_specs=[whole(vmem)] * 5,
        out_specs=whole(vmem),
        compiler_params=limit(24),
        cost_estimate=pl.CostEstimate(
            flops=2 * 10**9, bytes_accessed=10**6, transcendentals=10**5
        ),
        name="late_columns",
    )(match, first, inner[3], inner[4], inner[8])
    high = views * (MAX_SHIFT + 16) + 8
    return pl.pallas_call(
        outer_body,
        out_shape=shape((GROUPS, planes, rows, width), bf16),
        in_specs=[whole(vmem)] * 12,
        out_specs=whole(pltpu.HBM),
        scratch_shapes=[
            pltpu.VMEM((views, LEAD + width + EDGE, lanes), f32),
            pltpu.VMEM((EDGE + width + EDGE, lanes), f32),
            pltpu.VMEM((high, span), f32),
            pltpu.VMEM((high, span), f32),
            pltpu.VMEM((width, out_lanes), f32),
            pltpu.VMEM((GROUPS, planes, rows, width), bf16),
            pltpu.SemaphoreType.DMA((2,)),
        ],
        compiler_params=limit(24),
        name="outer_columns",
    )(*inner, late, got, swapped)


def solution(mesh):
    placed = (
        P(None, None, "tile"),
        P(None, "plane", None, "tile"),
        P(None, "plane"),
        P(),
        P(),
        P(),
        P(),
        P(),
    )
    return jax.shard_map(
        per_device,
        mesh=mesh,
        in_specs=placed,
        out_specs=P(None, "plane", None, "tile"),
        check_vma=False,
    )
```
